32 devices in a mesh: dp: 4 (over z), fsdp: 8 (over y, x, core).
Axes of the slice: x: 2, y: 2, z: 4, core: 2. Of those that a mesh axis runs over, the one named last changes fastest.
Arguments:
- input_token_ids: int32 [2, 32, 256], P(None, ('dp', 'fsdp')), may hold values from 0 to 50303
- lengths: int32 [2, 32], P(None, ('dp', 'fsdp')), may hold values from 64 to 256, as said below
- scored_slots: int32 [2, 32, 32], P(None, ('dp', 'fsdp')), may hold values from 0 to 255, as said below
- scored_targets: int32 [2, 32, 32], P(None, ('dp', 'fsdp')), may hold values from 0 to 50303
- wte: bfloat16 [50304, 1024], P('fsdp'), may hold values from -0.359375 to 0.359375
- wpe: bfloat16 [256, 1024], replicated, may hold values from -0.359375 to 0.359375
- frozen_attention: bfloat16 [2, 1024, 4096], P(None, 'fsdp'), may hold values from -0.25 to 0.25
- frozen_feed_input: bfloat16 [2, 1024, 4096], P(None, 'fsdp'), may hold values from -0.1875 to 0.1875
- frozen_feed_output: bfloat16 [2, 4096, 1024], P(None, 'fsdp'), may hold values from -0.09375 to 0.09375
- frozen_bias_gain: bfloat16 [2, 13312], P(None, 'fsdp'), as said below
- final_norm_params: bfloat16 [2, 1024], replicated, as said below
- adapter_down: float32 [2, 1024, 12], replicated, may hold values from -0.1875 to 0.1875
- adapter_down_feed: float32 [2, 4096, 4], replicated, may hold values from -0.09375 to 0.09375
- adapter_up: float32 [2, 4, 9216], replicated, may hold values from -0.06 to 0.06
- first_moment_down: float32 [2, 1024, 12], replicated, may hold values from -3.8146973e-05 to 3.8146973e-05
- first_moment_feed: float32 [2, 4096, 4], replicated, may hold values from -3.8146973e-05 to 3.8146973e-05
- first_moment_up: float32 [2, 4, 9216], replicated, may hold values from -3.8146973e-05 to 3.8146973e-05
- second_moment_down: float32 [2, 1024, 12], replicated, may hold values from 3.0517578e-12 to 1.2207031e-11
- second_moment_feed: float32 [2, 4096, 4], replicated, may hold values from 3.0517578e-12 to 1.2207031e-11
- second_moment_up: float32 [2, 4, 9216], replicated, may hold values from 3.0517578e-12 to 1.2207031e-11
- optimizer_step: int32 [1], replicated, may hold values from 2 to 20
Outputs:
- loss: float32 [], replicated
- grad_norm: float32 [], replicated
- new_lora_a: float32 [2, 1024, 12], replicated
- new_lora_a_ff: float32 [2, 4096, 4], replicated
- new_lora_b: float32 [2, 4, 9216], replicated
- new_mom_a: float32 [2, 1024, 12], replicated
- new_mom_a_ff: float32 [2, 4096, 4], replicated
- new_mom_b: float32 [2, 4, 9216], replicated
- new_sq_a: float32 [2, 1024, 12], replicated
- new_sq_a_ff: float32 [2, 4096, 4], replicated
- new_sq_b: float32 [2, 4, 9216], replicated
- row_losses: float32 [2, 32, 32], P(None, ('dp', 'fsdp'))
The draws below stay inside these ranges and needn't reach their ends.
Inputs may be any that keep to these rules, and one draw needn't show every extreme that they name: `lengths`: each row's live slots; some row holds all 256. `scored_slots`: the first listed position of each row lies under 64; positions may repeat. `frozen_bias_gain`: per layer: biases of the four projections, then the first norm's gain and shift, then the second's. `final_norm_params`: row 0 is the gain, row 1 the shift.
All inputs are finite; a program needn't handle non-finite values.
Results may differ from the reference program's by a relative error of at most 0.008.
Values may be sent and summed in bfloat16 or wider, within the bound.
No kernel may reach another device: no remote copies, remote signals or barrier semaphores. Data moves between devices by JAX's collectives and lax.ppermute only.
A program may use at most 256 MiB of HBM per device.

```python
import math
import jax
import jax.numpy as jnp
import numpy as np
from jax import lax

MODEL_WIDTH = 1024
H = 16
HD = 64
HIDDEN_UNITS = 4096
VOCAB = 50304
LAYER_COUNT = 2
ADAPTER_RANK = 4
SEQ = 256
MIN_LEN = 64
LOSS_POS = 32
MICRO = 2
ROWS = 32
NPARAM = 131072


def draw_lengths(key, part):
    key_one, key_two, key_three = jax.random.split(key, 3)
    shape = (MICRO, ROWS)
    shorter = jax.random.randint(key_one, shape, MIN_LEN, min(2 * MIN_LEN, SEQ) + 1)
    longer = jax.random.randint(key_two, shape, MIN_LEN, SEQ + 1)
    selector = jax.random.randint(key_three, shape, 0, 4)
    spans = jnp.where(selector == 0, longer, shorter)
    return spans.at[0, 0].set(SEQ).astype(jnp.int32)


def draw_scored_slots(key, part):
    key_one, key_two = jax.random.split(key)
    spots = jax.random.randint(key_one, (MICRO, ROWS, LOSS_POS), 0, SEQ)
    early = jax.random.randint(key_two, (MICRO, ROWS), 0, MIN_LEN)
    return spots.at[:, :, 0].set(early).astype(jnp.int32)


def draw_frozen_bias_gain(key, part):
    noise = jax.random.normal(key, (LAYER_COUNT, 9 * MODEL_WIDTH + HIDDEN_UNITS), jnp.float32)
    column = jnp.arange(9 * MODEL_WIDTH + HIDDEN_UNITS)
    start = 5 * MODEL_WIDTH + HIDDEN_UNITS
    gains = (column >= start) & (column < start + MODEL_WIDTH) | (column >= start + 2 * MODEL_WIDTH) & (column < start + 3 * MODEL_WIDTH)
    return jnp.where(gains[None], 1.0 + 0.1 * noise, 0.2 * noise).astype(jnp.bfloat16)


def draw_final_norm_params(key, part):
    noise = jax.random.normal(key, (2, MODEL_WIDTH), jnp.float32)
    return jnp.stack([1.0 + 0.1 * noise[0], 0.2 * noise[1]]).astype(jnp.bfloat16)


def touch_ends(entries, rng, low, high):
    longest = entries.shape.index(max(entries.shape))
    spots = []
    for shift in (0, 1):
        where = [jax.random.randint(jax.random.fold_in(rng, axis), (), 0, length) for axis, length in enumerate(entries.shape)]
        where[longest] = (where[longest] + shift) % entries.shape[longest]
        spots.append(tuple(where))
    return entries.at[spots[0]].set(low).at[spots[1]].set(high)


def block_levels(own_key, extent, shards, smallest, largest):
    def one(dim, shards_of):
        draws = jax.random.uniform(jax.random.fold_in(jax.random.fold_in(own_key, 6), dim), (shards_of,), jnp.float32, smallest / len(shards), largest / len(shards))
        return jnp.repeat(jnp.exp(draws), extent[dim] // shards_of).reshape((-1,) + (1,) * (len(extent) - dim - 1))

    loudness = one(*shards[0])
    for cut in shards[1:]:
        loudness = loudness * one(*cut)
    return loudness


def rank_table(count, lean):
    portions = [(1 << 20) // math.isqrt(rank ** lean) + 1 for rank in range(1, count + 1)]
    scale = 1 + sum(portions) // (1 << 30)
    return np.cumsum(np.array([max(1, weight // scale) for weight in portions]))


def ranked(rng, shape, number_of, lean):
    table = rank_table(number_of, lean)
    ticket = jax.random.randint(jax.random.fold_in(rng, 1), shape, 0, int(table[number_of - 1]))
    standing = jnp.searchsorted(jnp.asarray(table, jnp.int32), ticket, side="right")
    return jax.random.permutation(jax.random.fold_in(rng, 2), number_of)[standing].astype(jnp.int32)


def centred(own_key, shape, deviation, most, pieces=(), kind=jnp.bfloat16):
    result = jax.random.normal(own_key, shape, jnp.float32) * deviation
    if len(pieces) > 0:
        result = block_levels(own_key, shape, pieces, -0.22, 0.18) * result
    return jnp.clip(result, min=-most, max=most).astype(kind)


def setup_inputs(seed: int = 0) -> dict:
    seeds = jax.random.split(jax.random.key(seed), 22)
    return {
        "input_token_ids": touch_ends(ranked(seeds[0], (MICRO, ROWS, SEQ), VOCAB, 2), jax.random.fold_in(seeds[0], 3), 0, VOCAB - 1).astype(jnp.int32),
        "lengths": draw_lengths(jax.random.fold_in(seeds[21], 71), 0),
        "scored_slots": draw_scored_slots(jax.random.fold_in(seeds[21], 71), 0),
        "scored_targets": touch_ends(ranked(seeds[3], (MICRO, ROWS, LOSS_POS), VOCAB, 2), jax.random.fold_in(seeds[3], 3), 0, VOCAB - 1).astype(jnp.int32),
        "wte": centred(seeds[4], (VOCAB, MODEL_WIDTH), 0.06, 0.359375, ((0, 8),)),
        "wpe": centred(seeds[5], (SEQ, MODEL_WIDTH), 0.06, 0.359375),
        "frozen_attention": centred(seeds[6], (LAYER_COUNT, MODEL_WIDTH, 4 * MODEL_WIDTH), (MODEL_WIDTH // 2) ** -0.5, 0.25, ((1, 8),)),
        "frozen_feed_input": centred(seeds[7], (LAYER_COUNT, MODEL_WIDTH, HIDDEN_UNITS), MODEL_WIDTH ** -0.5, 0.1875, ((1, 8),)),
        "frozen_feed_output": centred(seeds[8], (LAYER_COUNT, HIDDEN_UNITS, MODEL_WIDTH), HIDDEN_UNITS ** -0.5, 0.09375, ((1, 8),)),
        "frozen_bias_gain": draw_frozen_bias_gain(jax.random.fold_in(seeds[21], 71), 0),
        "final_norm_params": draw_final_norm_params(jax.random.fold_in(seeds[21], 71), 0),
        "adapter_down": centred(seeds[11], (LAYER_COUNT, MODEL_WIDTH, 3 * ADAPTER_RANK), MODEL_WIDTH ** -0.5, 0.1875, (), jnp.float32),
        "adapter_down_feed": centred(seeds[12], (LAYER_COUNT, HIDDEN_UNITS, ADAPTER_RANK), HIDDEN_UNITS ** -0.5, 0.09375, (), jnp.float32),
        "adapter_up": centred(seeds[13], (LAYER_COUNT, ADAPTER_RANK, 5 * MODEL_WIDTH + HIDDEN_UNITS), 0.01, 0.06, (), jnp.float32),
        "first_moment_down": centred(seeds[14], (LAYER_COUNT, MODEL_WIDTH, 3 * ADAPTER_RANK), ((NPARAM * 202500) ** -0.5), 3.814697265625e-05, (), jnp.float32),
        "first_moment_feed": centred(seeds[15], (LAYER_COUNT, HIDDEN_UNITS, ADAPTER_RANK), ((NPARAM * 202500) ** -0.5), 3.814697265625e-05, (), jnp.float32),
        "first_moment_up": centred(seeds[16], (LAYER_COUNT, ADAPTER_RANK, 5 * MODEL_WIDTH + HIDDEN_UNITS), ((NPARAM * 202500) ** -0.5), 3.814697265625e-05, (), jnp.float32),
        "second_moment_down": jnp.clip(jnp.exp(jax.random.uniform(seeds[17], (LAYER_COUNT, MODEL_WIDTH, 3 * ADAPTER_RANK), jnp.float32, math.log(3.051757848163139e-12), math.log(1.2207031392652556e-11))), 3.051757848163139e-12, 1.2207031392652556e-11),
        "second_moment_feed": jnp.clip(jnp.exp(jax.random.uniform(seeds[18], (LAYER_COUNT, HIDDEN_UNITS, ADAPTER_RANK), jnp.float32, math.log(3.051757848163139e-12), math.log(1.2207031392652556e-11))), 3.051757848163139e-12, 1.2207031392652556e-11),
        "second_moment_up": jnp.clip(jnp.exp(jax.random.uniform(seeds[19], (LAYER_COUNT, ADAPTER_RANK, 5 * MODEL_WIDTH + HIDDEN_UNITS), jnp.float32, math.log(3.051757848163139e-12), math.log(1.2207031392652556e-11))), 3.051757848163139e-12, 1.2207031392652556e-11),
        "optimizer_step": jax.random.randint(seeds[20], (1,), 2, 21).astype(jnp.int32),
    }


@jax.custom_vjp
def low(v):
    return lax.optimization_barrier(v.astype(jnp.bfloat16)).astype(jnp.float32)

@jax.custom_vjp
def low_back(v):
    return v

def low_keep(v):
    return (low(v), None)

def low_pass(kept, grad):
    return (grad,)

def back_keep(v):
    return (v, None)

def back_low(kept, grad):
    return (low(grad),)
low.defvjp(low_keep, low_pass)
low_back.defvjp(back_keep, back_low)
ADAPTER_SCALE = 8.0
EPS_NORM = 1e-05
BETA_ONE = 0.9
BETA_TWO = 0.999
RATE = 0.02
DECAY = 0.01
EPS_ADAM = 1e-08
CLIP = 0.02
NEGATIVE = -1e+30
HIGH = lax.Precision.HIGHEST

def matrix_product(left, right):
    return jnp.dot(left, right, precision=HIGH, preferred_element_type=jnp.float32)

def layer_norm(hidden_rows, norm_gain, norm_shift):
    row_mean = lax.optimization_barrier(jnp.mean(hidden_rows, axis=-1, keepdims=True))
    centered = hidden_rows - row_mean
    var = lax.optimization_barrier(jnp.mean(centered * centered, axis=-1, keepdims=True))
    return centered * lax.rsqrt(var + EPS_NORM) * norm_gain + norm_shift

def log_total(values):
    top = lax.optimization_barrier(jnp.max(values, axis=-1, keepdims=True))
    return top + jnp.log(lax.optimization_barrier(jnp.sum(jnp.exp(values - top), axis=-1, keepdims=True)))

def adapter_term(input_rows, down_maps, up_maps):
    inner_product = low_back(low(matrix_product(input_rows, low(down_maps))))
    return ADAPTER_SCALE * matrix_product(inner_product, low(up_maps))

def block(hidden_rows, row_lengths, attention_weight, feed_input, feed_output, small, down_width, down_feed, up_maps_every):
    base = 5 * MODEL_WIDTH + HIDDEN_UNITS
    coeff_query_key = small[:3 * MODEL_WIDTH]
    coeff_output = small[3 * MODEL_WIDTH:4 * MODEL_WIDTH]
    coeff_feed_input = small[4 * MODEL_WIDTH:4 * MODEL_WIDTH + HIDDEN_UNITS]
    coeff_feed_output = small[4 * MODEL_WIDTH + HIDDEN_UNITS:base]
    gain_one = small[base:base + MODEL_WIDTH]
    shift_one = small[base + MODEL_WIDTH:base + 2 * MODEL_WIDTH]
    gain_two = small[base + 2 * MODEL_WIDTH:base + 3 * MODEL_WIDTH]
    shift_two = small[base + 3 * MODEL_WIDTH:base + 4 * MODEL_WIDTH]
    rows = row_lengths.shape[0]
    seq = hidden_rows.shape[0] // rows
    attention_values = low(layer_norm(hidden_rows, gain_one, shift_one))
    query_key_value = matrix_product(attention_values, attention_weight[:, :3 * MODEL_WIDTH]) + coeff_query_key + adapter_term(attention_values, down_width[:, :ADAPTER_RANK], up_maps_every[:, :3 * MODEL_WIDTH])
    query_key_value = low_back(low(query_key_value))
    parts = query_key_value.reshape(rows, seq, 3, H, HD)
    query = parts[:, :, 0]
    key = parts[:, :, 1]
    value = parts[:, :, 2]
    raw = low_back(jnp.einsum('bqhe,bkhe->bhqk', query, key, precision=HIGH) * HD ** (-0.5))
    qpos = lax.broadcasted_iota(jnp.int32, (seq, seq), 0)
    kpos = lax.broadcasted_iota(jnp.int32, (seq, seq), 1)
    allowed = (kpos <= qpos)[None, None] & (kpos[None, None] < row_lengths[:, None, None, None])
    masked = jnp.where(allowed, raw, NEGATIVE)
    prob = low(jnp.exp(masked - log_total(masked)))
    attention_output = jnp.einsum('bhqk,bkhe->bqhe', prob, value, precision=HIGH)
    attention_output = low_back(low(attention_output.reshape(rows * seq, MODEL_WIDTH)))
    residual_branch = matrix_product(attention_output, attention_weight[:, 3 * MODEL_WIDTH:]) + coeff_output + adapter_term(attention_output, down_width[:, ADAPTER_RANK:2 * ADAPTER_RANK], up_maps_every[:, 3 * MODEL_WIDTH:4 * MODEL_WIDTH])
    middle_rows = hidden_rows + low_back(residual_branch)
    feed_values = low(layer_norm(middle_rows, gain_two, shift_two))
    prenorm_rows = low_back(matrix_product(feed_values, feed_input) + coeff_feed_input + adapter_term(feed_values, down_width[:, 2 * ADAPTER_RANK:], up_maps_every[:, 4 * MODEL_WIDTH:4 * MODEL_WIDTH + HIDDEN_UNITS]))
    activation = low(jax.nn.gelu(prenorm_rows, approximate=True))
    feed_branch = matrix_product(activation, feed_output) + coeff_feed_output + adapter_term(activation, down_feed, up_maps_every[:, 4 * MODEL_WIDTH + HIDDEN_UNITS:])
    return middle_rows + low_back(feed_branch)

def moment_update(weight, first, second, gradient_value, scale_factor, step_number):
    clipped = gradient_value * scale_factor
    first_new = BETA_ONE * first + (1.0 - BETA_ONE) * clipped
    second_new = BETA_TWO * second + (1.0 - BETA_TWO) * clipped * clipped
    first_hat = first_new / (1.0 - BETA_ONE ** step_number)
    second_hat = second_new / (1.0 - BETA_TWO ** step_number)
    weight_new = weight - RATE * (first_hat / (jnp.sqrt(second_hat) + EPS_ADAM) + DECAY * weight)
    return (weight_new, first_new, second_new)

def reference(input_token_ids, lengths, scored_slots, scored_targets, wte, wpe, frozen_attention, frozen_feed_input, frozen_feed_output, frozen_bias_gain, final_norm_params, adapter_down, adapter_down_feed, adapter_up, first_moment_down, first_moment_feed, first_moment_up, second_moment_down, second_moment_feed, second_moment_up, optimizer_step):
    table = wte.astype(jnp.float32)
    places = wpe.astype(jnp.float32)
    attn_all = frozen_attention.astype(jnp.float32)
    mlp_in_all = frozen_feed_input.astype(jnp.float32)
    mlp_out_all = frozen_feed_output.astype(jnp.float32)
    small_all = frozen_bias_gain.astype(jnp.float32)
    final = final_norm_params.astype(jnp.float32)
    group = 16
    groups = MICRO * ROWS // group
    ids = input_token_ids.reshape(groups, group, SEQ)
    row_lengths = lengths.reshape(groups, group)
    spots = scored_slots.reshape(groups, group, LOSS_POS)
    targets = scored_targets.reshape(groups, group, LOSS_POS)

    def summed_loss(down_width, down_feed, up_maps_every):

        def group_step(carry, data):
            gid, glen, gpos, gtgt = data
            hidden_rows = (table[gid] + places[None]).reshape(group * SEQ, MODEL_WIDTH)
            for layer_index in range(LAYER_COUNT):
                hidden_rows = block(hidden_rows, glen, attn_all[layer_index], mlp_in_all[layer_index], mlp_out_all[layer_index], small_all[layer_index], down_width[layer_index], down_feed[layer_index], up_maps_every[layer_index])
            hidden = low(layer_norm(hidden_rows, final[0], final[1]))
            index = (gpos + jnp.arange(group, dtype=jnp.int32)[:, None] * SEQ).reshape(-1)
            logits = low_back(jnp.dot(hidden[index], table.T, precision=HIGH, preferred_element_type=jnp.float32))
            lse = log_total(logits)[:, 0]
            picked = jnp.take_along_axis(logits, gtgt.reshape(-1, 1), axis=1)[:, 0]
            valid = (gpos < glen[:, None]).reshape(-1).astype(jnp.float32)
            terms = (lse - picked) * valid
            return (carry + jnp.sum(terms), terms.reshape(group, LOSS_POS))
        output_rows, per_rows = lax.scan(jax.checkpoint(group_step), jnp.zeros((), jnp.float32), (ids, row_lengths, spots, targets))
        return (output_rows, per_rows.reshape(MICRO, ROWS, LOSS_POS))
    running_total, pullback, row_losses = jax.vjp(summed_loss, adapter_down, adapter_down_feed, adapter_up, has_aux=True)
    gradient_tree = pullback(jnp.ones((), jnp.float32))
    count = jnp.sum((scored_slots < lengths[:, :, None]).astype(jnp.float32))
    gradient_tree = [g / count for g in gradient_tree]
    norm = jnp.sqrt(sum((jnp.sum(g * g) for g in gradient_tree)))
    scale_factor = jnp.minimum(1.0, CLIP / (norm + 1e-06))
    step_number = optimizer_step[0].astype(jnp.float32)
    updated_down, updated_first_down, updated_second_down = moment_update(adapter_down, first_moment_down, second_moment_down, gradient_tree[0], scale_factor, step_number)
    updated_feed, updated_first_feed, updated_second_feed = moment_update(adapter_down_feed, first_moment_feed, second_moment_feed, gradient_tree[1], scale_factor, step_number)
    updated_up, updated_first_up, updated_second_up = moment_update(adapter_up, first_moment_up, second_moment_up, gradient_tree[2], scale_factor, step_number)
    return (running_total / count, norm, updated_down, updated_feed, updated_up, updated_first_down, updated_first_feed, updated_first_up, updated_second_down, updated_second_feed, updated_second_up, row_losses)
```

```python
from functools import partial

import jax
import jax.numpy as jnp
from jax import lax
from jax.experimental import pallas as pl
from jax.experimental.pallas import tpu as pltpu
from jax.sharding import PartitionSpec as P

MODEL_WIDTH = 1024
H = 16
HD = 64
HIDDEN_UNITS = 4096
ADAPTER_RANK = 4


ADAPTER_SCALE = 8.0
EPS_NORM = 1e-05
BETA_ONE = 0.9
BETA_TWO = 0.999
RATE = 0.02
DECAY = 0.01
EPS_ADAM = 1e-08
CLIP = 0.02
NEGATIVE = -1e30


def product_plain(left, right):
    return jnp.dot(left, right, preferred_element_type=jnp.float32)


def product_left_transposed(left, right):
    return lax.dot_general(
        left, right, (((0,), (0,)), ((), ())), preferred_element_type=jnp.float32
    )


def product_right_transposed(left, right):
    return lax.dot_general(
        left, right, (((1,), (1,)), ((), ())), preferred_element_type=jnp.float32
    )


def norm_fwd(hidden_rows, norm_gain, norm_shift):
    row_mean = jnp.mean(hidden_rows, axis=-1, keepdims=True)
    centered = hidden_rows - row_mean
    inverse_deviation = lax.rsqrt(jnp.mean(centered * centered, axis=-1, keepdims=True) + EPS_NORM)
    normalized_rows = centered * inverse_deviation
    return (normalized_rows * norm_gain + norm_shift, normalized_rows, inverse_deviation)


def norm_backward(gradient_value, normalized_rows, inverse_deviation, norm_gain):
    scaled_rows = gradient_value * norm_gain
    return inverse_deviation * (
        scaled_rows
        - jnp.mean(scaled_rows, axis=-1, keepdims=True)
        - normalized_rows * jnp.mean(scaled_rows * normalized_rows, axis=-1, keepdims=True)
    )


def moment_update(weight, first, second, gradient_value, scale_factor, step_number):
    clipped = gradient_value * scale_factor
    first_new = BETA_ONE * first + (1.0 - BETA_ONE) * clipped
    second_new = BETA_TWO * second + (1.0 - BETA_TWO) * clipped * clipped
    first_hat = first_new / (1.0 - BETA_ONE**step_number)
    second_hat = second_new / (1.0 - BETA_TWO**step_number)
    weight_new = weight - RATE * (first_hat / (jnp.sqrt(second_hat) + EPS_ADAM) + DECAY * weight)
    return (weight_new, first_new, second_new)


CAPACITY = 80


def attention_scores(query, key, query_slots, row_lengths):
    raw = jnp.einsum("bqhe,bkhe->bhqk", query, key, preferred_element_type=jnp.float32) * HD ** (
        -0.5
    )
    kpos = jnp.arange(key.shape[1], dtype=jnp.int32)[None, None, :]
    allowed = (kpos <= query_slots[:, :, None]) & (kpos < row_lengths[:, None, None])
    return jnp.where(allowed[:, None], raw, NEGATIVE)


def attend(query, key, value, query_slots, row_lengths):
    masked = attention_scores(query, key, query_slots, row_lengths)
    top = jnp.max(masked, axis=-1, keepdims=True)
    lse = top + jnp.log(jnp.sum(jnp.exp(masked - top), axis=-1, keepdims=True))
    weights = jnp.exp(masked - lse).astype(jnp.bfloat16)
    output = jnp.einsum("bhqk,bkhe->bqhe", weights, value, preferred_element_type=jnp.float32)
    return (output.reshape(-1, MODEL_WIDTH).astype(jnp.bfloat16), lse)


def attend_back(d_heads, query, key, value, lse, query_slots, row_lengths):
    masked = attention_scores(query, key, query_slots, row_lengths)
    prob = jnp.exp(masked - lse)
    d_heads = d_heads.reshape(query.shape)
    d_prob = jnp.einsum("bqhe,bkhe->bhqk", d_heads, value, preferred_element_type=jnp.float32)
    d_value = jnp.einsum(
        "bhqk,bqhe->bkhe", prob.astype(jnp.bfloat16), d_heads, preferred_element_type=jnp.float32
    )
    d_raw = (prob * (d_prob - jnp.sum(prob * d_prob, axis=-1, keepdims=True))).astype(jnp.bfloat16)
    d_query = jnp.einsum(
        "bhqk,bkhe->bqhe", d_raw, key, preferred_element_type=jnp.float32
    ) * HD ** (-0.5)
    d_key = jnp.einsum(
        "bhqk,bqhe->bkhe", d_raw, query, preferred_element_type=jnp.float32
    ) * HD ** (-0.5)

    def flat(part):
        return part.reshape(-1, MODEL_WIDTH).astype(jnp.bfloat16)

    return flat(d_query), flat(d_key), flat(d_value)


def projection(rows_low, weight, bias, down, up):
    inner = product_plain(rows_low, down).astype(jnp.bfloat16)
    return (
        product_plain(rows_low, weight) + bias + ADAPTER_SCALE * product_plain(inner, up),
        inner,
    )


def projection_back(gradient_low, rows_low, inner, weight, down, up, into_rows=True):
    grad_up = ADAPTER_SCALE * product_left_transposed(inner, gradient_low)
    d_inner = (ADAPTER_SCALE * product_right_transposed(gradient_low, up)).astype(jnp.bfloat16)
    grad_down = product_left_transposed(d_inner, rows_low)
    d_rows = None
    if into_rows:
        d_rows = product_right_transposed(gradient_low, weight) + product_right_transposed(
            d_inner, down
        )
    return grad_down, grad_up, d_rows


def feed_forward(middle_rows, weights):
    feed_values, m_hat, m_rstd = norm_fwd(middle_rows, weights["g_two"], weights["b_two"])
    feed_low = feed_values.astype(jnp.bfloat16)
    prenorm, um = projection(
        feed_low, weights["w_fc"], weights["c_fc"], weights["d_fc"], weights["u_fc"]
    )
    act_low = jax.nn.gelu(prenorm, approximate=True).astype(jnp.bfloat16)
    branch, ug = projection(
        act_low, weights["w_fp"], weights["c_fp"], weights["d_fp"], weights["u_fp"]
    )
    return middle_rows + branch, (m_hat, m_rstd, feed_low, um, prenorm, act_low, ug)


def feed_backward(gradient_value, weights, saved):
    m_hat, m_rstd, feed_low, um, prenorm, act_low, ug = saved
    grad_dfp, grad_ufp, d_act = projection_back(
        gradient_value.astype(jnp.bfloat16),
        act_low,
        ug,
        weights["w_fp"],
        weights["d_fp"],
        weights["u_fp"],
    )
    d_pre = jax.vjp(partial(jax.nn.gelu, approximate=True), prenorm)[1](d_act)[0].astype(
        jnp.bfloat16
    )
    grad_dfc, grad_ufc, d_feed = projection_back(
        d_pre, feed_low, um, weights["w_fc"], weights["d_fc"], weights["u_fc"]
    )
    grad_mid = gradient_value + norm_backward(d_feed, m_hat, m_rstd, weights["g_two"])
    return grad_mid, (grad_dfp, grad_ufp, grad_dfc, grad_ufc)


def unpack(small, down, down_feed, up):
    smallf = small.astype(jnp.float32)
    start = 5 * MODEL_WIDTH + HIDDEN_UNITS
    down_low = down.astype(jnp.bfloat16)
    up_low = up.astype(jnp.bfloat16)
    return {
        "c_qkv": smallf[: 3 * MODEL_WIDTH],
        "c_o": smallf[3 * MODEL_WIDTH : 4 * MODEL_WIDTH],
        "c_fc": smallf[4 * MODEL_WIDTH : 4 * MODEL_WIDTH + HIDDEN_UNITS],
        "c_fp": smallf[4 * MODEL_WIDTH + HIDDEN_UNITS : start],
        "g_one": smallf[start : start + MODEL_WIDTH],
        "b_one": smallf[start + MODEL_WIDTH : start + 2 * MODEL_WIDTH],
        "g_two": smallf[start + 2 * MODEL_WIDTH : start + 3 * MODEL_WIDTH],
        "b_two": smallf[start + 3 * MODEL_WIDTH : start + 4 * MODEL_WIDTH],
        "d_qkv": down_low[:, :ADAPTER_RANK],
        "d_o": down_low[:, ADAPTER_RANK : 2 * ADAPTER_RANK],
        "d_fc": down_low[:, 2 * ADAPTER_RANK :],
        "d_fp": down_feed.astype(jnp.bfloat16),
        "u_qkv": up_low[:, : 3 * MODEL_WIDTH],
        "u_o": up_low[:, 3 * MODEL_WIDTH : 4 * MODEL_WIDTH],
        "u_fc": up_low[:, 4 * MODEL_WIDTH : 4 * MODEL_WIDTH + HIDDEN_UNITS],
        "u_fp": up_low[:, 4 * MODEL_WIDTH + HIDDEN_UNITS :],
    }


def lookup(table, ids, needed):
    shards = lax.axis_size("fsdp")
    total = ids.shape[0]
    order = jnp.arange(total, dtype=jnp.int32)
    owner = ids // table.shape[0]
    local = ids - owner * table.shape[0]
    same = (ids[:, None] == ids[None, :]) & needed[None, :]
    first = jnp.min(jnp.where(same, order[None, :], total), axis=1)
    leads = needed & (first == order)
    rank = jnp.sum(
        (leads & (owner[:, None] == owner[None, :]) & (order[None, :] < first[:, None])).astype(
            jnp.int32
        ),
        axis=1,
    )
    rounds = (jnp.max(jnp.where(needed, rank, 0)) + CAPACITY) // CAPACITY

    spots = jnp.arange(shards * CAPACITY, dtype=jnp.int32)

    def serve(turn):
        place = jnp.where(
            needed & (rank // CAPACITY == turn), owner * CAPACITY + rank % CAPACITY, -1
        )
        asked = jnp.sum(
            jnp.where(leads[:, None] & (place[:, None] == spots[None, :]), local[:, None], 0), axis=0
        ).reshape(shards, CAPACITY)
        message = jnp.concatenate([asked, jnp.full((shards, 1), rounds, jnp.int32)], 1)
        got = lax.all_to_all(message, "fsdp", 0, 0, tiled=True)
        sent = table.at[got[:, :CAPACITY].reshape(-1)].get(mode="promise_in_bounds")
        back = lax.all_to_all(sent, "fsdp", 0, 0, tiled=True)
        pick = (place[:, None] == spots[None, :]).astype(jnp.bfloat16)
        return product_plain(pick, back), jnp.max(got[:, CAPACITY])

    found, most = serve(0)
    groups = lax.axis_size("dp")
    others = [
        lax.ppermute(most, "dp", [(i, (i + k) % groups) for i in range(groups)])
        for k in range(1, groups)
    ]
    for other in others:
        most = jnp.maximum(most, other)
    return lax.fori_loop(1, most, lambda turn, so_far: so_far + serve(turn)[0], found)


def swap(part, bit):
    return lax.ppermute(part, "fsdp", [(i, i ^ bit) for i in range(lax.axis_size("fsdp"))])


def tie(parts, before):
    parts, _ = lax.optimization_barrier((parts, before))
    return parts


def place_kernel(places, rows, *refs):
    pieces, out = refs[:-1], refs[-1]
    me = lax.axis_index("fsdp")
    for (offset, first), piece in zip(places, pieces):
        start = pl.multiple_of(jnp.bitwise_xor(me, offset) * rows + first, 16)
        out[pl.ds(start, piece.shape[0]), :] = piece[...]


def placed(pieces, rows):
    places = tuple((offset, first) for offset, first, _ in pieces)
    arrays = [array for _, _, array in pieces]
    columns = arrays[0].shape[1]
    height = rows * lax.axis_size("fsdp")
    tile = columns // 4
    return pl.pallas_call(
        partial(place_kernel, places, rows),
        out_shape=jax.ShapeDtypeStruct((height, columns), arrays[0].dtype),
        grid=(columns // tile,),
        in_specs=[pl.BlockSpec((a.shape[0], tile), lambda j: (0, j)) for a in arrays],
        out_specs=pl.BlockSpec((height, tile), lambda j: (0, j)),
        compiler_params=pltpu.CompilerParams(vmem_limit_bytes=32 * 2**20),
        cost_estimate=pl.CostEstimate(
            flops=0, bytes_accessed=4 * height * columns, transcendentals=0
        ),
    )(*arrays)


def gather_units(units):
    if lax.axis_size("fsdp") != 8:
        return [lax.all_gather(unit, "fsdp", axis=0, tiled=True) for unit in units]
    wholes = []
    near = ()
    waiting = None
    for unit in list(units) + [None]:
        done = near
        if unit is not None:
            own = tie(unit, near)
            near = (swap(own, 2), swap(own, 4))
        if waiting is not None:
            before, (one, two) = waiting
            rows = before.shape[0]
            half = rows // 2
            far = (swap(one[:half], 4), swap(two[half:], 2))
            wholes.append(
                placed(
                    [
                        (0, 0, before),
                        (1, 0, swap(before, 1)),
                        (2, 0, one),
                        (3, 0, swap(one, 1)),
                        (4, 0, two),
                        (5, 0, swap(two, 1)),
                        (6, 0, far[0]),
                        (6, half, far[1]),
                        (7, 0, swap(far[0], 1)),
                        (7, half, swap(far[1], 1)),
                    ],
                    rows,
                )
            )
        waiting = (own, near)
    return wholes


def everywhere(part):
    shards = lax.axis_size("fsdp")
    return lax.all_to_all(
        jnp.tile(part, (shards,) + (1,) * (part.ndim - 1)), "fsdp", 0, 0, tiled=True
    )


def owned_parts(parts):
    shards = lax.axis_size("fsdp")
    rows = parts.shape[0] // shards
    return lax.all_to_all(parts, "fsdp", 0, 0, tiled=True).reshape(
        (shards, rows) + parts.shape[1:]
    )


def split_feed_forward(middle_rows, weights):
    feed_values, m_hat, m_rstd = norm_fwd(middle_rows, weights["g_two"], weights["b_two"])
    feed_low = everywhere(feed_values.astype(jnp.bfloat16))
    prenorm, um = projection(
        feed_low, weights["w_fc"], weights["c_fc"], weights["d_fc"], weights["u_fc"]
    )
    act_low = jax.nn.gelu(prenorm, approximate=True).astype(jnp.bfloat16)
    branch, ug = projection(act_low, weights["w_fp"], 0.0, weights["d_fp"], weights["u_fp"])
    branch = jnp.sum(owned_parts(branch.astype(jnp.bfloat16)).astype(jnp.float32), axis=0)
    return (
        middle_rows + (branch + weights["c_fp"]),
        (m_hat, m_rstd, feed_low, um, prenorm, act_low, ug),
    )


def split_feed_backward(gradient_value, weights, saved):
    m_hat, m_rstd, feed_low, um, prenorm, act_low, ug = saved
    grad_dfp, grad_ufp, d_act = projection_back(
        everywhere(gradient_value.astype(jnp.bfloat16)),
        act_low,
        ug,
        weights["w_fp"],
        weights["d_fp"],
        weights["u_fp"],
    )
    d_pre = jax.vjp(partial(jax.nn.gelu, approximate=True), prenorm)[1](d_act)[0].astype(
        jnp.bfloat16
    )
    grad_dfc, grad_ufc, d_feed = projection_back(
        d_pre, feed_low, um, weights["w_fc"], weights["d_fc"], weights["u_fc"]
    )
    d_feed = jnp.sum(owned_parts(d_feed.astype(jnp.bfloat16)).astype(jnp.float32), axis=0)
    grad_mid = gradient_value + norm_backward(d_feed, m_hat, m_rstd, weights["g_two"])
    return grad_mid, (grad_dfp, grad_ufp, grad_dfc, grad_ufc)


def summed_everywhere(gradients, extras):
    shards = lax.axis_size("fsdp")
    groups = lax.axis_size("dp")
    rows, columns = gradients.shape
    width = columns // shards
    blocks = gradients.reshape(rows, shards, width).transpose(1, 0, 2)
    tail = jnp.zeros((rows, 128), jnp.float32).at[0, : extras.shape[0]].set(extras)
    blocks = jnp.concatenate([blocks, jnp.tile(tail[None], (shards, 1, 1))], 2)
    block = jnp.sum(owned_parts(blocks.reshape(shards * rows, -1)), axis=0)
    others = [
        lax.ppermute(block, "dp", [(i, (i + k) % groups) for i in range(groups)])
        for k in range(1, groups)
    ]
    stacked = jnp.stack([block] + others)
    order = (lax.axis_index("dp") - jnp.arange(groups)) % groups
    ranks = (order[None, :] == jnp.arange(groups)[:, None])[:, :, None, None]
    total = jnp.sum(jnp.sum(jnp.where(ranks, stacked[None], 0.0), axis=1), axis=0)
    whole = everywhere(total).reshape(shards, rows, width + 128)
    return (
        whole[:, :, :width].transpose(1, 0, 2).reshape(rows, columns),
        whole[0, 0, width : width + extras.shape[0]],
    )


def body(
    input_token_ids,
    lengths,
    scored_slots,
    scored_targets,
    wte,
    wpe,
    frozen_attention,
    frozen_feed_input,
    frozen_feed_output,
    frozen_bias_gain,
    final_norm_params,
    adapter_down,
    adapter_down_feed,
    adapter_up,
    first_moment_down,
    first_moment_feed,
    first_moment_up,
    second_moment_down,
    second_moment_feed,
    second_moment_up,
    optimizer_step,
):
    micro, seqs, seq = input_token_ids.shape
    rows = micro * seqs
    picks = scored_slots.shape[2]
    layers = frozen_attention.shape[0]
    last = layers - 1
    shards = lax.axis_size("fsdp")
    row_lengths = lengths.reshape(rows)
    slots = scored_slots.reshape(rows, picks)
    valid = slots < row_lengths[:, None]
    mask = valid.reshape(-1).astype(jnp.float32)
    all_slots = jnp.tile(jnp.arange(seq, dtype=jnp.int32)[None], (rows, 1))
    gain_final = final_norm_params[0].astype(jnp.float32)
    shift_final = final_norm_params[1].astype(jnp.float32)

    me = lax.axis_index("fsdp")
    small_all = everywhere(frozen_bias_gain[None]).transpose(1, 0, 2).reshape(layers, -1)
    weights = [
        unpack(small_all[layer], adapter_down[layer], adapter_down_feed[layer], adapter_up[layer])
        for layer in range(layers)
    ]
    units = []
    for layer in range(layers):
        units.append(frozen_attention[layer])
        if layer < last:
            units += [frozen_feed_input[layer], frozen_feed_output[layer]]
    wholes = gather_units(units)
    for layer in range(layers):
        attention = wholes[3 * layer]
        weights[layer]["w_qkv"] = attention[:, : 3 * MODEL_WIDTH]
        weights[layer]["w_o"] = attention[:, 3 * MODEL_WIDTH :]
        if layer < last:
            weights[layer]["w_fc"] = wholes[3 * layer + 1]
            weights[layer]["w_fp"] = wholes[3 * layer + 2]
    share = HIDDEN_UNITS // shards
    own_units = partial(lax.dynamic_slice_in_dim, start_index=me * share, slice_size=share)
    weights[last]["w_fc"] = lax.all_to_all(
        tie(frozen_feed_input[last], wholes[2]), "fsdp", 1, 0, tiled=True
    )
    weights[last]["w_fp"] = frozen_feed_output[last]
    weights[last]["c_fc"] = own_units(weights[last]["c_fc"])
    weights[last]["d_fp"] = own_units(weights[last]["d_fp"])
    weights[last]["u_fc"] = own_units(weights[last]["u_fc"], axis=1)

    useful = jnp.max(jnp.where(valid, slots, -1), axis=1)
    needed = jnp.concatenate([(all_slots <= useful[:, None]).reshape(-1), valid.reshape(-1)])
    ids = jnp.concatenate([input_token_ids.reshape(-1), scored_targets.reshape(-1)])
    looked_up = lookup(wte, ids, needed)
    hidden = looked_up[: rows * seq] + jnp.tile(wpe.astype(jnp.float32), (rows, 1))
    target_rows = looked_up[rows * seq :]

    def heads(part):
        return part.reshape(rows, -1, H, HD)

    saved_layers = []
    for layer in range(last):
        w = weights[layer]
        values, a_hat, a_rstd = norm_fwd(hidden, w["g_one"], w["b_one"])
        a_low = values.astype(jnp.bfloat16)
        qkv, ua = projection(a_low, w["w_qkv"], w["c_qkv"], w["d_qkv"], w["u_qkv"])
        qkv_low = qkv.astype(jnp.bfloat16)
        query, key, value = (heads(part) for part in jnp.split(qkv_low, 3, axis=1))
        o_low, lse = attend(query, key, value, all_slots, row_lengths)
        branch, uo = projection(o_low, w["w_o"], w["c_o"], w["d_o"], w["u_o"])
        middle = hidden + branch
        hidden, feed_saved = feed_forward(middle, w)
        saved_layers.append((a_hat, a_rstd, a_low, ua, query, key, value, lse, o_low, uo, feed_saved))

    w = weights[last]
    values, a_hat, a_rstd = norm_fwd(hidden, w["g_one"], w["b_one"])
    a_low = values.astype(jnp.bfloat16)
    picked = (slots[:, :, None] == all_slots[:, None, :]).astype(jnp.bfloat16)
    flat_index = (slots + seq * jnp.arange(rows, dtype=jnp.int32)[:, None]).reshape(-1)
    a_sel = jnp.einsum(
        "rps,rsd->rpd",
        picked,
        a_low.reshape(rows, seq, -1),
        preferred_element_type=jnp.bfloat16,
    ).reshape(rows * picks, -1)
    hidden_sel = jnp.take(hidden, flat_index, axis=0)
    split = MODEL_WIDTH
    kv, ua = projection(
        a_low, w["w_qkv"][:, split:], w["c_qkv"][split:], w["d_qkv"], w["u_qkv"][:, split:]
    )
    q_sel, ua_sel = projection(
        a_sel, w["w_qkv"][:, :split], w["c_qkv"][:split], w["d_qkv"], w["u_qkv"][:, :split]
    )
    kv_low = kv.astype(jnp.bfloat16)
    key, value = heads(kv_low[:, :split]), heads(kv_low[:, split:])
    query = heads(q_sel.astype(jnp.bfloat16))
    o_low, lse = attend(query, key, value, slots, row_lengths)
    branch, uo = projection(o_low, w["w_o"], w["c_o"], w["d_o"], w["u_o"])
    middle = hidden_sel + branch
    final, feed_saved = split_feed_forward(middle, w)

    h_val, h_hat, h_rstd = norm_fwd(final, gain_final, shift_final)
    h_low = h_val.astype(jnp.bfloat16)
    h_all = everywhere(h_low)
    logits = product_right_transposed(h_all, wte)
    top = jnp.max(logits, axis=-1, keepdims=True)
    weight_low = jnp.exp(logits - top).astype(jnp.bfloat16)
    part_sum = jnp.sum(jnp.exp(logits - top), axis=-1, keepdims=True)
    part_rows = product_plain(weight_low, wte).astype(jnp.bfloat16)
    got_rows = owned_parts(part_rows)
    got_stats = owned_parts(jnp.concatenate([top, part_sum], 1))
    whole_top = jnp.max(got_stats[:, :, 0], axis=0)
    whole_lse = whole_top + jnp.log(
        jnp.sum(got_stats[:, :, 1] * jnp.exp(got_stats[:, :, 0] - whole_top), axis=0)
    )
    shares = jnp.exp(got_stats[:, :, 0] - whole_lse)
    target_logit = jnp.sum(h_low.astype(jnp.float32) * target_rows, axis=-1)
    own_terms = (whole_lse - target_logit) * mask
    d_hidden = mask[:, None] * (
        jnp.sum(got_rows.astype(jnp.float32) * shares[:, :, None], axis=0) - target_rows
    )
    gradient = norm_backward(d_hidden, h_hat, h_rstd, gain_final)

    grads = [None] * layers
    gradient, feed_grads = split_feed_backward(gradient, w, feed_saved)
    grad_do, grad_uo, d_heads = projection_back(
        gradient.astype(jnp.bfloat16), o_low, uo, w["w_o"], w["d_o"], w["u_o"]
    )
    d_query, d_key, d_value = attend_back(
        d_heads.astype(jnp.bfloat16), query, key, value, lse, slots, row_lengths
    )
    grad_dq, grad_uq, d_sel = projection_back(
        d_query, a_sel, ua_sel, w["w_qkv"][:, :split], w["d_qkv"], w["u_qkv"][:, :split]
    )
    d_kv = jnp.concatenate([d_key, d_value], 1)
    grad_dkv, grad_ukv, d_all = projection_back(
        d_kv, a_low, ua, w["w_qkv"][:, split:], w["d_qkv"], w["u_qkv"][:, split:]
    )
    own_first = jnp.zeros((ADAPTER_RANK, HIDDEN_UNITS), jnp.float32)
    grads[last] = [
        grad_dq + grad_dkv,
        grad_do,
        feed_grads[2],
        lax.dynamic_update_slice_in_dim(own_first, feed_grads[0], me * share, 1),
        grad_uq,
        grad_ukv,
        grad_uo,
        lax.dynamic_update_slice_in_dim(own_first, feed_grads[3], me * share, 1),
        feed_grads[1],
    ]
    spread = jnp.einsum(
        "rps,rpd->rsd",
        picked.astype(jnp.float32),
        jnp.concatenate([d_sel, gradient], 1).reshape(rows, picks, -1),
        precision=lax.Precision.HIGHEST,
    ).reshape(rows * seq, -1)
    gradient = spread[:, MODEL_WIDTH:] + norm_backward(
        d_all + spread[:, :MODEL_WIDTH], a_hat, a_rstd, w["g_one"]
    )

    for layer in reversed(range(last)):
        w = weights[layer]
        a_hat, a_rstd, a_low, ua, query, key, value, lse, o_low, uo, feed_saved = saved_layers[layer]
        gradient, feed_grads = feed_backward(gradient, w, feed_saved)
        grad_do, grad_uo, d_heads = projection_back(
            gradient.astype(jnp.bfloat16), o_low, uo, w["w_o"], w["d_o"], w["u_o"]
        )
        d_qkv = jnp.concatenate(
            attend_back(
                d_heads.astype(jnp.bfloat16), query, key, value, lse, all_slots, row_lengths
            ),
            1,
        )
        grad_dqkv, grad_uqkv, d_norm = projection_back(
            d_qkv, a_low, ua, w["w_qkv"], w["d_qkv"], w["u_qkv"], into_rows=layer > 0
        )
        if layer > 0:
            gradient = gradient + norm_backward(d_norm, a_hat, a_rstd, w["g_one"])
        grads[layer] = [
            grad_dqkv,
            grad_do,
            feed_grads[2],
            feed_grads[0],
            grad_uqkv,
            grad_uo,
            feed_grads[3],
            feed_grads[1],
        ]

    gradients = jnp.concatenate([jnp.concatenate(parts, 1) for parts in grads], 0)
    gradients, totals = summed_everywhere(
        gradients, jnp.stack([jnp.sum(own_terms), jnp.sum(mask)])
    )
    loss_total, count = totals[0], totals[1]
    gradients = gradients / count
    norm = jnp.sqrt(jnp.sum(gradients * gradients))
    by_layer = gradients.reshape(layers, ADAPTER_RANK, -1)
    gradient_tree = [
        by_layer[:, :, : 3 * MODEL_WIDTH]
        .reshape(layers, ADAPTER_RANK, 3, MODEL_WIDTH)
        .transpose(0, 3, 2, 1)
        .reshape(layers, MODEL_WIDTH, 3 * ADAPTER_RANK),
        by_layer[:, :, 3 * MODEL_WIDTH : 3 * MODEL_WIDTH + HIDDEN_UNITS].transpose(0, 2, 1),
        by_layer[:, :, 3 * MODEL_WIDTH + HIDDEN_UNITS :],
    ]
    scale_factor = jnp.minimum(1.0, CLIP / (norm + 1e-06))
    step_number = optimizer_step[0].astype(jnp.float32)
    updated = [
        moment_update(weight, first, second, gradient_value, scale_factor, step_number)
        for weight, first, second, gradient_value in zip(
            (adapter_down, adapter_down_feed, adapter_up),
            (first_moment_down, first_moment_feed, first_moment_up),
            (second_moment_down, second_moment_feed, second_moment_up),
            gradient_tree,
        )
    ]
    return (
        loss_total / count,
        norm,
        *(part[0] for part in updated),
        *(part[1] for part in updated),
        *(part[2] for part in updated),
        own_terms.reshape(micro, seqs, picks),
    )


def solution(mesh):
    in_specs = (
        P(None, ("dp", "fsdp"), None),
        P(None, ("dp", "fsdp")),
        P(None, ("dp", "fsdp"), None),
        P(None, ("dp", "fsdp"), None),
        P("fsdp", None),
        P(),
        P(None, "fsdp", None),
        P(None, "fsdp", None),
        P(None, "fsdp", None),
        P(None, "fsdp"),
        P(),
        P(),
        P(),
        P(),
        P(),
        P(),
        P(),
        P(),
        P(),
        P(),
        P(),
    )
    out_specs = (
        P(),
        P(),
        P(),
        P(),
        P(),
        P(),
        P(),
        P(),
        P(),
        P(),
        P(),
        P(None, ("dp", "fsdp"), None),
    )
    return jax.shard_map(body, mesh=mesh, in_specs=in_specs, out_specs=out_specs, check_vma=False)
```

```python
import math
from functools import partial
from typing import NamedTuple

import jax
import jax.numpy as jnp
from jax import lax
from jax.experimental import pallas as pl
from jax.experimental.pallas import tpu as pltpu
from jax.sharding import PartitionSpec as P

MODEL_WIDTH = 1024
H = 16
HD = 64
HIDDEN_UNITS = 4096
ADAPTER_RANK = 4


ADAPTER_SCALE = 8.0
EPS_NORM = 1e-05
BETA_ONE = 0.9
BETA_TWO = 0.999
RATE = 0.02
DECAY = 0.01
EPS_ADAM = 1e-08
CLIP = 0.02
NEGATIVE = -1e30


def product_plain(left, right):
    return jnp.dot(left, right, preferred_element_type=jnp.float32)


def product_left_transposed(left, right):
    return lax.dot_general(
        left, right, (((0,), (0,)), ((), ())), preferred_element_type=jnp.float32
    )


def product_right_transposed(left, right):
    return lax.dot_general(
        left, right, (((1,), (1,)), ((), ())), preferred_element_type=jnp.float32
    )


def norm_fwd(hidden_rows, norm_gain, norm_shift):
    row_mean = jnp.mean(hidden_rows, axis=-1, keepdims=True)
    centered = hidden_rows - row_mean
    inverse_deviation = lax.rsqrt(jnp.mean(centered * centered, axis=-1, keepdims=True) + EPS_NORM)
    normalized_rows = centered * inverse_deviation
    return (normalized_rows * norm_gain + norm_shift, normalized_rows, inverse_deviation)


def norm_backward(gradient_value, normalized_rows, inverse_deviation, norm_gain):
    scaled_rows = gradient_value * norm_gain
    return inverse_deviation * (
        scaled_rows
        - jnp.mean(scaled_rows, axis=-1, keepdims=True)
        - normalized_rows * jnp.mean(scaled_rows * normalized_rows, axis=-1, keepdims=True)
    )


def moment_update(weight, first, second, gradient_value, scale_factor, step_number):
    clipped = gradient_value * scale_factor
    first_new = BETA_ONE * first + (1.0 - BETA_ONE) * clipped
    second_new = BETA_TWO * second + (1.0 - BETA_TWO) * clipped * clipped
    first_hat = first_new / (1.0 - BETA_ONE**step_number)
    second_hat = second_new / (1.0 - BETA_TWO**step_number)
    weight_new = weight - RATE * (first_hat / (jnp.sqrt(second_hat) + EPS_ADAM) + DECAY * weight)
    return (weight_new, first_new, second_new)


CAPACITY = 80


LANES = 16
HALF_TILE = 512
BLOCK = 1024
VMEM_BYTES = 63 * 2**20


def whole(array, *lead):
    shape = (None,) * len(lead) + array.shape[len(lead) :]
    place = lead + (0,) * (array.ndim - len(lead))
    return array, pl.BlockSpec(shape, lambda *_: place, pipeline_mode=pl.Buffered(1))


def strip(array, width, column, *lead):
    shape = (None,) * len(lead) + (array.shape[-2], width)
    if callable(column):
        return array, pl.BlockSpec(shape, lambda j, *_: lead + (0, column(j)))
    place = lead + (0, column)
    return array, pl.BlockSpec(shape, lambda *_: place, pipeline_mode=pl.Buffered(1))


def rows_strip(array, height, row, *lead):
    shape = (None,) * len(lead) + (height, array.shape[-1])
    return array, pl.BlockSpec(shape, lambda j, *_: lead + (row(j), 0))


def result(shape, dtype, block=None, place=None):
    kind = jax.ShapeDtypeStruct(shape, dtype)
    if block is None:
        block, zeros = shape, (0,) * len(shape)
        return kind, pl.BlockSpec(block, lambda *_: zeros)
    return kind, pl.BlockSpec(block, place)


def launch(kernel, grid, operands, results, scratch=(), scalars=(), flops=0):
    moved = sum(a.size * a.dtype.itemsize for a, _ in operands)
    return pl.pallas_call(
        kernel,
        out_shape=[kind for kind, _ in results],
        grid_spec=pltpu.PrefetchScalarGridSpec(
            num_scalar_prefetch=len(scalars),
            grid=grid,
            in_specs=[spec for _, spec in operands],
            out_specs=[spec for _, spec in results],
            scratch_shapes=list(scratch),
        ),
        compiler_params=pltpu.CompilerParams(vmem_limit_bytes=VMEM_BYTES),
        cost_estimate=pl.CostEstimate(flops=flops, bytes_accessed=moved, transcendentals=0),
    )(*scalars, *(a for a, _ in operands))


class Unit(NamedTuple):
    places: tuple
    arrays: tuple
    rows: int

    def operands(self):
        return [(array, pl.BlockSpec(memory_space=pltpu.HBM)) for array in self.arrays]


def shard_of(place):
    if isinstance(place, int):
        return place
    me = lax.axis_index("fsdp")
    return jnp.bitwise_xor(me, jnp.where(lax.rem(me, 2) == 0, *place))


def moves(unit, refs, target, sems, column, width):
    columns = pl.ds(pl.multiple_of(column * width, width), width)
    copies = []
    for n, (place, ref) in enumerate(zip(unit.places, refs)):
        start = pl.multiple_of(shard_of(place) * unit.rows, 16)
        copies.append(
            pltpu.make_async_copy(
                ref.at[:, columns], target.at[pl.ds(start, ref.shape[0]), :], sems.at[n]
            )
        )
    return copies


def begin(copies):
    for copy in copies:
        copy.start()


def finish(copies):
    for copy in copies:
        copy.wait()


def next_strip(unit, refs, slots, sems, width):
    j = pl.program_id(0)

    def strip_moves(step):
        slot = lax.rem(step, 2)
        return moves(unit, refs, slots.at[slot], sems.at[slot], step, width)

    pl.when(j == 0)(lambda: begin(strip_moves(j)))
    pl.when(j + 1 < pl.num_programs(0))(lambda: begin(strip_moves(j + 1)))
    finish(strip_moves(j))
    return slots.at[lax.rem(j, 2)]


def slots_for(unit, height, width):
    return [
        pltpu.VMEM((2, height, width), jnp.bfloat16),
        pltpu.SemaphoreType.DMA((2, len(unit.arrays))),
    ]


def one_slot_for(unit):
    return [
        pltpu.VMEM((MODEL_WIDTH, BLOCK), jnp.bfloat16),
        pltpu.SemaphoreType.DMA((len(unit.arrays),)),
    ]


def taken(refs, *units):
    groups = []
    for unit in units:
        groups.append(refs[: len(unit.arrays)])
        refs = refs[len(unit.arrays) :]
    return groups + [refs]


def over_rows(total, size, work):
    def turn(i, carry):
        work(pl.ds(pl.multiple_of(i * size, size), size))
        return carry

    lax.fori_loop(0, total // size, turn, 0)


def low(value):
    return value.astype(jnp.bfloat16)


def adapter(inner, up):
    return ADAPTER_SCALE * product_plain(inner, up)


def norm_into(out_ref, rows_ref, gain, shift):
    def part(rows):
        out_ref[rows, :] = low(norm_fwd(rows_ref[rows, :], gain, shift)[0])

    over_rows(rows_ref.shape[0], min(64, rows_ref.shape[0]), part)


def norm_back_into(out_ref, gradient_ref, rows_ref, gain, residual_ref=None):
    def part(rows):
        _, normalized, deviation = norm_fwd(rows_ref[rows, :], gain, 0.0)
        value = norm_backward(gradient_ref[rows, :], normalized, deviation, gain)
        if residual_ref is not None:
            value = value + residual_ref[rows, :]
        out_ref[rows, :] = value

    over_rows(rows_ref.shape[0], min(64, rows_ref.shape[0]), part)


def front_kernel(unit, *refs):
    pieces, refs = taken(refs, unit)
    x, gain, shift, bias, down, up, qkv, a, ua, slots, sems = refs
    weight = next_strip(unit, pieces, slots, sems, BLOCK)

    @pl.when(pl.program_id(0) == 0)
    def _():
        norm_into(a, x, gain[...], shift[...])
        ua[...] = low(product_right_transposed(a[...], down[...]))

    qkv[...] = low(product_plain(a[...], weight[...]) + bias[...] + adapter(ua[...], up[...]))


def front(x, unit, p, layer):
    tokens = x.shape[0]
    return launch(
        partial(front_kernel, unit),
        (3,),
        unit.operands()
        + [
            whole(x),
            strip(p["small"], BLOCK, 9, layer),
            strip(p["small"], BLOCK, 10, layer),
            strip(p["small"], BLOCK, lambda j: j, layer),
            whole(p["down_t"], layer, 0),
            strip(p["up"], BLOCK, lambda j: j, layer),
        ],
        [
            result((tokens, 3 * MODEL_WIDTH), jnp.bfloat16, (tokens, BLOCK), lambda j: (0, j)),
            result((tokens, MODEL_WIDTH), jnp.bfloat16),
            result((tokens, LANES), jnp.bfloat16),
        ],
        scratch=slots_for(unit, MODEL_WIDTH, BLOCK),
        flops=6 * tokens * MODEL_WIDTH**2,
    )


def pick_rows(index, source, target):
    def turn(i, carry):
        target[pl.ds(i, 1), :] = source[pl.ds(index[i], 1), :]
        return carry

    lax.fori_loop(0, target.shape[0], turn, 0)


def add_rows(index, source, target):
    def turn(i, carry):
        rows = pl.ds(index[i], 1)
        target[rows, :] = target[rows, :] + source[pl.ds(i, 1), :]
        return carry

    lax.fori_loop(0, source.shape[0], turn, 0)


def front_last_kernel(unit, index, *refs):
    pieces, refs = taken(refs, unit)
    x, gain, shift, bias, down, up, q, kv, a, a_sel, ua, ua_sel, x_sel, slots, sems = refs
    j = pl.program_id(0)
    weight = next_strip(unit, pieces, slots, sems, BLOCK)

    @pl.when(j == 0)
    def _():
        norm_into(a, x, gain[...], shift[...])
        ua[...] = low(product_right_transposed(a[...], down[...]))
        pick_rows(index, x, x_sel)
        norm_into(a_sel, x_sel, gain[...], shift[...])
        ua_sel[...] = low(product_right_transposed(a_sel[...], down[...]))

    @pl.when(j == 0)
    def _():
        q[...] = low(
            product_plain(a_sel[...], weight[...]) + bias[...] + adapter(ua_sel[...], up[...])
        )

    @pl.when(j > 0)
    def _():
        kv[...] = low(product_plain(a[...], weight[...]) + bias[...] + adapter(ua[...], up[...]))


def front_last(index, x, unit, p, layer):
    tokens, count = x.shape[0], index.shape[0]
    return launch(
        partial(front_last_kernel, unit),
        (3,),
        unit.operands()
        + [
            whole(x),
            strip(p["small"], BLOCK, 9, layer),
            strip(p["small"], BLOCK, 10, layer),
            strip(p["small"], BLOCK, lambda j: j, layer),
            whole(p["down_t"], layer, 0),
            strip(p["up"], BLOCK, lambda j: j, layer),
        ],
        [
            result((count, MODEL_WIDTH), jnp.bfloat16),
            result(
                (tokens, 2 * MODEL_WIDTH),
                jnp.bfloat16,
                (tokens, BLOCK),
                lambda j, *_: (0, jnp.maximum(j - 1, 0)),
            ),
            result((tokens, MODEL_WIDTH), jnp.bfloat16),
            result((count, MODEL_WIDTH), jnp.bfloat16),
            result((tokens, LANES), jnp.bfloat16),
            result((count, LANES), jnp.bfloat16),
            result((count, MODEL_WIDTH), jnp.float32),
        ],
        scratch=slots_for(unit, MODEL_WIDTH, BLOCK),
        scalars=(index,),
        flops=4 * tokens * MODEL_WIDTH**2,
    )


def attend_kernel(lengths, slots, query, key, value, out):
    length = lengths[pl.program_id(0)]
    kpos = lax.broadcasted_iota(jnp.int32, (query.shape[0], key.shape[0]), 1)
    allowed = (kpos <= slots[...]) & (kpos < length)
    heads = []
    for start in range(0, query.shape[1], HD):
        part = slice(start, start + HD)
        raw = product_right_transposed(query[:, part], key[:, part]) * HD ** (-0.5)
        raw = jnp.where(allowed, raw, NEGATIVE)
        prob = jnp.exp(raw - jnp.max(raw, axis=1, keepdims=True))
        prob = prob * (1.0 / jnp.sum(prob, axis=1, keepdims=True))
        heads.append(product_plain(low(prob), value[:, part]))
    out[...] = low(jnp.concatenate(heads, axis=1))


def own_lanes(count, heads):
    shape = (heads * count, heads * HD)
    row = lax.broadcasted_iota(jnp.int32, shape, 0) // count
    lane = lax.broadcasted_iota(jnp.int32, shape, 1) // HD
    return row == lane


def stacked_heads(rows, own):
    heads = own.shape[0] // rows.shape[0]
    tall = jnp.concatenate([rows.astype(jnp.float32)] * heads, axis=0)
    return low(jnp.where(own, tall, 0.0))


def own_heads(tall, own, count):
    tall = jnp.where(own, tall, 0.0)
    total = tall[:count]
    for start in range(count, tall.shape[0], count):
        total = total + tall[start : start + count]
    return total


def few_scores(length, slots, tall, key):
    raw = product_right_transposed(tall, key[...]) * HD ** (-0.5)
    kpos = lax.broadcasted_iota(jnp.int32, raw.shape, 1)
    places = jnp.concatenate([slots[...]] * (raw.shape[0] // slots.shape[0]), axis=0)
    raw = jnp.where((kpos <= places) & (kpos < length), raw, NEGATIVE)
    prob = jnp.exp(raw - jnp.max(raw, axis=1, keepdims=True))
    return prob * (1.0 / jnp.sum(prob, axis=1, keepdims=True))


def attend_few_kernel(lengths, slots, query, key, value, out):
    count = query.shape[0]
    own = own_lanes(count, query.shape[1] // HD)
    prob = few_scores(lengths[pl.program_id(0)], slots, stacked_heads(query[...], own), key)
    out[...] = low(own_heads(product_plain(low(prob), value[...]), own, count))


def attend_few_back_kernel(lengths, slots, query, key, value, d_out, d_query, d_key, d_value):
    count = query.shape[0]
    own = own_lanes(count, query.shape[1] // HD)
    tall = stacked_heads(query[...], own)
    d_tall = stacked_heads(d_out[...], own)
    prob = few_scores(lengths[pl.program_id(0)], slots, tall, key)
    d_prob = product_right_transposed(d_tall, value[...])
    d_raw = low(prob * (d_prob - jnp.sum(prob * d_prob, axis=1, keepdims=True)))
    d_value[...] = low(product_left_transposed(low(prob), d_tall))
    d_key[...] = low(product_left_transposed(d_raw, tall) * HD ** (-0.5))
    d_query[...] = low(own_heads(product_plain(d_raw, key[...]), own, count) * HD ** (-0.5))


def head_blocks(array, height, third, steps):
    offset = third * steps
    return array, pl.BlockSpec((height, MODEL_WIDTH // steps), lambda r, h, *_: (r, offset + h))


def head_steps(count):
    return 2 if count > 128 else 1


def attend(lengths, slots, query, key, value):
    rows, count = slots.shape
    seq = key[0].shape[0] // rows
    steps = head_steps(count)
    column = slots.reshape(-1, 1)
    (out,) = launch(
        attend_kernel if steps > 1 else attend_few_kernel,
        (rows, steps),
        [
            (column, pl.BlockSpec((count, 1), lambda r, h, *_: (r, 0))),
            head_blocks(query[0], count, query[1], steps),
            head_blocks(key[0], seq, key[1], steps),
            head_blocks(value[0], seq, value[1], steps),
        ],
        [
            result(
                (rows * count, MODEL_WIDTH),
                jnp.bfloat16,
                (count, MODEL_WIDTH // steps),
                lambda r, h, *_: (r, h),
            )
        ],
        scalars=(lengths,),
        flops=4 * rows * count * seq * MODEL_WIDTH,
    )
    return out


def attend_back_kernel(lengths, slots, query, key, value, d_out, d_query, d_key, d_value):
    length = lengths[pl.program_id(0)]
    kpos = lax.broadcasted_iota(jnp.int32, (key.shape[0], query.shape[0]), 0)
    allowed = (kpos <= slots[...]) & (kpos < length)
    parts = []
    for start in range(0, query.shape[1], HD):
        part = slice(start, start + HD)
        q, k, v, d_o = query[:, part], key[:, part], value[:, part], d_out[:, part]
        raw = product_right_transposed(k, q) * HD ** (-0.5)
        raw = jnp.where(allowed, raw, NEGATIVE)
        prob = jnp.exp(raw - jnp.max(raw, axis=0, keepdims=True))
        prob = prob * (1.0 / jnp.sum(prob, axis=0, keepdims=True))
        d_prob = product_right_transposed(v, d_o)
        d_raw = low(prob * (d_prob - jnp.sum(prob * d_prob, axis=0, keepdims=True)))
        parts.append(
            (
                product_left_transposed(d_raw, k) * HD ** (-0.5),
                product_plain(d_raw, q) * HD ** (-0.5),
                product_plain(low(prob), d_o),
            )
        )
    for n, ref in enumerate((d_query, d_key, d_value)):
        ref[...] = low(jnp.concatenate([part[n] for part in parts], axis=1))


def attend_back(lengths, slots, query, key, value, d_out):
    rows, count = slots.shape
    seq = key[0].shape[0] // rows
    steps = head_steps(count)
    heights = (count, seq, seq)
    return launch(
        attend_back_kernel if steps > 1 else attend_few_back_kernel,
        (rows, steps),
        [
            (
                slots.reshape(rows, 1, count),
                pl.BlockSpec((None, 1, count), lambda r, h, *_: (r, 0, 0)),
            )
            if steps > 1
            else (slots.reshape(-1, 1), pl.BlockSpec((count, 1), lambda r, h, *_: (r, 0))),
            head_blocks(query[0], count, query[1], steps),
            head_blocks(key[0], seq, key[1], steps),
            head_blocks(value[0], seq, value[1], steps),
            head_blocks(d_out, count, 0, steps),
        ],
        [
            result(
                (rows * height, MODEL_WIDTH),
                jnp.bfloat16,
                (height, MODEL_WIDTH // steps),
                lambda r, h, *_: (r, h),
            )
            for height in heights
        ],
        scalars=(lengths,),
        flops=10 * rows * count * seq * MODEL_WIDTH,
    )


def gelu_parts(value):
    root = 0.7978845608028654
    square = value * value
    bend = jnp.tanh(root * value * (1.0 + 0.044715 * square))
    half = 0.5 * (1.0 + bend)
    slope = half + 0.5 * value * (1.0 - bend * bend) * root * (1.0 + 3 * 0.044715 * square)
    return value * half, slope


def middle_into(x2, uo, x, o, w_o, c_o, d_o, u_o):
    uo[...] = low(product_right_transposed(o[...], d_o[...]))
    x2[...] = x[...] + (
        product_plain(o[...], w_o[...]) + c_o[...] + adapter(uo[...], u_o[...])
    )


FIRST_FEED = 4 * MODEL_WIDTH // BLOCK
FEED_STEPS = HIDDEN_UNITS // BLOCK
PIECES = 8
CHUNK = BLOCK // PIECES


def chunk_place(unit):
    part, rest = unit // (CHUNK * FEED_STEPS), unit % (CHUNK * FEED_STEPS)
    return pl.ds(pl.multiple_of(rest // CHUNK * BLOCK + part * CHUNK, CHUNK), CHUNK)


def chunked(part):
    return jnp.concatenate(jnp.split(part, FEED_STEPS), axis=1)


def feed_step(j):
    return jnp.minimum(j, FEED_STEPS - 1)


def late_step(j):
    return jnp.maximum(j - FEED_STEPS, 0)


def feed_in_kernel(unit, unit_fc, *refs):
    pieces, pieces_fc, refs = taken(refs, unit, unit_fc)
    x, o, c_o, d_o, u_o, gain, shift, c_fc, d_fc, u_fc = refs[:10]
    x2, uo, m, um, act, slope, weight_o, sems_o, slots, sems, pre = refs[10:]
    first = moves(unit, pieces, weight_o, sems_o, 3, BLOCK)
    pl.when(pl.program_id(0) == 0)(lambda: begin(first))
    weight = next_strip(unit_fc, pieces_fc, slots, sems, BLOCK)

    @pl.when(pl.program_id(0) == 0)
    def _():
        finish(first)
        middle_into(x2, uo, x, o, weight_o, c_o, d_o, u_o)
        norm_into(m, x2, gain[...], shift[...])
        um[...] = low(product_right_transposed(m[...], d_fc[...]))

    pre[...] = product_plain(m[...], weight[...]) + c_fc[...] + adapter(um[...], u_fc[...])
    j = pl.program_id(0)

    def part(rows):
        first, second = gelu_parts(pre[rows, :])
        slope[rows, :] = low(second)
        first = low(first)
        for start in range(0, BLOCK, CHUNK):
            act[rows, chunk_place(j * BLOCK + start)] = first[:, start : start + CHUNK]

    over_rows(pre.shape[0], 16, part)


def feed_in(x, o, unit, unit_fc, p, layer):
    tokens = x.shape[0]
    small, up = p["small"], p["up"]
    wide = (tokens, HIDDEN_UNITS), jnp.bfloat16, (tokens, BLOCK), lambda j: (0, j)
    return launch(
        partial(feed_in_kernel, unit, unit_fc),
        (FEED_STEPS,),
        unit.operands()
        + unit_fc.operands()
        + [
            whole(x),
            whole(o),
            strip(small, BLOCK, 3, layer),
            whole(p["down_t"], layer, 1),
            strip(up, BLOCK, 3, layer),
            strip(small, BLOCK, 11, layer),
            strip(small, BLOCK, 12, layer),
            strip(small, BLOCK, lambda j: FIRST_FEED + j, layer),
            whole(p["down_t"], layer, 2),
            strip(up, BLOCK, lambda j: FIRST_FEED + j, layer),
        ],
        [
            result((tokens, MODEL_WIDTH), jnp.float32),
            result((tokens, LANES), jnp.bfloat16),
            result((tokens, MODEL_WIDTH), jnp.bfloat16),
            result((tokens, LANES), jnp.bfloat16),
            result((tokens, HIDDEN_UNITS), jnp.bfloat16),
            result(*wide),
        ],
        scratch=one_slot_for(unit)
        + slots_for(unit_fc, MODEL_WIDTH, BLOCK)
        + [pltpu.VMEM((tokens, BLOCK), jnp.float32)],
        flops=2 * tokens * MODEL_WIDTH * (MODEL_WIDTH + HIDDEN_UNITS),
    )


def feed_out_kernel(unit_fp, *refs):
    pieces_fp, refs = taken(refs, unit_fp)
    x2, act, d_fp, c_fp, u_fp, final, x3, ug, h, slots, sems = refs
    j = pl.program_id(0)
    weight = next_strip(unit_fp, pieces_fp, slots, sems, BLOCK)

    @pl.when(j == 0)
    def _():
        ug[...] = jnp.zeros_like(ug)
        x3[...] = x2[...] + c_fp[...]

    columns = pl.ds(pl.multiple_of(j * BLOCK, BLOCK), BLOCK)
    taken_act = act[:, columns]
    x3[...] += product_plain(taken_act, weight[...])
    maps = [
        d_fp[:, pl.ds(pl.multiple_of((n * FEED_STEPS + j) * CHUNK, CHUNK), CHUNK)]
        for n in range(PIECES)
    ]
    ug[...] += product_right_transposed(taken_act, jnp.concatenate(maps, axis=1))

    @pl.when(j == pl.num_programs(0) - 1)
    def _():
        x3[...] += adapter(low(ug[...]), u_fp[...])
        gains = final[...].astype(jnp.float32)
        if h.shape == x3.shape:
            norm_into(h, x3, gains[0:1], gains[1:2])


def feed_out(x2, act, unit_fp, final, p, layer, with_norm):
    tokens = x2.shape[0]
    return launch(
        partial(feed_out_kernel, unit_fp),
        (FEED_STEPS,),
        unit_fp.operands()
        + [
            whole(x2),
            whole(act),
            whole(p["feed_t"], layer),
            strip(p["small"], BLOCK, 8, layer),
            strip(p["up"], BLOCK, 8, layer),
            whole(final),
        ],
        [
            result((tokens, MODEL_WIDTH), jnp.float32),
            result((tokens, LANES), jnp.float32),
            result((tokens if with_norm else 16, MODEL_WIDTH), jnp.bfloat16),
        ],
        scratch=slots_for(unit_fp, BLOCK, MODEL_WIDTH),
        flops=2 * tokens * MODEL_WIDTH * HIDDEN_UNITS,
    )


def three_parts(value):
    first = low(value)
    rest = value - first.astype(jnp.float32)
    second = low(rest)
    return [first, second, low(rest - second.astype(jnp.float32))]


def head_kernel(h, table, out, logits, total, top, bulk):
    j = pl.program_id(0)

    @pl.when(j == 0)
    def _():
        top[...] = jnp.full_like(top, NEGATIVE)
        bulk[...] = jnp.zeros_like(bulk)
        total[...] = jnp.zeros_like(total)

    def part(rows):
        logits[...] = product_right_transposed(h[rows, :], table[...])
        before = top[rows, :]
        now = jnp.maximum(before, jnp.max(logits[...], axis=1, keepdims=True))
        fade = jnp.exp(before - now)
        top[rows, :] = now
        weight = jnp.exp(logits[...] - now)
        bulk[rows, :] = bulk[rows, :] * fade + jnp.sum(weight, axis=1, keepdims=True)
        total[rows, :] = total[rows, :] * fade + product_plain(low(weight), table[...])

    over_rows(h.shape[0], logits.shape[0], part)

    @pl.when(j == pl.num_programs(0) - 1)
    def _():
        out[:, :MODEL_WIDTH] = low(total[...])
        columns = three_parts(top[...]) + three_parts(bulk[...])
        rest = jnp.zeros((h.shape[0], 128 - len(columns)), jnp.bfloat16)
        out[:, MODEL_WIDTH:] = jnp.concatenate(columns + [rest], axis=1)


def head(h, table):
    tokens, vocab = h.shape[0], table.shape[0]
    steps = 3 if vocab % 48 == 0 else 1
    tile = vocab // steps
    chunk = 256
    (out,) = launch(
        head_kernel,
        (steps,),
        [whole(h), rows_strip(table, tile, lambda j: j)],
        [result((tokens, MODEL_WIDTH + 128), jnp.bfloat16)],
        scratch=[
            pltpu.VMEM((chunk, tile), jnp.float32),
            pltpu.VMEM((tokens, MODEL_WIDTH), jnp.float32),
            pltpu.VMEM((tokens, 1), jnp.float32),
            pltpu.VMEM((tokens, 1), jnp.float32),
        ],
        flops=4 * tokens * vocab * MODEL_WIDTH,
    )
    return out


def head_back_kernel(parts, targets, h, x3, final, mask, terms, d_x3, d_hidden):
    tails = [
        parts[n, :, MODEL_WIDTH:].astype(jnp.float32) for n in range(parts.shape[0])
    ]
    tops = [tail[:, 0:1] + tail[:, 1:2] + tail[:, 2:3] for tail in tails]
    sums = [tail[:, 3:4] + tail[:, 4:5] + tail[:, 5:6] for tail in tails]
    top = tops[0]
    for other in tops[1:]:
        top = jnp.maximum(top, other)
    whole_sum = sum(s * jnp.exp(t - top) for t, s in zip(tops, sums))
    lse = top + jnp.log(whole_sum)
    wanted = targets[...]
    logit = jnp.sum(h[...].astype(jnp.float32) * wanted, axis=1, keepdims=True)
    terms[...] = (lse - logit) * mask[...]
    gathered = -wanted
    for n, t in enumerate(tops):
        gathered = gathered + parts[n, :, :MODEL_WIDTH].astype(jnp.float32) * jnp.exp(t - lse)
    d_hidden[...] = gathered * mask[...]
    norm_back_into(d_x3, d_hidden, x3, final[...].astype(jnp.float32)[0:1])


def head_back(parts, targets, h, x3, final, mask):
    count = h.shape[0]
    return launch(
        head_back_kernel,
        (1,),
        [whole(parts), whole(targets), whole(h), whole(x3), whole(final), whole(mask)],
        [
            result((count, 1), jnp.float32),
            result((count, MODEL_WIDTH), jnp.float32),
        ],
        scratch=[pltpu.VMEM((count, MODEL_WIDTH), jnp.float32)],
    )


def output_back(d_heads, grad_uo, grad_do, d_x2, o, uo, w_o, u_o, d_o):
    d_low = low(d_x2[...])
    grad_uo[...] = ADAPTER_SCALE * product_left_transposed(uo[...], d_low)
    duo = low(ADAPTER_SCALE * product_right_transposed(d_low, u_o[...]))
    grad_do[...] = product_left_transposed(duo, o[...])
    d_heads[...] = low(
        product_right_transposed(d_low, w_o[...]) + product_plain(duo, d_o[...])
    )


def front_last_back_kernel(unit, index, *refs):
    pieces, refs = taken(refs, unit)
    d_query, d_key, d_value, a, a_sel, ua, ua_sel, up, down, d_x2, x, gain = refs[:12]
    d_x, grad_up, grad_down, rows, rows_sel, inner, inner_sel, slots, sems = refs[12:]
    j = pl.program_id(0)
    weight = next_strip(unit, pieces, slots, sems, BLOCK)

    @pl.when(j == 0)
    def _():
        rows[...] = jnp.zeros_like(rows)
        inner[...] = jnp.zeros_like(inner)

    @pl.when(j == 0)
    def _():
        gradient = d_query[...]
        grad_up[...] = ADAPTER_SCALE * product_left_transposed(ua_sel[...], gradient)
        inner_sel[...] = ADAPTER_SCALE * product_right_transposed(gradient, up[...])
        rows_sel[...] = product_right_transposed(gradient, weight[...])

    def step(ref):
        gradient = ref[...]
        grad_up[...] = ADAPTER_SCALE * product_left_transposed(ua[...], gradient)
        inner[...] += ADAPTER_SCALE * product_right_transposed(gradient, up[...])
        rows[...] += product_right_transposed(gradient, weight[...])

    pl.when(j == 1)(lambda: step(d_key))
    pl.when(j == 2)(lambda: step(d_value))

    @pl.when(j == pl.num_programs(0) - 1)
    def _():
        last, last_sel = low(inner[...]), low(inner_sel[...])
        grad_down[...] = product_left_transposed(last, a[...]) + product_left_transposed(
            last_sel, a_sel[...]
        )
        rows[...] += product_plain(last, down[...])
        rows_sel[...] += product_plain(last_sel, down[...])
        add_rows(index, rows_sel, rows)
        norm_back_into(d_x, rows, x, gain[...])
        add_rows(index, d_x2, d_x)


def front_last_back(index, d_query, d_key, d_value, saved, d_x2, x, unit, p, layer):
    a, a_sel, ua, ua_sel = saved
    tokens, count = x.shape[0], index.shape[0]
    return launch(
        partial(front_last_back_kernel, unit),
        (3,),
        unit.operands()
        + [
            whole(d_query),
            whole(d_key),
            whole(d_value),
            whole(a),
            whole(a_sel),
            whole(ua),
            whole(ua_sel),
            strip(p["up"], BLOCK, lambda j: j, layer),
            whole(p["down_t"], layer, 0),
            whole(d_x2),
            whole(x),
            strip(p["small"], BLOCK, 9, layer),
        ],
        [
            result((tokens, MODEL_WIDTH), jnp.float32),
            result((LANES, 3 * MODEL_WIDTH), jnp.float32, (LANES, BLOCK), lambda j, *_: (0, j)),
            result((LANES, MODEL_WIDTH), jnp.float32),
        ],
        scratch=[
            pltpu.VMEM((tokens, MODEL_WIDTH), jnp.float32),
            pltpu.VMEM((count, MODEL_WIDTH), jnp.float32),
            pltpu.VMEM((tokens, LANES), jnp.float32),
            pltpu.VMEM((count, LANES), jnp.float32),
        ]
        + slots_for(unit, MODEL_WIDTH, BLOCK),
        scalars=(index,),
        flops=4 * tokens * MODEL_WIDTH**2,
    )


def feed_back_kernel(unit, unit_fc, unit_fp, *refs):
    pieces, pieces_fc, pieces_fp, refs = taken(refs, unit, unit_fc, unit_fp)
    d_x3, x2, m, um, ug, uo, o, act, slope, d_fp, u_fc, u_fp, d_fc, gain, u_o, d_o = refs[:16]
    d_x2, d_heads, grad_ufp, grad_dfp, grad_ufc, grad_dfc, grad_uo, grad_do = refs[16:24]
    d_out, dug, d_pre, inner, d_feed, weight_o, sems_o, slots, sems = refs[24:]
    j = pl.program_id(0)
    last = pl.num_programs(0) - 1
    out_moves = moves(unit, pieces, weight_o, sems_o, 3, BLOCK)

    def each(step, act):
        slot = lax.rem(step, 2)
        for some, refs, first in ((unit_fp, pieces_fp, 0), (unit_fc, pieces_fc, FEED_STEPS)):

            @pl.when((step >= first) & (step < first + FEED_STEPS))
            def _(some=some, refs=refs, first=first):
                column = jnp.clip(step - first, 0, FEED_STEPS - 1)
                act(moves(some, refs, slots.at[slot], sems.at[slot], column, BLOCK))

    pl.when(j == 0)(lambda: each(j, begin))
    pl.when(j < last)(lambda: each(j + 1, begin))
    pl.when(j == last)(lambda: begin(out_moves))

    @pl.when(j == 0)
    def _():
        d_out[...] = low(d_x3[...])
        dug[...] = low(ADAPTER_SCALE * product_right_transposed(d_out[...], u_fp[...]))
        grad_ufp[...] = ADAPTER_SCALE * product_left_transposed(low(ug[...]), d_out[...])
        inner[...] = jnp.zeros_like(inner)
        d_feed[...] = jnp.zeros_like(d_feed)

    each(j, finish)
    weight = slots.at[lax.rem(j, 2)]

    @pl.when(j < FEED_STEPS)
    def _():
        d_act = product_right_transposed(d_out[...], weight[...])
        from_act = product_left_transposed(dug[...], act[...])
        for n in range(PIECES):
            place = pl.ds(pl.multiple_of((n * FEED_STEPS + j) * CHUNK, CHUNK), CHUNK)
            part = slice(n * CHUNK, (n + 1) * CHUNK)
            value = d_act[:, part] + product_plain(dug[...], d_fp[:, place])
            d_pre[:, place] = low(value * slope[:, place].astype(jnp.float32))
            grad_dfp[:, place] = from_act[:, part]

    @pl.when(j >= FEED_STEPS)
    def _():
        columns = pl.ds(pl.multiple_of((j - FEED_STEPS) * BLOCK, BLOCK), BLOCK)
        gradient = d_pre[:, columns]
        grad_ufc[...] = ADAPTER_SCALE * product_left_transposed(um[...], gradient)
        inner[...] += ADAPTER_SCALE * product_right_transposed(gradient, u_fc[...])
        d_feed[...] += product_right_transposed(gradient, weight[...])

    @pl.when(j == last)
    def _():
        dum = low(inner[...])
        grad_dfc[...] = product_left_transposed(dum, m[...])
        d_feed[...] += product_plain(dum, d_fc[...])
        norm_back_into(d_x2, d_feed, x2, gain[...], d_x3)
        finish(out_moves)
        output_back(d_heads, grad_uo, grad_do, d_x2, o, uo, weight_o, u_o, d_o)


def feed_back(d_x3, saved, unit, unit_fc, unit_fp, p, layer):
    x2, m, um, ug, uo, o, act, slope = saved
    tokens = x2.shape[0]
    square = (LANES, MODEL_WIDTH), jnp.float32
    return launch(
        partial(feed_back_kernel, unit, unit_fc, unit_fp),
        (2 * FEED_STEPS,),
        unit.operands()
        + unit_fc.operands()
        + unit_fp.operands()
        + [
            whole(d_x3),
            whole(x2),
            whole(m),
            whole(um),
            whole(ug),
            whole(uo),
            whole(o),
            strip(act, BLOCK, feed_step),
            whole(slope),
            whole(p["feed_t"], layer),
            strip(p["up"], BLOCK, lambda j: FIRST_FEED + late_step(j), layer),
            strip(p["up"], BLOCK, 8, layer),
            whole(p["down_t"], layer, 2),
            strip(p["small"], BLOCK, 11, layer),
            strip(p["up"], BLOCK, 3, layer),
            whole(p["down_t"], layer, 1),
        ],
        [
            result((tokens, MODEL_WIDTH), jnp.float32),
            result((tokens, MODEL_WIDTH), jnp.bfloat16),
            result(*square),
            result((LANES, HIDDEN_UNITS), jnp.float32),
            result(
                (LANES, HIDDEN_UNITS), jnp.float32, (LANES, BLOCK), lambda j: (0, late_step(j))
            ),
            result(*square),
            result(*square),
            result(*square),
        ],
        scratch=[
            pltpu.VMEM((tokens, MODEL_WIDTH), jnp.bfloat16),
            pltpu.VMEM((tokens, LANES), jnp.bfloat16),
            pltpu.VMEM((tokens, HIDDEN_UNITS), jnp.bfloat16),
            pltpu.VMEM((tokens, LANES), jnp.float32),
            pltpu.VMEM((tokens, MODEL_WIDTH), jnp.float32),
        ]
        + one_slot_for(unit)
        + slots_for(unit_fc, MODEL_WIDTH, BLOCK),
        flops=2 * tokens * MODEL_WIDTH * (MODEL_WIDTH + 2 * HIDDEN_UNITS),
    )


def front_back_kernel(d_query, d_key, d_value, a, ua, up, grad_up, grad_down):
    inner = 0.0
    for n, ref in enumerate((d_query, d_key, d_value)):
        columns = slice(n * MODEL_WIDTH, (n + 1) * MODEL_WIDTH)
        grad_up[:, columns] = ADAPTER_SCALE * product_left_transposed(ua[...], ref[...])
        inner = inner + ADAPTER_SCALE * product_right_transposed(ref[...], up[:, columns])
    grad_down[...] = product_left_transposed(low(inner), a[...])


def front_back(d_query, d_key, d_value, a, ua, p, layer):
    return launch(
        front_back_kernel,
        (1,),
        [
            whole(d_query),
            whole(d_key),
            whole(d_value),
            whole(a),
            whole(ua),
            strip(p["up"], 3 * MODEL_WIDTH, 0, layer),
        ],
        [
            result((LANES, 3 * MODEL_WIDTH), jnp.float32),
            result((LANES, MODEL_WIDTH), jnp.float32),
        ],
    )


def pack_kernel(columns, *refs):
    extras, parts, out = refs[0], refs[1:-1], refs[-1]
    shards, width = out.shape[0], out.shape[2] - 128
    for n in range(shards):
        out[n, :, width:] = jnp.broadcast_to(extras[...], (out.shape[1], 128))
    for part, (row, start) in zip(parts, columns):
        values = part[0:ADAPTER_RANK, :]
        size = values.shape[1]
        done = 0
        while done < size:
            block, offset = divmod(start + done, width)
            step = min(width - offset, size - done)
            out[block, row : row + ADAPTER_RANK, offset : offset + step] = values[
                :, done : done + step
            ]
            done += step


def packed(by_layer, extras):
    shards = lax.axis_size("fsdp")
    columns, parts = [], []
    for layer, row in enumerate(by_layer):
        start = 0
        for part in row:
            parts.append(part)
            columns.append((layer * ADAPTER_RANK, start))
            start += part.shape[1]
    shape = (shards, len(by_layer) * ADAPTER_RANK, start // shards + 128)
    (out,) = launch(
        partial(pack_kernel, tuple(columns)),
        (1,),
        [whole(extras)] + [whole(part) for part in parts],
        [result(shape, jnp.float32)],
    )
    return out


def asking(table, ids, needed):
    shards = lax.axis_size("fsdp")
    total = ids.shape[0]
    order = jnp.arange(total, dtype=jnp.int32)
    owner = ids // table.shape[0]
    local = ids - owner * table.shape[0]
    same = (ids[:, None] == ids[None, :]) & needed[None, :]
    first = jnp.min(jnp.where(same, order[None, :], total), axis=1)
    leads = needed & (first == order)
    rank = jnp.sum(
        (leads & (owner[:, None] == owner[None, :]) & (order[None, :] < first[:, None])).astype(
            jnp.int32
        ),
        axis=1,
    )
    rounds = (jnp.max(jnp.where(needed, rank, 0)) + CAPACITY) // CAPACITY

    spots = jnp.arange(shards * CAPACITY, dtype=jnp.int32)

    def place_of(turn):
        return jnp.where(
            needed & (rank // CAPACITY == turn), owner * CAPACITY + rank % CAPACITY, -1
        )

    def ask(turn):
        place = place_of(turn)
        asked = jnp.sum(
            jnp.where(leads[:, None] & (place[:, None] == spots[None, :]), local[:, None], 0), axis=0
        )
        return asked.reshape(shards, CAPACITY)

    def sent_for(asked):
        return table.at[asked.reshape(-1)].get(mode="promise_in_bounds")

    def exchanged(part):
        return lax.all_to_all(part, "fsdp", 0, 0, tiled=True)

    def found(turn, back):
        pick = (place_of(turn)[:, None] == spots[None, :]).astype(jnp.bfloat16)
        return product_plain(pick, back)

    def later(first, most):
        def more(so_far):
            return lax.fori_loop(
                1,
                most,
                lambda turn, total: total
                + found(turn, exchanged(sent_for(exchanged(ask(turn))))),
                so_far,
            )

        return lax.cond(most > 1, more, lambda so_far: so_far, first)

    return ask, rounds, exchanged, sent_for, found, later


def as_low(numbers):
    return low(numbers // 256), low(numbers % 256)


def as_numbers(high, rest):
    return high.astype(jnp.int32) * 256 + rest.astype(jnp.int32)


def swap(part, bit):
    return lax.ppermute(part, "fsdp", [(i, i ^ bit) for i in range(lax.axis_size("fsdp"))])


def tie(parts, before):
    parts, _ = lax.optimization_barrier((parts, before))
    return parts


def hop(part):
    return lax.ppermute(
        part, "fsdp", [(i, i ^ (4 if i % 2 else 2)) for i in range(lax.axis_size("fsdp"))]
    )


class Gathering:
    PLACES = (0, 0), (1, 1), (2, 4), (3, 5), (5, 3), (4, 2), (7, 7), (6, 6)

    def __init__(self, shard, in_chunks=False):
        self.shard, self.in_chunks = shard, in_chunks
        self.direct = lax.axis_size("fsdp") == PIECES

    def begin(self, before=()):
        if self.direct:
            own = chunked(self.shard) if self.in_chunks else self.shard
            own = tie(own, before)
            other = swap(own, 1)
            self.arrays = own, other, hop(own), hop(other)

    def pass_on(self, value):
        if self.direct:
            own, other, first, second = self.arrays
            first, value = lax.optimization_barrier((first, value))
            handed = swap(first, 1)
            self.arrays = own, other, first, second, handed, swap(second, 1), hop(handed)
        return value

    def settle(self, value):
        if not self.direct:
            parts = jnp.split(lax.all_gather(self.shard, "fsdp", axis=0, tiled=True), PIECES)
            parts = [chunked(part) for part in parts] if self.in_chunks else parts
            return value, Unit(tuple(range(PIECES)), tuple(parts), parts[0].shape[0])
        far, value = lax.optimization_barrier((self.arrays[-1], value))
        arrays = self.arrays[:-1] + (far, swap(far, 1))
        return value, Unit(self.PLACES, arrays, arrays[0].shape[0])


def everywhere(part):
    shards = lax.axis_size("fsdp")
    return lax.all_to_all(
        jnp.tile(part, (shards,) + (1,) * (part.ndim - 1)), "fsdp", 0, 0, tiled=True
    )


def owned_parts(parts):
    shards = lax.axis_size("fsdp")
    rows = parts.shape[0] // shards
    return lax.all_to_all(parts, "fsdp", 0, 0, tiled=True).reshape(
        (shards, rows) + parts.shape[1:]
    )


def summed_everywhere(blocks):
    shards, rows, columns = blocks.shape
    groups = lax.axis_size("dp")
    width = columns - 128
    block = jnp.sum(owned_parts(blocks.reshape(shards * rows, columns)), axis=0)
    others = [
        lax.ppermute(block, "dp", [(i, (i + k) % groups) for i in range(groups)])
        for k in range(1, groups)
    ]
    stacked = jnp.stack([block] + others)
    order = (lax.axis_index("dp") - jnp.arange(groups)) % groups
    ranks = (order[None, :] == jnp.arange(groups)[:, None])[:, :, None, None]
    total = jnp.sum(jnp.sum(jnp.where(ranks, stacked[None], 0.0), axis=1), axis=0)
    gathered = everywhere(total).reshape(shards, rows, columns)
    return (
        gathered[:, :, :width].transpose(1, 0, 2).reshape(rows, shards * width),
        gathered[0, 0, width : width + 2],
    )


def body(
    input_token_ids,
    lengths,
    scored_slots,
    scored_targets,
    wte,
    wpe,
    frozen_attention,
    frozen_feed_input,
    frozen_feed_output,
    frozen_bias_gain,
    final_norm_params,
    adapter_down,
    adapter_down_feed,
    adapter_up,
    first_moment_down,
    first_moment_feed,
    first_moment_up,
    second_moment_down,
    second_moment_feed,
    second_moment_up,
    optimizer_step,
):
    micro, seqs, seq = input_token_ids.shape
    rows = micro * seqs
    picks = scored_slots.shape[2]
    layers = frozen_attention.shape[0]
    shards = lax.axis_size("fsdp")
    row_lengths = lengths.reshape(rows)
    slots = scored_slots.reshape(rows, picks)
    valid = slots < row_lengths[:, None]
    mask = valid.reshape(-1, 1).astype(jnp.float32)
    all_slots = jnp.tile(jnp.arange(seq, dtype=jnp.int32)[None], (rows, 1))

    useful = jnp.max(jnp.where(valid, slots, -1), axis=1)
    needed = jnp.concatenate([(all_slots <= useful[:, None]).reshape(-1), valid.reshape(-1)])
    ids = jnp.concatenate([input_token_ids.reshape(-1), scored_targets.reshape(-1)])
    attention_one, attention_two = Gathering(frozen_attention[0]), Gathering(frozen_attention[1])
    feed_in_one, feed_in_two = Gathering(frozen_feed_input[0]), Gathering(frozen_feed_input[1])
    feed_out_one = Gathering(frozen_feed_output[0], in_chunks=True)
    feed_out_two = Gathering(frozen_feed_output[1], in_chunks=True)
    attention_one.begin()
    ask, rounds, exchanged, sent_for, found, later = asking(wte, ids, needed)
    count = CAPACITY
    requests = as_low(jnp.concatenate([ask(0), jnp.full((shards, 1), rounds, jnp.int32)], 1))
    biases = jnp.tile(frozen_bias_gain.reshape(1, -1), (shards, 1))
    got = exchanged(jnp.concatenate([*requests, biases], 1))
    got = attention_one.pass_on(got)
    feed_in_one.begin(got)
    numbers = as_numbers(got[:, : count + 1], got[:, count + 1 : 2 * count + 2])
    small = (
        got[:, 2 * count + 2 :].reshape(shards, layers, -1).transpose(1, 0, 2).reshape(layers, 1, -1)
    )
    sent = sent_for(numbers[:, :count])
    most = jnp.max(numbers[:, count])
    extra = LANES - ADAPTER_RANK
    down_t = adapter_down.reshape(layers, MODEL_WIDTH, 3, ADAPTER_RANK).transpose(0, 2, 3, 1)
    p = {
        "small": small.astype(jnp.float32),
        "down_t": low(jnp.pad(down_t, ((0, 0), (0, 0), (0, extra), (0, 0)))),
        "feed_t": low(jnp.pad(adapter_down_feed.transpose(0, 2, 1), ((0, 0), (0, extra), (0, 0)))),
        "up": low(jnp.pad(adapter_up, ((0, 0), (0, extra), (0, 0)))),
    }
    back, p = lax.optimization_barrier((exchanged(sent), p))
    back, attention_one = attention_one.settle(back)
    back = feed_in_one.pass_on(back)
    feed_out_one.begin(back)
    looked_up = later(found(0, back), most)
    x0 = looked_up[: rows * seq] + jnp.tile(wpe.astype(jnp.float32), (rows, 1))
    targets = looked_up[rows * seq :]
    index = (slots + seq * jnp.arange(rows, dtype=jnp.int32)[:, None]).reshape(-1)

    qkv, a_one, ua_one = front(x0, attention_one, p, 0)
    qkv, feed_in_one = feed_in_one.settle(qkv)
    split_qkv = (qkv, 0), (qkv, 1), (qkv, 2)
    o_one = attend(row_lengths, all_slots, *split_qkv)
    o_one = feed_out_one.pass_on(o_one)
    attention_two.begin(o_one)
    x2_one, uo_one, m_one, um_one, act_one, slope_one = feed_in(
        x0, o_one, attention_one, feed_in_one, p, 0
    )
    act_one, feed_out_one = feed_out_one.settle(act_one)
    act_one = attention_two.pass_on(act_one)
    feed_in_two.begin(act_one)
    x1, ug_one, _ = feed_out(x2_one, act_one, feed_out_one, final_norm_params, p, 0, False)

    x1, attention_two = attention_two.settle(x1)
    query, kv, a_two, a_sel, ua_two, ua_sel, x_sel = front_last(index, x1, attention_two, p, 1)
    query = feed_in_two.pass_on(query)
    feed_out_two.begin(query)
    parts_two = (query, 0), (kv, 0), (kv, 1)
    o_two = attend(row_lengths, slots, *parts_two)
    o_two, feed_in_two = feed_in_two.settle(o_two)
    x2_two, uo_two, m_two, um_two, act_two, slope_two = feed_in(
        x_sel, o_two, attention_two, feed_in_two, p, 1
    )
    act_two = feed_out_two.pass_on(act_two)
    act_two, feed_out_two = feed_out_two.settle(act_two)
    x3, ug_two, h = feed_out(x2_two, act_two, feed_out_two, final_norm_params, p, 1, True)

    weighed = owned_parts(head(everywhere(h), wte))
    terms, d_x3 = head_back(weighed, targets, h, x3, final_norm_params, mask)

    d_x2, d_heads, grad_ufp, grad_dfp, grad_ufc, grad_dfc, grad_uo, grad_do = feed_back(
        d_x3,
        (x2_two, m_two, um_two, ug_two, uo_two, o_two, act_two, slope_two),
        attention_two,
        feed_in_two,
        feed_out_two,
        p,
        1,
    )
    d_parts = attend_back(row_lengths, slots, *parts_two, d_heads)
    d_x1, grad_uqkv, grad_dqkv = front_last_back(
        index, *d_parts, (a_two, a_sel, ua_two, ua_sel), d_x2, x1, attention_two, p, 1
    )
    grads_two = [
        grad_dqkv, grad_do, grad_dfc, grad_dfp, grad_uqkv, grad_uo, grad_ufc, grad_ufp
    ]

    _, d_heads, grad_ufp, grad_dfp, grad_ufc, grad_dfc, grad_uo, grad_do = feed_back(
        d_x1,
        (x2_one, m_one, um_one, ug_one, uo_one, o_one, act_one, slope_one),
        attention_one,
        feed_in_one,
        feed_out_one,
        p,
        0,
    )
    d_parts = attend_back(row_lengths, all_slots, *split_qkv, d_heads)
    grad_uqkv, grad_dqkv = front_back(*d_parts, a_one, ua_one, p, 0)
    grads_one = [
        grad_dqkv, grad_do, grad_dfc, grad_dfp, grad_uqkv, grad_uo, grad_ufc, grad_ufp
    ]

    tail = jnp.pad(jnp.stack([jnp.sum(terms), jnp.sum(mask)])[None], ((0, 0), (0, 126)))
    gradients, totals = summed_everywhere(packed((grads_one, grads_two), tail))
    loss_total, count = totals[0], totals[1]
    gradients = gradients / count
    norm = jnp.sqrt(jnp.sum(gradients * gradients))
    by_layer = gradients.reshape(layers, ADAPTER_RANK, -1)
    gradient_tree = [
        by_layer[:, :, : 3 * MODEL_WIDTH]
        .reshape(layers, ADAPTER_RANK, 3, MODEL_WIDTH)
        .transpose(0, 3, 2, 1)
        .reshape(layers, MODEL_WIDTH, 3 * ADAPTER_RANK),
        by_layer[:, :, 3 * MODEL_WIDTH : 3 * MODEL_WIDTH + HIDDEN_UNITS].transpose(0, 2, 1),
        by_layer[:, :, 3 * MODEL_WIDTH + HIDDEN_UNITS :],
    ]
    scale_factor = jnp.minimum(1.0, CLIP / (norm + 1e-06))
    step_number = optimizer_step[0].astype(jnp.float32)
    updated = [
        moment_update(weight, first, second, gradient_value, scale_factor, step_number)
        for weight, first, second, gradient_value in zip(
            (adapter_down, adapter_down_feed, adapter_up),
            (first_moment_down, first_moment_feed, first_moment_up),
            (second_moment_down, second_moment_feed, second_moment_up),
            gradient_tree,
        )
    ]
    return (
        loss_total / count,
        norm,
        *(part[0] for part in updated),
        *(part[1] for part in updated),
        *(part[2] for part in updated),
        terms.reshape(micro, seqs, picks),
    )


def solution(mesh):
    in_specs = (
        P(None, ("dp", "fsdp"), None),
        P(None, ("dp", "fsdp")),
        P(None, ("dp", "fsdp"), None),
        P(None, ("dp", "fsdp"), None),
        P("fsdp", None),
        P(),
        P(None, "fsdp", None),
        P(None, "fsdp", None),
        P(None, "fsdp", None),
        P(None, "fsdp"),
        P(),
        P(),
        P(),
        P(),
        P(),
        P(),
        P(),
        P(),
        P(),
        P(),
        P(),
    )
    out_specs = (
        P(),
        P(),
        P(),
        P(),
        P(),
        P(),
        P(),
        P(),
        P(),
        P(),
        P(),
        P(None, ("dp", "fsdp"), None),
    )
    return jax.shard_map(body, mesh=mesh, in_specs=in_specs, out_specs=out_specs, check_vma=False)
```

```python
import math
from functools import partial
from typing import NamedTuple

import jax
import jax.numpy as jnp
from jax import lax
from jax.experimental import pallas as pl
from jax.experimental.pallas import tpu as pltpu
from jax.sharding import PartitionSpec as P

MODEL_WIDTH = 1024
H = 16
HD = 64
HIDDEN_UNITS = 4096
ADAPTER_RANK = 4


ADAPTER_SCALE = 8.0
EPS_NORM = 1e-05
BETA_ONE = 0.9
BETA_TWO = 0.999
RATE = 0.02
DECAY = 0.01
EPS_ADAM = 1e-08
CLIP = 0.02
NEGATIVE = -1e30


def product_plain(left, right):
    return jnp.dot(left, right, preferred_element_type=jnp.float32)


def product_left_transposed(left, right):
    return lax.dot_general(
        left, right, (((0,), (0,)), ((), ())), preferred_element_type=jnp.float32
    )


def product_right_transposed(left, right):
    return lax.dot_general(
        left, right, (((1,), (1,)), ((), ())), preferred_element_type=jnp.float32
    )


def norm_fwd(hidden_rows, norm_gain, norm_shift):
    row_mean = jnp.mean(hidden_rows, axis=-1, keepdims=True)
    centered = hidden_rows - row_mean
    inverse_deviation = lax.rsqrt(jnp.mean(centered * centered, axis=-1, keepdims=True) + EPS_NORM)
    normalized_rows = centered * inverse_deviation
    return (normalized_rows * norm_gain + norm_shift, normalized_rows, inverse_deviation)


def norm_backward(gradient_value, normalized_rows, inverse_deviation, norm_gain):
    scaled_rows = gradient_value * norm_gain
    return inverse_deviation * (
        scaled_rows
        - jnp.mean(scaled_rows, axis=-1, keepdims=True)
        - normalized_rows * jnp.mean(scaled_rows * normalized_rows, axis=-1, keepdims=True)
    )


def moment_update(weight, first, second, gradient_value, scale_factor, step_number):
    clipped = gradient_value * scale_factor
    first_new = BETA_ONE * first + (1.0 - BETA_ONE) * clipped
    second_new = BETA_TWO * second + (1.0 - BETA_TWO) * clipped * clipped
    first_hat = first_new / (1.0 - BETA_ONE**step_number)
    second_hat = second_new / (1.0 - BETA_TWO**step_number)
    weight_new = weight - RATE * (first_hat / (jnp.sqrt(second_hat) + EPS_ADAM) + DECAY * weight)
    return (weight_new, first_new, second_new)


CAPACITY = 80


LANES = 16
HALF_TILE = 512
BLOCK = 1024
VMEM_BYTES = 63 * 2**20


def whole(array, *lead):
    shape = (None,) * len(lead) + array.shape[len(lead) :]
    place = lead + (0,) * (array.ndim - len(lead))
    return array, pl.BlockSpec(shape, lambda *_: place, pipeline_mode=pl.Buffered(1))


def some_rows(array, count, row=0):
    shape = (count, array.shape[1])
    return array, pl.BlockSpec(shape, lambda *_: (row, 0), pipeline_mode=pl.Buffered(1))


def strip(array, width, column, *lead):
    shape = (None,) * len(lead) + (array.shape[-2], width)
    if callable(column):
        return array, pl.BlockSpec(shape, lambda j, *_: lead + (0, column(j)))
    place = lead + (0, column)
    return array, pl.BlockSpec(shape, lambda *_: place, pipeline_mode=pl.Buffered(1))


def rows_strip(array, height, row, *lead):
    shape = (None,) * len(lead) + (height, array.shape[-1])
    return array, pl.BlockSpec(shape, lambda j, *_: lead + (row(j), 0))


def result(shape, dtype, block=None, place=None):
    kind = jax.ShapeDtypeStruct(shape, dtype)
    if block is None:
        block, zeros = shape, (0,) * len(shape)
        return kind, pl.BlockSpec(block, lambda *_: zeros)
    return kind, pl.BlockSpec(block, place)


def launch(kernel, grid, operands, results, scratch=(), scalars=(), flops=0):
    moved = sum(a.size * a.dtype.itemsize for a, _ in operands)
    return pl.pallas_call(
        kernel,
        out_shape=[kind for kind, _ in results],
        grid_spec=pltpu.PrefetchScalarGridSpec(
            num_scalar_prefetch=len(scalars),
            grid=grid,
            in_specs=[spec for _, spec in operands],
            out_specs=[spec for _, spec in results],
            scratch_shapes=list(scratch),
        ),
        compiler_params=pltpu.CompilerParams(vmem_limit_bytes=VMEM_BYTES),
        cost_estimate=pl.CostEstimate(flops=flops, bytes_accessed=moved, transcendentals=0),
    )(*scalars, *(a for a, _ in operands))


class Unit(NamedTuple):
    places: tuple
    arrays: tuple
    rows: int

    def operands(self):
        return [(array, pl.BlockSpec(memory_space=pltpu.HBM)) for array in self.arrays]


def shard_of(place):
    if isinstance(place, int):
        return place
    me = lax.axis_index("fsdp")
    return jnp.bitwise_xor(me, jnp.where(lax.rem(me, 2) == 0, *place))


def moves(unit, refs, target, sems, column, width):
    columns = pl.ds(pl.multiple_of(column * width, width), width)
    copies = []
    for n, (place, ref) in enumerate(zip(unit.places, refs)):
        start = pl.multiple_of(shard_of(place) * unit.rows, 16)
        copies.append(
            pltpu.make_async_copy(
                ref.at[:, columns], target.at[pl.ds(start, ref.shape[0]), :], sems.at[n]
            )
        )
    return copies


def begin(copies):
    for copy in copies:
        copy.start()


def finish(copies):
    for copy in copies:
        copy.wait()


def next_strip(unit, refs, slots, sems, width):
    j = pl.program_id(0)

    def strip_moves(step):
        slot = lax.rem(step, 2)
        return moves(unit, refs, slots.at[slot], sems.at[slot], step, width)

    pl.when(j == 0)(lambda: begin(strip_moves(j)))
    pl.when(j + 1 < pl.num_programs(0))(lambda: begin(strip_moves(j + 1)))
    finish(strip_moves(j))
    return slots.at[lax.rem(j, 2)]


def slots_for(unit, height, width):
    return [
        pltpu.VMEM((2, height, width), jnp.bfloat16),
        pltpu.SemaphoreType.DMA((2, len(unit.arrays))),
    ]


def one_slot_for(unit):
    return [
        pltpu.VMEM((MODEL_WIDTH, BLOCK), jnp.bfloat16),
        pltpu.SemaphoreType.DMA((len(unit.arrays),)),
    ]


def taken(refs, *units):
    groups = []
    for unit in units:
        groups.append(refs[: len(unit.arrays)])
        refs = refs[len(unit.arrays) :]
    return groups + [refs]


def over_rows(total, size, work):
    def turn(i, carry):
        work(pl.ds(pl.multiple_of(i * size, size), size))
        return carry

    lax.fori_loop(0, total // size, turn, 0)


def low(value):
    return value.astype(jnp.bfloat16)


def adapter(inner, up):
    return ADAPTER_SCALE * product_plain(inner, up)


def norm_into(out_ref, rows_ref, gain, shift):
    def part(rows):
        out_ref[rows, :] = low(norm_fwd(rows_ref[rows, :], gain, shift)[0])

    over_rows(rows_ref.shape[0], min(64, rows_ref.shape[0]), part)


def norm_back_into(out_ref, gradient_ref, rows_ref, gain, residual_ref=None):
    def part(rows):
        _, normalized, deviation = norm_fwd(rows_ref[rows, :], gain, 0.0)
        value = norm_backward(gradient_ref[rows, :], normalized, deviation, gain)
        if residual_ref is not None:
            value = value + residual_ref[rows, :]
        out_ref[rows, :] = value

    over_rows(rows_ref.shape[0], min(64, rows_ref.shape[0]), part)


def front_kernel(unit, *refs):
    pieces, refs = taken(refs, unit)
    x, gain, shift, bias, down, up, qkv, a, ua, slots, sems = refs
    weight = next_strip(unit, pieces, slots, sems, BLOCK)

    @pl.when(pl.program_id(0) == 0)
    def _():
        norm_into(a, x, gain[...], shift[...])
        ua[...] = low(product_right_transposed(a[...], down[...]))

    qkv[...] = low(product_plain(a[...], weight[...]) + bias[...] + adapter(ua[...], up[...]))


def front(x, tokens, unit, p, layer):
    return launch(
        partial(front_kernel, unit),
        (3,),
        unit.operands()
        + [
            some_rows(x, tokens),
            strip(p["small"], BLOCK, 9, layer),
            strip(p["small"], BLOCK, 10, layer),
            strip(p["small"], BLOCK, lambda j: j, layer),
            whole(p["down_t"], layer, 0),
            strip(p["up"], BLOCK, lambda j: j, layer),
        ],
        [
            result((tokens, 3 * MODEL_WIDTH), jnp.bfloat16, (tokens, BLOCK), lambda j: (0, j)),
            result((tokens, MODEL_WIDTH), jnp.bfloat16),
            result((tokens, LANES), jnp.bfloat16),
        ],
        scratch=slots_for(unit, MODEL_WIDTH, BLOCK),
        flops=6 * tokens * MODEL_WIDTH**2,
    )


def pick_rows(index, source, target):
    def turn(i, carry):
        target[pl.ds(i, 1), :] = source[pl.ds(index[i], 1), :]
        return carry

    lax.fori_loop(0, target.shape[0], turn, 0)


def add_rows(index, source, target):
    def turn(i, carry):
        rows = pl.ds(index[i], 1)
        target[rows, :] = target[rows, :] + source[pl.ds(i, 1), :]
        return carry

    lax.fori_loop(0, source.shape[0], turn, 0)


def front_last_kernel(unit, index, *refs):
    pieces, refs = taken(refs, unit)
    x, gain, shift, bias, down, up, q, kv, a, a_sel, ua, ua_sel, x_sel, slots, sems = refs
    j = pl.program_id(0)
    weight = next_strip(unit, pieces, slots, sems, BLOCK)

    @pl.when(j == 0)
    def _():
        norm_into(a, x, gain[...], shift[...])
        ua[...] = low(product_right_transposed(a[...], down[...]))
        pick_rows(index, x, x_sel)
        norm_into(a_sel, x_sel, gain[...], shift[...])
        ua_sel[...] = low(product_right_transposed(a_sel[...], down[...]))

    @pl.when(j == 0)
    def _():
        q[...] = low(
            product_plain(a_sel[...], weight[...]) + bias[...] + adapter(ua_sel[...], up[...])
        )

    @pl.when(j > 0)
    def _():
        kv[...] = low(product_plain(a[...], weight[...]) + bias[...] + adapter(ua[...], up[...]))


def front_last(index, x, unit, p, layer):
    tokens, count = x.shape[0], index.shape[0]
    return launch(
        partial(front_last_kernel, unit),
        (3,),
        unit.operands()
        + [
            whole(x),
            strip(p["small"], BLOCK, 9, layer),
            strip(p["small"], BLOCK, 10, layer),
            strip(p["small"], BLOCK, lambda j: j, layer),
            whole(p["down_t"], layer, 0),
            strip(p["up"], BLOCK, lambda j: j, layer),
        ],
        [
            result((count, MODEL_WIDTH), jnp.bfloat16),
            result(
                (tokens, 2 * MODEL_WIDTH),
                jnp.bfloat16,
                (tokens, BLOCK),
                lambda j, *_: (0, jnp.maximum(j - 1, 0)),
            ),
            result((tokens, MODEL_WIDTH), jnp.bfloat16),
            result((count, MODEL_WIDTH), jnp.bfloat16),
            result((tokens, LANES), jnp.bfloat16),
            result((count, LANES), jnp.bfloat16),
            result((count, MODEL_WIDTH), jnp.float32),
        ],
        scratch=slots_for(unit, MODEL_WIDTH, BLOCK),
        scalars=(index,),
        flops=4 * tokens * MODEL_WIDTH**2,
    )


def attend_kernel(lengths, slots, query, key, value, out):
    length = lengths[pl.program_id(0)]
    kpos = lax.broadcasted_iota(jnp.int32, (query.shape[0], key.shape[0]), 1)
    allowed = (kpos <= slots[...]) & (kpos < length)
    heads = []
    for start in range(0, query.shape[1], HD):
        part = slice(start, start + HD)
        raw = product_right_transposed(query[:, part], key[:, part]) * HD ** (-0.5)
        raw = jnp.where(allowed, raw, NEGATIVE)
        prob = jnp.exp(raw - jnp.max(raw, axis=1, keepdims=True))
        prob = prob * (1.0 / jnp.sum(prob, axis=1, keepdims=True))
        heads.append(product_plain(low(prob), value[:, part]))
    out[...] = low(jnp.concatenate(heads, axis=1))


def own_lanes(count, heads):
    shape = (heads * count, heads * HD)
    row = lax.broadcasted_iota(jnp.int32, shape, 0) // count
    lane = lax.broadcasted_iota(jnp.int32, shape, 1) // HD
    return row == lane


def stacked_heads(rows, own):
    heads = own.shape[0] // rows.shape[0]
    tall = jnp.concatenate([rows.astype(jnp.float32)] * heads, axis=0)
    return low(jnp.where(own, tall, 0.0))


def own_heads(tall, own, count):
    tall = jnp.where(own, tall, 0.0)
    total = tall[:count]
    for start in range(count, tall.shape[0], count):
        total = total + tall[start : start + count]
    return total


def few_scores(length, slots, tall, key):
    raw = product_right_transposed(tall, key[...]) * HD ** (-0.5)
    kpos = lax.broadcasted_iota(jnp.int32, raw.shape, 1)
    places = jnp.concatenate([slots[...]] * (raw.shape[0] // slots.shape[0]), axis=0)
    raw = jnp.where((kpos <= places) & (kpos < length), raw, NEGATIVE)
    prob = jnp.exp(raw - jnp.max(raw, axis=1, keepdims=True))
    return prob * (1.0 / jnp.sum(prob, axis=1, keepdims=True))


def attend_few_kernel(lengths, slots, query, key, value, out):
    count = query.shape[0]
    own = own_lanes(count, query.shape[1] // HD)
    prob = few_scores(lengths[pl.program_id(0)], slots, stacked_heads(query[...], own), key)
    out[...] = low(own_heads(product_plain(low(prob), value[...]), own, count))


def attend_few_back_kernel(lengths, slots, query, key, value, d_out, d_query, d_key, d_value):
    count = query.shape[0]
    own = own_lanes(count, query.shape[1] // HD)
    tall = stacked_heads(query[...], own)
    d_tall = stacked_heads(d_out[...], own)
    prob = few_scores(lengths[pl.program_id(0)], slots, tall, key)
    d_prob = product_right_transposed(d_tall, value[...])
    d_raw = low(prob * (d_prob - jnp.sum(prob * d_prob, axis=1, keepdims=True)))
    d_value[...] = low(product_left_transposed(low(prob), d_tall))
    d_key[...] = low(product_left_transposed(d_raw, tall) * HD ** (-0.5))
    d_query[...] = low(own_heads(product_plain(d_raw, key[...]), own, count) * HD ** (-0.5))


def head_blocks(array, height, third, steps):
    offset = third * steps
    return array, pl.BlockSpec((height, MODEL_WIDTH // steps), lambda r, h, *_: (r, offset + h))


def head_steps(count):
    return 2 if count > 128 else 1


def attend(lengths, slots, query, key, value):
    rows, count = slots.shape
    seq = key[0].shape[0] // rows
    steps = head_steps(count)
    column = slots.reshape(-1, 1)
    (out,) = launch(
        attend_kernel if steps > 1 else attend_few_kernel,
        (rows, steps),
        [
            (column, pl.BlockSpec((count, 1), lambda r, h, *_: (r, 0))),
            head_blocks(query[0], count, query[1], steps),
            head_blocks(key[0], seq, key[1], steps),
            head_blocks(value[0], seq, value[1], steps),
        ],
        [
            result(
                (rows * count, MODEL_WIDTH),
                jnp.bfloat16,
                (count, MODEL_WIDTH // steps),
                lambda r, h, *_: (r, h),
            )
        ],
        scalars=(lengths,),
        flops=4 * rows * count * seq * MODEL_WIDTH,
    )
    return out


def attend_back_kernel(lengths, slots, query, key, value, d_out, d_query, d_key, d_value):
    length = lengths[pl.program_id(0)]
    kpos = lax.broadcasted_iota(jnp.int32, (key.shape[0], query.shape[0]), 0)
    allowed = (kpos <= slots[...]) & (kpos < length)
    parts = []
    for start in range(0, query.shape[1], HD):
        part = slice(start, start + HD)
        q, k, v, d_o = query[:, part], key[:, part], value[:, part], d_out[:, part]
        raw = product_right_transposed(k, q) * HD ** (-0.5)
        raw = jnp.where(allowed, raw, NEGATIVE)
        prob = jnp.exp(raw - jnp.max(raw, axis=0, keepdims=True))
        prob = prob * (1.0 / jnp.sum(prob, axis=0, keepdims=True))
        d_prob = product_right_transposed(v, d_o)
        d_raw = low(prob * (d_prob - jnp.sum(prob * d_prob, axis=0, keepdims=True)))
        parts.append(
            (
                product_left_transposed(d_raw, k) * HD ** (-0.5),
                product_plain(d_raw, q) * HD ** (-0.5),
                product_plain(low(prob), d_o),
            )
        )
    for n, ref in enumerate((d_query, d_key, d_value)):
        ref[...] = low(jnp.concatenate([part[n] for part in parts], axis=1))


def attend_back(lengths, slots, query, key, value, d_out):
    rows, count = slots.shape
    seq = key[0].shape[0] // rows
    steps = head_steps(count)
    heights = (count, seq, seq)
    return launch(
        attend_back_kernel if steps > 1 else attend_few_back_kernel,
        (rows, steps),
        [
            (
                slots.reshape(rows, 1, count),
                pl.BlockSpec((None, 1, count), lambda r, h, *_: (r, 0, 0)),
            )
            if steps > 1
            else (slots.reshape(-1, 1), pl.BlockSpec((count, 1), lambda r, h, *_: (r, 0))),
            head_blocks(query[0], count, query[1], steps),
            head_blocks(key[0], seq, key[1], steps),
            head_blocks(value[0], seq, value[1], steps),
            head_blocks(d_out, count, 0, steps),
        ],
        [
            result(
                (rows * height, MODEL_WIDTH),
                jnp.bfloat16,
                (height, MODEL_WIDTH // steps),
                lambda r, h, *_: (r, h),
            )
            for height in heights
        ],
        scalars=(lengths,),
        flops=10 * rows * count * seq * MODEL_WIDTH,
    )


def gelu_parts(value):
    root = 0.7978845608028654
    square = value * value
    bend = jnp.tanh(root * value * (1.0 + 0.044715 * square))
    half = 0.5 * (1.0 + bend)
    slope = half + 0.5 * value * (1.0 - bend * bend) * root * (1.0 + 3 * 0.044715 * square)
    return value * half, slope


def middle_into(x2, uo, x, o, w_o, c_o, d_o, u_o):
    uo[...] = low(product_right_transposed(o[...], d_o[...]))
    x2[...] = x[...] + (
        product_plain(o[...], w_o[...]) + c_o[...] + adapter(uo[...], u_o[...])
    )


FIRST_FEED = 4 * MODEL_WIDTH // BLOCK
FEED_STEPS = HIDDEN_UNITS // BLOCK
PIECES = 8
CHUNK = BLOCK // PIECES


def chunk_place(unit):
    part, rest = unit // (CHUNK * FEED_STEPS), unit % (CHUNK * FEED_STEPS)
    return pl.ds(pl.multiple_of(rest // CHUNK * BLOCK + part * CHUNK, CHUNK), CHUNK)


def chunked(part):
    return jnp.concatenate(jnp.split(part, FEED_STEPS), axis=1)


def feed_step(j):
    return jnp.minimum(j, FEED_STEPS - 1)


def late_step(j):
    return jnp.maximum(j - FEED_STEPS, 0)


def feed_in_kernel(unit, unit_fc, *refs):
    pieces, pieces_fc, refs = taken(refs, unit, unit_fc)
    x, o, c_o, d_o, u_o, gain, shift, c_fc, d_fc, u_fc = refs[:10]
    x2, uo, m, um, act, slope, weight_o, sems_o, slots, sems, pre = refs[10:]
    first = moves(unit, pieces, weight_o, sems_o, 3, BLOCK)
    pl.when(pl.program_id(0) == 0)(lambda: begin(first))
    weight = next_strip(unit_fc, pieces_fc, slots, sems, BLOCK)

    @pl.when(pl.program_id(0) == 0)
    def _():
        finish(first)
        middle_into(x2, uo, x, o, weight_o, c_o, d_o, u_o)
        norm_into(m, x2, gain[...], shift[...])
        um[...] = low(product_right_transposed(m[...], d_fc[...]))

    pre[...] = product_plain(m[...], weight[...]) + c_fc[...] + adapter(um[...], u_fc[...])
    j = pl.program_id(0)

    def part(rows):
        first, second = gelu_parts(pre[rows, :])
        slope[rows, :] = low(second)
        first = low(first)
        for start in range(0, BLOCK, CHUNK):
            act[rows, chunk_place(j * BLOCK + start)] = first[:, start : start + CHUNK]

    over_rows(pre.shape[0], 16, part)


def feed_in(x, o, unit, unit_fc, p, layer):
    tokens = o.shape[0]
    small, up = p["small"], p["up"]
    wide = (tokens, HIDDEN_UNITS), jnp.bfloat16, (tokens, BLOCK), lambda j: (0, j)
    return launch(
        partial(feed_in_kernel, unit, unit_fc),
        (FEED_STEPS,),
        unit.operands()
        + unit_fc.operands()
        + [
            some_rows(x, tokens),
            whole(o),
            strip(small, BLOCK, 3, layer),
            whole(p["down_t"], layer, 1),
            strip(up, BLOCK, 3, layer),
            strip(small, BLOCK, 11, layer),
            strip(small, BLOCK, 12, layer),
            strip(small, BLOCK, lambda j: FIRST_FEED + j, layer),
            whole(p["down_t"], layer, 2),
            strip(up, BLOCK, lambda j: FIRST_FEED + j, layer),
        ],
        [
            result((tokens, MODEL_WIDTH), jnp.float32),
            result((tokens, LANES), jnp.bfloat16),
            result((tokens, MODEL_WIDTH), jnp.bfloat16),
            result((tokens, LANES), jnp.bfloat16),
            result((tokens, HIDDEN_UNITS), jnp.bfloat16),
            result(*wide),
        ],
        scratch=one_slot_for(unit)
        + slots_for(unit_fc, MODEL_WIDTH, BLOCK)
        + [pltpu.VMEM((tokens, BLOCK), jnp.float32)],
        flops=2 * tokens * MODEL_WIDTH * (MODEL_WIDTH + HIDDEN_UNITS),
    )


def feed_out_kernel(unit_fp, *refs):
    pieces_fp, refs = taken(refs, unit_fp)
    x2, act, d_fp, c_fp, u_fp, final, x3, ug, h, slots, sems = refs
    j = pl.program_id(0)
    weight = next_strip(unit_fp, pieces_fp, slots, sems, BLOCK)

    @pl.when(j == 0)
    def _():
        ug[...] = jnp.zeros_like(ug)
        x3[...] = x2[...] + c_fp[...]

    columns = pl.ds(pl.multiple_of(j * BLOCK, BLOCK), BLOCK)
    taken_act = act[:, columns]
    x3[...] += product_plain(taken_act, weight[...])
    maps = [
        d_fp[:, pl.ds(pl.multiple_of((n * FEED_STEPS + j) * CHUNK, CHUNK), CHUNK)]
        for n in range(PIECES)
    ]
    ug[...] += product_right_transposed(taken_act, jnp.concatenate(maps, axis=1))

    @pl.when(j == pl.num_programs(0) - 1)
    def _():
        x3[...] += adapter(low(ug[...]), u_fp[...])
        gains = final[...].astype(jnp.float32)
        if h.shape == x3.shape:
            norm_into(h, x3, gains[0:1], gains[1:2])


def feed_out(x2, act, unit_fp, final, p, layer, with_norm):
    tokens = x2.shape[0]
    return launch(
        partial(feed_out_kernel, unit_fp),
        (FEED_STEPS,),
        unit_fp.operands()
        + [
            whole(x2),
            whole(act),
            whole(p["feed_t"], layer),
            strip(p["small"], BLOCK, 8, layer),
            strip(p["up"], BLOCK, 8, layer),
            whole(final),
        ],
        [
            result((tokens, MODEL_WIDTH), jnp.float32),
            result((tokens, LANES), jnp.float32),
            result((tokens if with_norm else 16, MODEL_WIDTH), jnp.bfloat16),
        ],
        scratch=slots_for(unit_fp, BLOCK, MODEL_WIDTH),
        flops=2 * tokens * MODEL_WIDTH * HIDDEN_UNITS,
    )


def three_parts(value):
    first = low(value)
    rest = value - first.astype(jnp.float32)
    second = low(rest)
    return [first, second, low(rest - second.astype(jnp.float32))]


def head_kernel(h, table, out, logits, total, top, bulk):
    j = pl.program_id(0)

    @pl.when(j == 0)
    def _():
        top[...] = jnp.full_like(top, NEGATIVE)
        bulk[...] = jnp.zeros_like(bulk)
        total[...] = jnp.zeros_like(total)

    def part(rows):
        logits[...] = product_right_transposed(h[rows, :], table[...])
        before = top[rows, :]
        now = jnp.maximum(before, jnp.max(logits[...], axis=1, keepdims=True))
        fade = jnp.exp(before - now)
        top[rows, :] = now
        weight = jnp.exp(logits[...] - now)
        bulk[rows, :] = bulk[rows, :] * fade + jnp.sum(weight, axis=1, keepdims=True)
        total[rows, :] = total[rows, :] * fade + product_plain(low(weight), table[...])

    over_rows(h.shape[0], logits.shape[0], part)

    @pl.when(j == pl.num_programs(0) - 1)
    def _():
        out[:, :MODEL_WIDTH] = low(total[...])
        columns = three_parts(top[...]) + three_parts(bulk[...])
        rest = jnp.zeros((h.shape[0], 128 - len(columns)), jnp.bfloat16)
        out[:, MODEL_WIDTH:] = jnp.concatenate(columns + [rest], axis=1)


def head(h, table):
    tokens, vocab = h.shape[0], table.shape[0]
    steps = 3 if vocab % 48 == 0 else 1
    tile = vocab // steps
    chunk = 256
    (out,) = launch(
        head_kernel,
        (steps,),
        [whole(h), rows_strip(table, tile, lambda j: j)],
        [result((tokens, MODEL_WIDTH + 128), jnp.bfloat16)],
        scratch=[
            pltpu.VMEM((chunk, tile), jnp.float32),
            pltpu.VMEM((tokens, MODEL_WIDTH), jnp.float32),
            pltpu.VMEM((tokens, 1), jnp.float32),
            pltpu.VMEM((tokens, 1), jnp.float32),
        ],
        flops=4 * tokens * vocab * MODEL_WIDTH,
    )
    return out


def head_back_kernel(parts, targets, h, x3, final, mask, terms, d_x3, d_hidden):
    tails = [
        parts[n, :, MODEL_WIDTH:].astype(jnp.float32) for n in range(parts.shape[0])
    ]
    tops = [tail[:, 0:1] + tail[:, 1:2] + tail[:, 2:3] for tail in tails]
    sums = [tail[:, 3:4] + tail[:, 4:5] + tail[:, 5:6] for tail in tails]
    top = tops[0]
    for other in tops[1:]:
        top = jnp.maximum(top, other)
    whole_sum = sum(s * jnp.exp(t - top) for t, s in zip(tops, sums))
    lse = top + jnp.log(whole_sum)
    wanted = targets[...]
    logit = jnp.sum(h[...].astype(jnp.float32) * wanted, axis=1, keepdims=True)
    terms[...] = (lse - logit) * mask[...]
    gathered = -wanted
    for n, t in enumerate(tops):
        gathered = gathered + parts[n, :, :MODEL_WIDTH].astype(jnp.float32) * jnp.exp(t - lse)
    d_hidden[...] = gathered * mask[...]
    norm_back_into(d_x3, d_hidden, x3, final[...].astype(jnp.float32)[0:1])


def head_back(parts, targets, h, x3, final, mask):
    count = h.shape[0]
    return launch(
        head_back_kernel,
        (1,),
        [whole(parts), some_rows(targets, count, targets.shape[0] // count - 1), whole(h), whole(x3), whole(final), whole(mask)],
        [
            result((count, 1), jnp.float32),
            result((count, MODEL_WIDTH), jnp.float32),
        ],
        scratch=[pltpu.VMEM((count, MODEL_WIDTH), jnp.float32)],
    )


def output_back(d_heads, grad_uo, grad_do, d_x2, o, uo, w_o, u_o, d_o):
    d_low = low(d_x2[...])
    grad_uo[...] = ADAPTER_SCALE * product_left_transposed(uo[...], d_low)
    duo = low(ADAPTER_SCALE * product_right_transposed(d_low, u_o[...]))
    grad_do[...] = product_left_transposed(duo, o[...])
    d_heads[...] = low(
        product_right_transposed(d_low, w_o[...]) + product_plain(duo, d_o[...])
    )


def front_last_back_kernel(unit, index, *refs):
    pieces, refs = taken(refs, unit)
    d_query, d_key, d_value, a, a_sel, ua, ua_sel, up, down, d_x2, x, gain = refs[:12]
    d_x, grad_up, grad_down, rows, rows_sel, inner, inner_sel, slots, sems = refs[12:]
    j = pl.program_id(0)
    weight = next_strip(unit, pieces, slots, sems, BLOCK)

    @pl.when(j == 0)
    def _():
        rows[...] = jnp.zeros_like(rows)
        inner[...] = jnp.zeros_like(inner)

    @pl.when(j == 0)
    def _():
        gradient = d_query[...]
        grad_up[...] = ADAPTER_SCALE * product_left_transposed(ua_sel[...], gradient)
        inner_sel[...] = ADAPTER_SCALE * product_right_transposed(gradient, up[...])
        rows_sel[...] = product_right_transposed(gradient, weight[...])

    def step(ref):
        gradient = ref[...]
        grad_up[...] = ADAPTER_SCALE * product_left_transposed(ua[...], gradient)
        inner[...] += ADAPTER_SCALE * product_right_transposed(gradient, up[...])
        rows[...] += product_right_transposed(gradient, weight[...])

    pl.when(j == 1)(lambda: step(d_key))
    pl.when(j == 2)(lambda: step(d_value))

    @pl.when(j == pl.num_programs(0) - 1)
    def _():
        last, last_sel = low(inner[...]), low(inner_sel[...])
        grad_down[...] = product_left_transposed(last, a[...]) + product_left_transposed(
            last_sel, a_sel[...]
        )
        rows[...] += product_plain(last, down[...])
        rows_sel[...] += product_plain(last_sel, down[...])
        add_rows(index, rows_sel, rows)
        norm_back_into(d_x, rows, x, gain[...])
        add_rows(index, d_x2, d_x)


def front_last_back(index, d_query, d_key, d_value, saved, d_x2, x, unit, p, layer):
    a, a_sel, ua, ua_sel = saved
    tokens, count = x.shape[0], index.shape[0]
    return launch(
        partial(front_last_back_kernel, unit),
        (3,),
        unit.operands()
        + [
            whole(d_query),
            whole(d_key),
            whole(d_value),
            whole(a),
            whole(a_sel),
            whole(ua),
            whole(ua_sel),
            strip(p["up"], BLOCK, lambda j: j, layer),
            whole(p["down_t"], layer, 0),
            whole(d_x2),
            whole(x),
            strip(p["small"], BLOCK, 9, layer),
        ],
        [
            result((tokens, MODEL_WIDTH), jnp.float32),
            result((LANES, 3 * MODEL_WIDTH), jnp.float32, (LANES, BLOCK), lambda j, *_: (0, j)),
            result((LANES, MODEL_WIDTH), jnp.float32),
        ],
        scratch=[
            pltpu.VMEM((tokens, MODEL_WIDTH), jnp.float32),
            pltpu.VMEM((count, MODEL_WIDTH), jnp.float32),
            pltpu.VMEM((tokens, LANES), jnp.float32),
            pltpu.VMEM((count, LANES), jnp.float32),
        ]
        + slots_for(unit, MODEL_WIDTH, BLOCK),
        scalars=(index,),
        flops=4 * tokens * MODEL_WIDTH**2,
    )


def feed_back_kernel(unit, unit_fc, unit_fp, *refs):
    pieces, pieces_fc, pieces_fp, refs = taken(refs, unit, unit_fc, unit_fp)
    d_x3, x2, m, um, ug, uo, o, act, slope, d_fp, u_fc, u_fp, d_fc, gain, u_o, d_o = refs[:16]
    d_x2, d_heads, grad_ufp, grad_dfp, grad_ufc, grad_dfc, grad_uo, grad_do = refs[16:24]
    d_out, dug, d_pre, inner, d_feed, weight_o, sems_o, slots, sems = refs[24:]
    j = pl.program_id(0)
    last = pl.num_programs(0) - 1
    out_moves = moves(unit, pieces, weight_o, sems_o, 3, BLOCK)

    def each(step, act):
        slot = lax.rem(step, 2)
        for some, refs, first in ((unit_fp, pieces_fp, 0), (unit_fc, pieces_fc, FEED_STEPS)):

            @pl.when((step >= first) & (step < first + FEED_STEPS))
            def _(some=some, refs=refs, first=first):
                column = jnp.clip(step - first, 0, FEED_STEPS - 1)
                act(moves(some, refs, slots.at[slot], sems.at[slot], column, BLOCK))

    pl.when(j == 0)(lambda: each(j, begin))
    pl.when(j < last)(lambda: each(j + 1, begin))
    pl.when(j == last)(lambda: begin(out_moves))

    @pl.when(j == 0)
    def _():
        d_out[...] = low(d_x3[...])
        dug[...] = low(ADAPTER_SCALE * product_right_transposed(d_out[...], u_fp[...]))
        grad_ufp[...] = ADAPTER_SCALE * product_left_transposed(low(ug[...]), d_out[...])
        inner[...] = jnp.zeros_like(inner)
        d_feed[...] = jnp.zeros_like(d_feed)

    each(j, finish)
    weight = slots.at[lax.rem(j, 2)]

    @pl.when(j < FEED_STEPS)
    def _():
        d_act = product_right_transposed(d_out[...], weight[...])
        from_act = product_left_transposed(dug[...], act[...])
        for n in range(PIECES):
            place = pl.ds(pl.multiple_of((n * FEED_STEPS + j) * CHUNK, CHUNK), CHUNK)
            part = slice(n * CHUNK, (n + 1) * CHUNK)
            value = d_act[:, part] + product_plain(dug[...], d_fp[:, place])
            d_pre[:, place] = low(value * slope[:, place].astype(jnp.float32))
            grad_dfp[:, place] = from_act[:, part]

    @pl.when(j >= FEED_STEPS)
    def _():
        columns = pl.ds(pl.multiple_of((j - FEED_STEPS) * BLOCK, BLOCK), BLOCK)
        gradient = d_pre[:, columns]
        grad_ufc[...] = ADAPTER_SCALE * product_left_transposed(um[...], gradient)
        inner[...] += ADAPTER_SCALE * product_right_transposed(gradient, u_fc[...])
        d_feed[...] += product_right_transposed(gradient, weight[...])

    @pl.when(j == last)
    def _():
        dum = low(inner[...])
        grad_dfc[...] = product_left_transposed(dum, m[...])
        d_feed[...] += product_plain(dum, d_fc[...])
        norm_back_into(d_x2, d_feed, x2, gain[...], d_x3)
        finish(out_moves)
        output_back(d_heads, grad_uo, grad_do, d_x2, o, uo, weight_o, u_o, d_o)


def feed_back(d_x3, saved, unit, unit_fc, unit_fp, p, layer):
    x2, m, um, ug, uo, o, act, slope = saved
    tokens = x2.shape[0]
    square = (LANES, MODEL_WIDTH), jnp.float32
    return launch(
        partial(feed_back_kernel, unit, unit_fc, unit_fp),
        (2 * FEED_STEPS,),
        unit.operands()
        + unit_fc.operands()
        + unit_fp.operands()
        + [
            whole(d_x3),
            whole(x2),
            whole(m),
            whole(um),
            whole(ug),
            whole(uo),
            whole(o),
            strip(act, BLOCK, feed_step),
            whole(slope),
            whole(p["feed_t"], layer),
            strip(p["up"], BLOCK, lambda j: FIRST_FEED + late_step(j), layer),
            strip(p["up"], BLOCK, 8, layer),
            whole(p["down_t"], layer, 2),
            strip(p["small"], BLOCK, 11, layer),
            strip(p["up"], BLOCK, 3, layer),
            whole(p["down_t"], layer, 1),
        ],
        [
            result((tokens, MODEL_WIDTH), jnp.float32),
            result((tokens, MODEL_WIDTH), jnp.bfloat16),
            result(*square),
            result((LANES, HIDDEN_UNITS), jnp.float32),
            result(
                (LANES, HIDDEN_UNITS), jnp.float32, (LANES, BLOCK), lambda j: (0, late_step(j))
            ),
            result(*square),
            result(*square),
            result(*square),
        ],
        scratch=[
            pltpu.VMEM((tokens, MODEL_WIDTH), jnp.bfloat16),
            pltpu.VMEM((tokens, LANES), jnp.bfloat16),
            pltpu.VMEM((tokens, HIDDEN_UNITS), jnp.bfloat16),
            pltpu.VMEM((tokens, LANES), jnp.float32),
            pltpu.VMEM((tokens, MODEL_WIDTH), jnp.float32),
        ]
        + one_slot_for(unit)
        + slots_for(unit_fc, MODEL_WIDTH, BLOCK),
        flops=2 * tokens * MODEL_WIDTH * (MODEL_WIDTH + 2 * HIDDEN_UNITS),
    )


def front_back_kernel(d_query, d_key, d_value, a, ua, up, grad_up, grad_down):
    inner = 0.0
    for n, ref in enumerate((d_query, d_key, d_value)):
        columns = slice(n * MODEL_WIDTH, (n + 1) * MODEL_WIDTH)
        grad_up[:, columns] = ADAPTER_SCALE * product_left_transposed(ua[...], ref[...])
        inner = inner + ADAPTER_SCALE * product_right_transposed(ref[...], up[:, columns])
    grad_down[...] = product_left_transposed(low(inner), a[...])


def front_back(d_query, d_key, d_value, a, ua, p, layer):
    return launch(
        front_back_kernel,
        (1,),
        [
            whole(d_query),
            whole(d_key),
            whole(d_value),
            whole(a),
            whole(ua),
            strip(p["up"], 3 * MODEL_WIDTH, 0, layer),
        ],
        [
            result((LANES, 3 * MODEL_WIDTH), jnp.float32),
            result((LANES, MODEL_WIDTH), jnp.float32),
        ],
    )


def pack_kernel(columns, *refs):
    extras, parts, out = refs[0], refs[1:-1], refs[-1]
    shards, width = out.shape[0], out.shape[2] - 128
    for n in range(shards):
        out[n, :, width:] = jnp.broadcast_to(extras[...], (out.shape[1], 128))
    for part, (row, start) in zip(parts, columns):
        values = part[0:ADAPTER_RANK, :]
        size = values.shape[1]
        done = 0
        while done < size:
            block, offset = divmod(start + done, width)
            step = min(width - offset, size - done)
            out[block, row : row + ADAPTER_RANK, offset : offset + step] = values[
                :, done : done + step
            ]
            done += step


def packed(by_layer, extras):
    shards = lax.axis_size("fsdp")
    columns, parts = [], []
    for layer, row in enumerate(by_layer):
        start = 0
        for part in row:
            parts.append(part)
            columns.append((layer * ADAPTER_RANK, start))
            start += part.shape[1]
    shape = (shards, len(by_layer) * ADAPTER_RANK, start // shards + 128)
    (out,) = launch(
        partial(pack_kernel, tuple(columns)),
        (1,),
        [whole(extras)] + [whole(part) for part in parts],
        [result(shape, jnp.float32)],
    )
    return out


def asking(table, ids, needed):
    shards = lax.axis_size("fsdp")
    total = ids.shape[0]
    order = jnp.arange(total, dtype=jnp.int32)
    owner = ids // table.shape[0]
    local = ids - owner * table.shape[0]
    same = (ids[:, None] == ids[None, :]) & needed[None, :]
    first = jnp.min(jnp.where(same, order[None, :], total), axis=1)
    leads = needed & (first == order)
    rank = jnp.sum(
        (leads & (owner[:, None] == owner[None, :]) & (order[None, :] < first[:, None])).astype(
            jnp.int32
        ),
        axis=1,
    )
    rounds = (jnp.max(jnp.where(needed, rank, 0)) + CAPACITY) // CAPACITY

    spots = jnp.arange(shards * CAPACITY, dtype=jnp.int32)

    def place_of(turn):
        return jnp.where(
            needed & (rank // CAPACITY == turn), owner * CAPACITY + rank % CAPACITY, -1
        )

    def ask(turn):
        place = place_of(turn)
        asked = jnp.sum(
            jnp.where(leads[:, None] & (place[:, None] == spots[None, :]), local[:, None], 0), axis=0
        )
        return asked.reshape(shards, CAPACITY)

    def sent_for(asked):
        return table.at[asked.reshape(-1)].get(mode="promise_in_bounds")

    def exchanged(part):
        return lax.all_to_all(part, "fsdp", 0, 0, tiled=True)

    def found(turn, back):
        pick = (place_of(turn)[:, None] == spots[None, :]).astype(jnp.bfloat16)
        return product_plain(pick, back)

    def with_rounds(most, added):
        def more(so_far):
            return lax.fori_loop(
                1,
                most,
                lambda turn, total: total
                + found(turn, exchanged(sent_for(exchanged(ask(turn))))),
                so_far,
            )

        return lax.cond(most > 1, more, lambda so_far: so_far, added)

    return ask, rounds, exchanged, sent_for, found, with_rounds


def as_low(numbers):
    return low(numbers // 256), low(numbers % 256)


def as_numbers(high, rest):
    return high.astype(jnp.int32) * 256 + rest.astype(jnp.int32)


def swap(part, bit):
    return lax.ppermute(part, "fsdp", [(i, i ^ bit) for i in range(lax.axis_size("fsdp"))])


def tie(parts, before):
    parts, _ = lax.optimization_barrier((parts, before))
    return parts


def hop(part):
    return lax.ppermute(
        part, "fsdp", [(i, i ^ (4 if i % 2 else 2)) for i in range(lax.axis_size("fsdp"))]
    )


class Gathering:
    PLACES = (0, 0), (1, 1), (2, 4), (3, 5), (5, 3), (4, 2), (7, 7), (6, 6)

    def __init__(self, shard, in_chunks=False):
        self.shard, self.in_chunks = shard, in_chunks
        self.direct = lax.axis_size("fsdp") == PIECES

    def begin(self, before=()):
        if self.direct:
            own = chunked(self.shard) if self.in_chunks else self.shard
            own = tie(own, before)
            other = swap(own, 1)
            self.arrays = own, other, hop(own), hop(other)

    def after_first(self, value):
        return tie(value, self.arrays[1]) if self.direct else value

    def after_last(self, value):
        return tie(value, self.arrays[4]) if self.direct else value

    def pass_on(self, value):
        if self.direct:
            own, other, first, second = self.arrays
            first, value = lax.optimization_barrier((first, value))
            handed = swap(first, 1)
            self.arrays = own, other, first, second, handed, swap(second, 1), hop(handed)
        return value

    def settle(self, value):
        if not self.direct:
            parts = jnp.split(lax.all_gather(self.shard, "fsdp", axis=0, tiled=True), PIECES)
            parts = [chunked(part) for part in parts] if self.in_chunks else parts
            return value, Unit(tuple(range(PIECES)), tuple(parts), parts[0].shape[0])
        far, value = lax.optimization_barrier((self.arrays[-1], value))
        arrays = self.arrays[:-1] + (far, swap(far, 1))
        return value, Unit(self.PLACES, arrays, arrays[0].shape[0])


def everywhere(part):
    shards = lax.axis_size("fsdp")
    return lax.all_to_all(
        jnp.tile(part, (shards,) + (1,) * (part.ndim - 1)), "fsdp", 0, 0, tiled=True
    )


def owned_parts(parts):
    shards = lax.axis_size("fsdp")
    rows = parts.shape[0] // shards
    return lax.all_to_all(parts, "fsdp", 0, 0, tiled=True).reshape(
        (shards, rows) + parts.shape[1:]
    )


def summed_everywhere(blocks):
    shards, rows, columns = blocks.shape
    groups = lax.axis_size("dp")
    width = columns - 128
    block = jnp.sum(owned_parts(blocks.reshape(shards * rows, columns)), axis=0)
    others = [
        lax.ppermute(block, "dp", [(i, (i + k) % groups) for i in range(groups)])
        for k in range(1, groups)
    ]
    stacked = jnp.stack([block] + others)
    order = (lax.axis_index("dp") - jnp.arange(groups)) % groups
    ranks = (order[None, :] == jnp.arange(groups)[:, None])[:, :, None, None]
    total = jnp.sum(jnp.sum(jnp.where(ranks, stacked[None], 0.0), axis=1), axis=0)
    gathered = everywhere(total).reshape(shards, rows, columns)
    return (
        gathered[:, :, :width].transpose(1, 0, 2).reshape(rows, shards * width),
        gathered[0, 0, width : width + 2],
    )


def body(
    input_token_ids,
    lengths,
    scored_slots,
    scored_targets,
    wte,
    wpe,
    frozen_attention,
    frozen_feed_input,
    frozen_feed_output,
    frozen_bias_gain,
    final_norm_params,
    adapter_down,
    adapter_down_feed,
    adapter_up,
    first_moment_down,
    first_moment_feed,
    first_moment_up,
    second_moment_down,
    second_moment_feed,
    second_moment_up,
    optimizer_step,
):
    micro, seqs, seq = input_token_ids.shape
    rows = micro * seqs
    picks = scored_slots.shape[2]
    layers = frozen_attention.shape[0]
    shards = lax.axis_size("fsdp")
    row_lengths = lengths.reshape(rows)
    slots = scored_slots.reshape(rows, picks)
    valid = slots < row_lengths[:, None]
    mask = valid.reshape(-1, 1).astype(jnp.float32)
    all_slots = jnp.tile(jnp.arange(seq, dtype=jnp.int32)[None], (rows, 1))

    useful = jnp.max(jnp.where(valid, slots, -1), axis=1)
    needed = jnp.concatenate([(all_slots <= useful[:, None]).reshape(-1), valid.reshape(-1)])
    ids = jnp.concatenate([input_token_ids.reshape(-1), scored_targets.reshape(-1)])
    attention_one, attention_two = Gathering(frozen_attention[0]), Gathering(frozen_attention[1])
    feed_in_one, feed_in_two = Gathering(frozen_feed_input[0]), Gathering(frozen_feed_input[1])
    feed_out_one = Gathering(frozen_feed_output[0], in_chunks=True)
    feed_out_two = Gathering(frozen_feed_output[1], in_chunks=True)
    attention_one.begin()
    ask, rounds, exchanged, sent_for, found, with_rounds = asking(wte, ids, needed)
    count = CAPACITY
    requests = as_low(jnp.concatenate([ask(0), jnp.full((shards, 1), rounds, jnp.int32)], 1))
    biases = jnp.tile(frozen_bias_gain.reshape(1, -1), (shards, 1))
    message = jnp.concatenate([*requests, biases], 1)
    got = exchanged(attention_one.after_first(message))
    got = attention_one.pass_on(got)
    feed_in_one.begin(got)
    numbers = as_numbers(got[:, : count + 1], got[:, count + 1 : 2 * count + 2])
    small = (
        got[:, 2 * count + 2 :].reshape(shards, layers, -1).transpose(1, 0, 2).reshape(layers, 1, -1)
    )
    sent = sent_for(attention_one.after_last(numbers[:, :count]))
    most = jnp.max(numbers[:, count])
    extra = LANES - ADAPTER_RANK
    down_t = adapter_down.reshape(layers, MODEL_WIDTH, 3, ADAPTER_RANK).transpose(0, 2, 3, 1)
    p = {
        "small": small.astype(jnp.float32),
        "down_t": low(jnp.pad(down_t, ((0, 0), (0, 0), (0, extra), (0, 0)))),
        "feed_t": low(jnp.pad(adapter_down_feed.transpose(0, 2, 1), ((0, 0), (0, extra), (0, 0)))),
        "up": low(jnp.pad(adapter_up, ((0, 0), (0, extra), (0, 0)))),
    }
    places = jnp.concatenate([wpe.astype(jnp.float32)] * rows)
    places = jnp.pad(places, ((0, rows * picks), (0, 0)))
    places = with_rounds(most, places)
    back, p, places = lax.optimization_barrier((exchanged(sent), p, places))
    back, attention_one = attention_one.settle(back)
    back = feed_in_one.pass_on(back)
    feed_out_one.begin(back)
    x0 = found(0, back) + places
    index = (slots + seq * jnp.arange(rows, dtype=jnp.int32)[:, None]).reshape(-1)

    qkv, a_one, ua_one = front(x0, rows * seq, attention_one, p, 0)
    qkv = feed_out_one.pass_on(qkv)
    attention_two.begin(qkv)
    split_qkv = (qkv, 0), (qkv, 1), (qkv, 2)
    o_one = attend(row_lengths, all_slots, *split_qkv)
    o_one, feed_in_one = feed_in_one.settle(o_one)
    o_one = attention_two.pass_on(o_one)
    feed_in_two.begin(o_one)
    x2_one, uo_one, m_one, um_one, act_one, slope_one = feed_in(
        x0, o_one, attention_one, feed_in_one, p, 0
    )
    act_one, feed_out_one = feed_out_one.settle(act_one)
    act_one = feed_in_two.pass_on(act_one)
    feed_out_two.begin(act_one)
    x1, ug_one, _ = feed_out(x2_one, act_one, feed_out_one, final_norm_params, p, 0, False)
    x1, attention_two = attention_two.settle(x1)
    x1 = feed_out_two.pass_on(x1)

    query, kv, a_two, a_sel, ua_two, ua_sel, x_sel = front_last(index, x1, attention_two, p, 1)
    query, feed_in_two = feed_in_two.settle(query)
    parts_two = (query, 0), (kv, 0), (kv, 1)
    o_two = attend(row_lengths, slots, *parts_two)
    x2_two, uo_two, m_two, um_two, act_two, slope_two = feed_in(
        x_sel, o_two, attention_two, feed_in_two, p, 1
    )
    act_two, feed_out_two = feed_out_two.settle(act_two)
    x3, ug_two, h = feed_out(x2_two, act_two, feed_out_two, final_norm_params, p, 1, True)

    weighed = owned_parts(head(everywhere(h), wte))
    terms, d_x3 = head_back(weighed, x0, h, x3, final_norm_params, mask)

    d_x2, d_heads, grad_ufp, grad_dfp, grad_ufc, grad_dfc, grad_uo, grad_do = feed_back(
        d_x3,
        (x2_two, m_two, um_two, ug_two, uo_two, o_two, act_two, slope_two),
        attention_two,
        feed_in_two,
        feed_out_two,
        p,
        1,
    )
    d_parts = attend_back(row_lengths, slots, *parts_two, d_heads)
    d_x1, grad_uqkv, grad_dqkv = front_last_back(
        index, *d_parts, (a_two, a_sel, ua_two, ua_sel), d_x2, x1, attention_two, p, 1
    )
    grads_two = [
        grad_dqkv, grad_do, grad_dfc, grad_dfp, grad_uqkv, grad_uo, grad_ufc, grad_ufp
    ]

    _, d_heads, grad_ufp, grad_dfp, grad_ufc, grad_dfc, grad_uo, grad_do = feed_back(
        d_x1,
        (x2_one, m_one, um_one, ug_one, uo_one, o_one, act_one, slope_one),
        attention_one,
        feed_in_one,
        feed_out_one,
        p,
        0,
    )
    d_parts = attend_back(row_lengths, all_slots, *split_qkv, d_heads)
    grad_uqkv, grad_dqkv = front_back(*d_parts, a_one, ua_one, p, 0)
    grads_one = [
        grad_dqkv, grad_do, grad_dfc, grad_dfp, grad_uqkv, grad_uo, grad_ufc, grad_ufp
    ]

    tail = jnp.pad(jnp.stack([jnp.sum(terms), jnp.sum(mask)])[None], ((0, 0), (0, 126)))
    gradients, totals = summed_everywhere(packed((grads_one, grads_two), tail))
    loss_total, count = totals[0], totals[1]
    gradients = gradients / count
    norm = jnp.sqrt(jnp.sum(gradients * gradients))
    by_layer = gradients.reshape(layers, ADAPTER_RANK, -1)
    gradient_tree = [
        by_layer[:, :, : 3 * MODEL_WIDTH]
        .reshape(layers, ADAPTER_RANK, 3, MODEL_WIDTH)
        .transpose(0, 3, 2, 1)
        .reshape(layers, MODEL_WIDTH, 3 * ADAPTER_RANK),
        by_layer[:, :, 3 * MODEL_WIDTH : 3 * MODEL_WIDTH + HIDDEN_UNITS].transpose(0, 2, 1),
        by_layer[:, :, 3 * MODEL_WIDTH + HIDDEN_UNITS :],
    ]
    scale_factor = jnp.minimum(1.0, CLIP / (norm + 1e-06))
    step_number = optimizer_step[0].astype(jnp.float32)
    updated = [
        moment_update(weight, first, second, gradient_value, scale_factor, step_number)
        for weight, first, second, gradient_value in zip(
            (adapter_down, adapter_down_feed, adapter_up),
            (first_moment_down, first_moment_feed, first_moment_up),
            (second_moment_down, second_moment_feed, second_moment_up),
            gradient_tree,
        )
    ]
    return (
        loss_total / count,
        norm,
        *(part[0] for part in updated),
        *(part[1] for part in updated),
        *(part[2] for part in updated),
        terms.reshape(micro, seqs, picks),
    )


def solution(mesh):
    in_specs = (
        P(None, ("dp", "fsdp"), None),
        P(None, ("dp", "fsdp")),
        P(None, ("dp", "fsdp"), None),
        P(None, ("dp", "fsdp"), None),
        P("fsdp", None),
        P(),
        P(None, "fsdp", None),
        P(None, "fsdp", None),
        P(None, "fsdp", None),
        P(None, "fsdp"),
        P(),
        P(),
        P(),
        P(),
        P(),
        P(),
        P(),
        P(),
        P(),
        P(),
        P(),
    )
    out_specs = (
        P(),
        P(),
        P(),
        P(),
        P(),
        P(),
        P(),
        P(),
        P(),
        P(),
        P(),
        P(None, ("dp", "fsdp"), None),
    )
    return jax.shard_map(body, mesh=mesh, in_specs=in_specs, out_specs=out_specs, check_vma=False)
```

```python
import math
from functools import partial
from typing import NamedTuple

import jax
import jax.numpy as jnp
from jax import lax
from jax.experimental import pallas as pl
from jax.experimental.pallas import tpu as pltpu
from jax.sharding import PartitionSpec as P

MODEL_WIDTH = 1024
H = 16
HD = 64
HIDDEN_UNITS = 4096
ADAPTER_RANK = 4


ADAPTER_SCALE = 8.0
EPS_NORM = 1e-05
BETA_ONE = 0.9
BETA_TWO = 0.999
RATE = 0.02
DECAY = 0.01
EPS_ADAM = 1e-08
CLIP = 0.02
NEGATIVE = -1e30


def product_plain(left, right):
    return jnp.dot(left, right, preferred_element_type=jnp.float32)


def product_left_transposed(left, right):
    return lax.dot_general(
        left, right, (((0,), (0,)), ((), ())), preferred_element_type=jnp.float32
    )


def product_right_transposed(left, right):
    return lax.dot_general(
        left, right, (((1,), (1,)), ((), ())), preferred_element_type=jnp.float32
    )


def norm_fwd(hidden_rows, norm_gain, norm_shift):
    row_mean = jnp.mean(hidden_rows, axis=-1, keepdims=True)
    centered = hidden_rows - row_mean
    inverse_deviation = lax.rsqrt(jnp.mean(centered * centered, axis=-1, keepdims=True) + EPS_NORM)
    normalized_rows = centered * inverse_deviation
    return (normalized_rows * norm_gain + norm_shift, normalized_rows, inverse_deviation)


def norm_backward(gradient_value, normalized_rows, inverse_deviation, norm_gain):
    scaled_rows = gradient_value * norm_gain
    return inverse_deviation * (
        scaled_rows
        - jnp.mean(scaled_rows, axis=-1, keepdims=True)
        - normalized_rows * jnp.mean(scaled_rows * normalized_rows, axis=-1, keepdims=True)
    )


def moment_update(weight, first, second, gradient_value, scale_factor, step_number):
    clipped = gradient_value * scale_factor
    first_new = BETA_ONE * first + (1.0 - BETA_ONE) * clipped
    second_new = BETA_TWO * second + (1.0 - BETA_TWO) * clipped * clipped
    first_hat = first_new / (1.0 - BETA_ONE**step_number)
    second_hat = second_new / (1.0 - BETA_TWO**step_number)
    weight_new = weight - RATE * (first_hat / (jnp.sqrt(second_hat) + EPS_ADAM) + DECAY * weight)
    return (weight_new, first_new, second_new)


CAPACITY = 80


LANES = 16
HALF_TILE = 512
BLOCK = 1024
VMEM_BYTES = 63 * 2**20


def whole(array, *lead):
    shape = (None,) * len(lead) + array.shape[len(lead) :]
    place = lead + (0,) * (array.ndim - len(lead))
    return array, pl.BlockSpec(shape, lambda *_: place, pipeline_mode=pl.Buffered(1))


def some_rows(array, count, row=0):
    shape = (count, array.shape[1])
    return array, pl.BlockSpec(shape, lambda *_: (row, 0), pipeline_mode=pl.Buffered(1))


def strip(array, width, column, *lead):
    shape = (None,) * len(lead) + (array.shape[-2], width)
    if callable(column):
        return array, pl.BlockSpec(shape, lambda j, *_: lead + (0, column(j)))
    place = lead + (0, column)
    return array, pl.BlockSpec(shape, lambda *_: place, pipeline_mode=pl.Buffered(1))


def rows_strip(array, height, row, *lead):
    shape = (None,) * len(lead) + (height, array.shape[-1])
    return array, pl.BlockSpec(shape, lambda j, *_: lead + (row(j), 0))


def result(shape, dtype, block=None, place=None):
    kind = jax.ShapeDtypeStruct(shape, dtype)
    if block is None:
        block, zeros = shape, (0,) * len(shape)
        return kind, pl.BlockSpec(block, lambda *_: zeros)
    return kind, pl.BlockSpec(block, place)


def launch(kernel, grid, operands, results, scratch=(), scalars=(), flops=0):
    moved = sum(a.size * a.dtype.itemsize for a, _ in operands)
    return pl.pallas_call(
        kernel,
        out_shape=[kind for kind, _ in results],
        grid_spec=pltpu.PrefetchScalarGridSpec(
            num_scalar_prefetch=len(scalars),
            grid=grid,
            in_specs=[spec for _, spec in operands],
            out_specs=[spec for _, spec in results],
            scratch_shapes=list(scratch),
        ),
        compiler_params=pltpu.CompilerParams(vmem_limit_bytes=VMEM_BYTES),
        cost_estimate=pl.CostEstimate(flops=flops, bytes_accessed=moved, transcendentals=0),
    )(*scalars, *(a for a, _ in operands))


class Unit(NamedTuple):
    places: tuple
    arrays: tuple
    rows: int

    def operands(self):
        return [(array, pl.BlockSpec(memory_space=pltpu.HBM)) for array in self.arrays]


def shard_of(place):
    if isinstance(place, int):
        return place
    me = lax.axis_index("fsdp")
    return jnp.bitwise_xor(me, jnp.where(lax.rem(me, 2) == 0, *place))


def moves(unit, refs, target, sems, column, width):
    columns = pl.ds(pl.multiple_of(column * width, width), width)
    copies = []
    for n, (place, ref) in enumerate(zip(unit.places, refs)):
        start = pl.multiple_of(shard_of(place) * unit.rows, 16)
        copies.append(
            pltpu.make_async_copy(
                ref.at[:, columns], target.at[pl.ds(start, ref.shape[0]), :], sems.at[n]
            )
        )
    return copies


def begin(copies):
    for copy in copies:
        copy.start()


def finish(copies):
    for copy in copies:
        copy.wait()


def next_strip(unit, refs, slots, sems, width):
    j = pl.program_id(0)

    def strip_moves(step):
        slot = lax.rem(step, 2)
        return moves(unit, refs, slots.at[slot], sems.at[slot], step, width)

    pl.when(j == 0)(lambda: begin(strip_moves(j)))
    pl.when(j + 1 < pl.num_programs(0))(lambda: begin(strip_moves(j + 1)))
    finish(strip_moves(j))
    return slots.at[lax.rem(j, 2)]


def slots_for(unit, height, width):
    return [
        pltpu.VMEM((2, height, width), jnp.bfloat16),
        pltpu.SemaphoreType.DMA((2, len(unit.arrays))),
    ]


def one_slot_for(unit):
    return [
        pltpu.VMEM((MODEL_WIDTH, BLOCK), jnp.bfloat16),
        pltpu.SemaphoreType.DMA((len(unit.arrays),)),
    ]


def taken(refs, *units):
    groups = []
    for unit in units:
        groups.append(refs[: len(unit.arrays)])
        refs = refs[len(unit.arrays) :]
    return groups + [refs]


def over_rows(total, size, work):
    def turn(i, carry):
        work(pl.ds(pl.multiple_of(i * size, size), size))
        return carry

    lax.fori_loop(0, total // size, turn, 0)


def low(value):
    return value.astype(jnp.bfloat16)


def adapter(inner, up):
    return ADAPTER_SCALE * product_plain(inner, up)


def norm_into(out_ref, rows_ref, gain, shift):
    def part(rows):
        out_ref[rows, :] = low(norm_fwd(rows_ref[rows, :], gain, shift)[0])

    over_rows(rows_ref.shape[0], min(64, rows_ref.shape[0]), part)


def norm_back_into(out_ref, gradient_ref, rows_ref, gain, residual_ref=None):
    def part(rows):
        _, normalized, deviation = norm_fwd(rows_ref[rows, :], gain, 0.0)
        value = norm_backward(gradient_ref[rows, :], normalized, deviation, gain)
        if residual_ref is not None:
            value = value + residual_ref[rows, :]
        out_ref[rows, :] = value

    over_rows(rows_ref.shape[0], min(64, rows_ref.shape[0]), part)


def front_kernel(unit, *refs):
    pieces, refs = taken(refs, unit)
    x, gain, shift, bias, down, up, qkv, a, ua, slots, sems = refs
    weight = next_strip(unit, pieces, slots, sems, BLOCK)

    @pl.when(pl.program_id(0) == 0)
    def _():
        norm_into(a, x, gain[...], shift[...])
        ua[...] = low(product_right_transposed(a[...], down[...]))

    qkv[...] = low(product_plain(a[...], weight[...]) + bias[...] + adapter(ua[...], up[...]))


def front(x, tokens, unit, p, layer):
    return launch(
        partial(front_kernel, unit),
        (3,),
        unit.operands()
        + [
            some_rows(x, tokens),
            strip(p["small"], BLOCK, 9, layer),
            strip(p["small"], BLOCK, 10, layer),
            strip(p["small"], BLOCK, lambda j: j, layer),
            whole(p["down_t"], layer, 0),
            strip(p["up"], BLOCK, lambda j: j, layer),
        ],
        [
            result((tokens, 3 * MODEL_WIDTH), jnp.bfloat16, (tokens, BLOCK), lambda j: (0, j)),
            result((tokens, MODEL_WIDTH), jnp.bfloat16),
            result((tokens, LANES), jnp.bfloat16),
        ],
        scratch=slots_for(unit, MODEL_WIDTH, BLOCK),
        flops=6 * tokens * MODEL_WIDTH**2,
    )


def pick_rows(index, source, target):
    def turn(i, carry):
        target[pl.ds(i, 1), :] = source[pl.ds(index[i], 1), :]
        return carry

    lax.fori_loop(0, target.shape[0], turn, 0)


def add_rows(index, source, target):
    def turn(i, carry):
        rows = pl.ds(index[i], 1)
        target[rows, :] = target[rows, :] + source[pl.ds(i, 1), :]
        return carry

    lax.fori_loop(0, source.shape[0], turn, 0)


def front_last_kernel(unit, index, *refs):
    pieces, refs = taken(refs, unit)
    x, gain, shift, bias, down, up, q, kv, a, a_sel, ua, ua_sel, x_sel, slots, sems = refs
    j = pl.program_id(0)
    weight = next_strip(unit, pieces, slots, sems, BLOCK)

    @pl.when(j == 0)
    def _():
        norm_into(a, x, gain[...], shift[...])
        ua[...] = low(product_right_transposed(a[...], down[...]))
        pick_rows(index, x, x_sel)
        norm_into(a_sel, x_sel, gain[...], shift[...])
        ua_sel[...] = low(product_right_transposed(a_sel[...], down[...]))

    @pl.when(j == 0)
    def _():
        q[...] = low(
            product_plain(a_sel[...], weight[...]) + bias[...] + adapter(ua_sel[...], up[...])
        )

    @pl.when(j > 0)
    def _():
        kv[...] = low(product_plain(a[...], weight[...]) + bias[...] + adapter(ua[...], up[...]))


def front_last(index, x, unit, p, layer):
    tokens, count = x.shape[0], index.shape[0]
    return launch(
        partial(front_last_kernel, unit),
        (3,),
        unit.operands()
        + [
            whole(x),
            strip(p["small"], BLOCK, 9, layer),
            strip(p["small"], BLOCK, 10, layer),
            strip(p["small"], BLOCK, lambda j: j, layer),
            whole(p["down_t"], layer, 0),
            strip(p["up"], BLOCK, lambda j: j, layer),
        ],
        [
            result((count, MODEL_WIDTH), jnp.bfloat16),
            result(
                (tokens, 2 * MODEL_WIDTH),
                jnp.bfloat16,
                (tokens, BLOCK),
                lambda j, *_: (0, jnp.maximum(j - 1, 0)),
            ),
            result((tokens, MODEL_WIDTH), jnp.bfloat16),
            result((count, MODEL_WIDTH), jnp.bfloat16),
            result((tokens, LANES), jnp.bfloat16),
            result((count, LANES), jnp.bfloat16),
            result((count, MODEL_WIDTH), jnp.float32),
        ],
        scratch=slots_for(unit, MODEL_WIDTH, BLOCK),
        scalars=(index,),
        flops=4 * tokens * MODEL_WIDTH**2,
    )


def attend_kernel(lengths, slots, query, key, value, out):
    length = lengths[pl.program_id(0)]
    kpos = lax.broadcasted_iota(jnp.int32, (query.shape[0], key.shape[0]), 1)
    allowed = (kpos <= slots[...]) & (kpos < length)
    heads = []
    for start in range(0, query.shape[1], HD):
        part = slice(start, start + HD)
        raw = product_right_transposed(query[:, part], key[:, part]) * HD ** (-0.5)
        raw = jnp.where(allowed, raw, NEGATIVE)
        prob = jnp.exp(raw - jnp.max(raw, axis=1, keepdims=True))
        prob = prob * (1.0 / jnp.sum(prob, axis=1, keepdims=True))
        heads.append(product_plain(low(prob), value[:, part]))
    out[...] = low(jnp.concatenate(heads, axis=1))


def own_lanes(count, heads):
    shape = (heads * count, heads * HD)
    row = lax.broadcasted_iota(jnp.int32, shape, 0) // count
    lane = lax.broadcasted_iota(jnp.int32, shape, 1) // HD
    return row == lane


def stacked_heads(rows, own):
    heads = own.shape[0] // rows.shape[0]
    tall = jnp.concatenate([rows.astype(jnp.float32)] * heads, axis=0)
    return low(jnp.where(own, tall, 0.0))


def own_heads(tall, own, count):
    tall = jnp.where(own, tall, 0.0)
    total = tall[:count]
    for start in range(count, tall.shape[0], count):
        total = total + tall[start : start + count]
    return total


def few_scores(length, slots, tall, key):
    raw = product_right_transposed(tall, key[...]) * HD ** (-0.5)
    kpos = lax.broadcasted_iota(jnp.int32, raw.shape, 1)
    places = jnp.concatenate([slots[...]] * (raw.shape[0] // slots.shape[0]), axis=0)
    raw = jnp.where((kpos <= places) & (kpos < length), raw, NEGATIVE)
    prob = jnp.exp(raw - jnp.max(raw, axis=1, keepdims=True))
    return prob * (1.0 / jnp.sum(prob, axis=1, keepdims=True))


def attend_few_kernel(lengths, slots, query, key, value, out):
    count = query.shape[0]
    own = own_lanes(count, query.shape[1] // HD)
    prob = few_scores(lengths[pl.program_id(0)], slots, stacked_heads(query[...], own), key)
    out[...] = low(own_heads(product_plain(low(prob), value[...]), own, count))


def attend_few_back_kernel(lengths, slots, query, key, value, d_out, d_query, d_key, d_value):
    count = query.shape[0]
    own = own_lanes(count, query.shape[1] // HD)
    tall = stacked_heads(query[...], own)
    d_tall = stacked_heads(d_out[...], own)
    prob = few_scores(lengths[pl.program_id(0)], slots, tall, key)
    d_prob = product_right_transposed(d_tall, value[...])
    d_raw = low(prob * (d_prob - jnp.sum(prob * d_prob, axis=1, keepdims=True)))
    d_value[...] = low(product_left_transposed(low(prob), d_tall))
    d_key[...] = low(product_left_transposed(d_raw, tall) * HD ** (-0.5))
    d_query[...] = low(own_heads(product_plain(d_raw, key[...]), own, count) * HD ** (-0.5))


def head_blocks(array, height, third, steps):
    offset = third * steps
    return array, pl.BlockSpec((height, MODEL_WIDTH // steps), lambda r, h, *_: (r, offset + h))


def head_steps(count):
    return 2 if count > 128 else 1


def attend(lengths, slots, query, key, value):
    rows, count = slots.shape
    seq = key[0].shape[0] // rows
    steps = head_steps(count)
    column = slots.reshape(-1, 1)
    (out,) = launch(
        attend_kernel if steps > 1 else attend_few_kernel,
        (rows, steps),
        [
            (column, pl.BlockSpec((count, 1), lambda r, h, *_: (r, 0))),
            head_blocks(query[0], count, query[1], steps),
            head_blocks(key[0], seq, key[1], steps),
            head_blocks(value[0], seq, value[1], steps),
        ],
        [
            result(
                (rows * count, MODEL_WIDTH),
                jnp.bfloat16,
                (count, MODEL_WIDTH // steps),
                lambda r, h, *_: (r, h),
            )
        ],
        scalars=(lengths,),
        flops=4 * rows * count * seq * MODEL_WIDTH,
    )
    return out


def attend_back_kernel(lengths, slots, query, key, value, d_out, d_query, d_key, d_value):
    length = lengths[pl.program_id(0)]
    kpos = lax.broadcasted_iota(jnp.int32, (key.shape[0], query.shape[0]), 0)
    allowed = (kpos <= slots[...]) & (kpos < length)
    parts = []
    for start in range(0, query.shape[1], HD):
        part = slice(start, start + HD)
        q, k, v, d_o = query[:, part], key[:, part], value[:, part], d_out[:, part]
        raw = product_right_transposed(k, q) * HD ** (-0.5)
        raw = jnp.where(allowed, raw, NEGATIVE)
        prob = jnp.exp(raw - jnp.max(raw, axis=0, keepdims=True))
        prob = prob * (1.0 / jnp.sum(prob, axis=0, keepdims=True))
        d_prob = product_right_transposed(v, d_o)
        d_raw = low(prob * (d_prob - jnp.sum(prob * d_prob, axis=0, keepdims=True)))
        parts.append(
            (
                product_left_transposed(d_raw, k) * HD ** (-0.5),
                product_plain(d_raw, q) * HD ** (-0.5),
                product_plain(low(prob), d_o),
            )
        )
    for n, ref in enumerate((d_query, d_key, d_value)):
        ref[...] = low(jnp.concatenate([part[n] for part in parts], axis=1))


def attend_back(lengths, slots, query, key, value, d_out):
    rows, count = slots.shape
    seq = key[0].shape[0] // rows
    steps = head_steps(count)
    heights = (count, seq, seq)
    return launch(
        attend_back_kernel if steps > 1 else attend_few_back_kernel,
        (rows, steps),
        [
            (
                slots.reshape(rows, 1, count),
                pl.BlockSpec((None, 1, count), lambda r, h, *_: (r, 0, 0)),
            )
            if steps > 1
            else (slots.reshape(-1, 1), pl.BlockSpec((count, 1), lambda r, h, *_: (r, 0))),
            head_blocks(query[0], count, query[1], steps),
            head_blocks(key[0], seq, key[1], steps),
            head_blocks(value[0], seq, value[1], steps),
            head_blocks(d_out, count, 0, steps),
        ],
        [
            result(
                (rows * height, MODEL_WIDTH),
                jnp.bfloat16,
                (height, MODEL_WIDTH // steps),
                lambda r, h, *_: (r, h),
            )
            for height in heights
        ],
        scalars=(lengths,),
        flops=10 * rows * count * seq * MODEL_WIDTH,
    )


def gelu_parts(value):
    root, bend = 0.7978845608028654, 0.044715
    square = value * value
    turned = jnp.tanh(value * (root + root * bend * square))
    half = 0.5 + 0.5 * turned
    steep = (1.0 - turned * turned) * (0.5 * root + 1.5 * root * bend * square)
    return value * half, half + value * steep


def middle_into(x2, uo, x, o, w_o, c_o, d_o, u_o):
    uo[...] = low(product_right_transposed(o[...], d_o[...]))
    x2[...] = x[...] + (
        product_plain(o[...], w_o[...]) + c_o[...] + adapter(uo[...], u_o[...])
    )


FIRST_FEED = 4 * MODEL_WIDTH // BLOCK
FEED_STEPS = HIDDEN_UNITS // BLOCK
PIECES = 8
CHUNK = BLOCK // PIECES


def chunk_place(unit):
    part, rest = unit // (CHUNK * FEED_STEPS), unit % (CHUNK * FEED_STEPS)
    return pl.ds(pl.multiple_of(rest // CHUNK * BLOCK + part * CHUNK, CHUNK), CHUNK)


def chunked(part):
    return jnp.concatenate(jnp.split(part, FEED_STEPS), axis=1)


def feed_step(j):
    return jnp.minimum(j, FEED_STEPS - 1)


def late_step(j):
    return jnp.maximum(j - FEED_STEPS, 0)


def feed_in_kernel(unit, unit_fc, *refs):
    pieces, pieces_fc, refs = taken(refs, unit, unit_fc)
    x, o, c_o, d_o, u_o, gain, shift, c_fc, d_fc, u_fc = refs[:10]
    x2, uo, m, um, act, slope, weight_o, sems_o, slots, sems, pre, plain = refs[10:]
    first = moves(unit, pieces, weight_o, sems_o, 3, BLOCK)
    pl.when(pl.program_id(0) == 0)(lambda: begin(first))
    weight = next_strip(unit_fc, pieces_fc, slots, sems, BLOCK)

    @pl.when(pl.program_id(0) == 0)
    def _():
        finish(first)
        middle_into(x2, uo, x, o, weight_o, c_o, d_o, u_o)
        norm_into(m, x2, gain[...], shift[...])
        um[...] = low(product_right_transposed(m[...], d_fc[...]))

    pre[...] = product_plain(m[...], weight[...]) + c_fc[...] + adapter(um[...], u_fc[...])
    j = pl.program_id(0)

    def part(rows):
        first, second = gelu_parts(pre[rows, :])
        slope[rows, :] = low(second)
        plain[rows, :] = low(first)

    over_rows(pre.shape[0], 64, part)
    for start in range(0, BLOCK, CHUNK):
        act[:, chunk_place(j * BLOCK + start)] = plain[:, start : start + CHUNK]


def feed_in(x, o, unit, unit_fc, p, layer):
    tokens = o.shape[0]
    small, up = p["small"], p["up"]
    wide = (tokens, HIDDEN_UNITS), jnp.bfloat16, (tokens, BLOCK), lambda j: (0, j)
    return launch(
        partial(feed_in_kernel, unit, unit_fc),
        (FEED_STEPS,),
        unit.operands()
        + unit_fc.operands()
        + [
            some_rows(x, tokens),
            whole(o),
            strip(small, BLOCK, 3, layer),
            whole(p["down_t"], layer, 1),
            strip(up, BLOCK, 3, layer),
            strip(small, BLOCK, 11, layer),
            strip(small, BLOCK, 12, layer),
            strip(small, BLOCK, lambda j: FIRST_FEED + j, layer),
            whole(p["down_t"], layer, 2),
            strip(up, BLOCK, lambda j: FIRST_FEED + j, layer),
        ],
        [
            result((tokens, MODEL_WIDTH), jnp.float32),
            result((tokens, LANES), jnp.bfloat16),
            result((tokens, MODEL_WIDTH), jnp.bfloat16),
            result((tokens, LANES), jnp.bfloat16),
            result((tokens, HIDDEN_UNITS), jnp.bfloat16),
            result(*wide),
        ],
        scratch=one_slot_for(unit)
        + slots_for(unit_fc, MODEL_WIDTH, BLOCK)
        + [pltpu.VMEM((tokens, BLOCK), jnp.float32), pltpu.VMEM((tokens, BLOCK), jnp.bfloat16)],
        flops=2 * tokens * MODEL_WIDTH * (MODEL_WIDTH + HIDDEN_UNITS),
    )


def feed_out_kernel(unit_fp, *refs):
    pieces_fp, refs = taken(refs, unit_fp)
    x2, act, d_fp, c_fp, u_fp, final, x3, ug, h, slots, sems = refs
    j = pl.program_id(0)
    weight = next_strip(unit_fp, pieces_fp, slots, sems, BLOCK)

    @pl.when(j == 0)
    def _():
        ug[...] = jnp.zeros_like(ug)
        x3[...] = x2[...] + c_fp[...]

    columns = pl.ds(pl.multiple_of(j * BLOCK, BLOCK), BLOCK)
    taken_act = act[:, columns]
    x3[...] += product_plain(taken_act, weight[...])
    maps = [
        d_fp[:, pl.ds(pl.multiple_of((n * FEED_STEPS + j) * CHUNK, CHUNK), CHUNK)]
        for n in range(PIECES)
    ]
    ug[...] += product_right_transposed(taken_act, jnp.concatenate(maps, axis=1))

    @pl.when(j == pl.num_programs(0) - 1)
    def _():
        x3[...] += adapter(low(ug[...]), u_fp[...])
        gains = final[...].astype(jnp.float32)
        if h.shape == x3.shape:
            norm_into(h, x3, gains[0:1], gains[1:2])


def feed_out(x2, act, unit_fp, final, p, layer, with_norm):
    tokens = x2.shape[0]
    return launch(
        partial(feed_out_kernel, unit_fp),
        (FEED_STEPS,),
        unit_fp.operands()
        + [
            whole(x2),
            whole(act),
            whole(p["feed_t"], layer),
            strip(p["small"], BLOCK, 8, layer),
            strip(p["up"], BLOCK, 8, layer),
            whole(final),
        ],
        [
            result((tokens, MODEL_WIDTH), jnp.float32),
            result((tokens, LANES), jnp.float32),
            result((tokens if with_norm else 16, MODEL_WIDTH), jnp.bfloat16),
        ],
        scratch=slots_for(unit_fp, BLOCK, MODEL_WIDTH),
        flops=2 * tokens * MODEL_WIDTH * HIDDEN_UNITS,
    )


def three_parts(value):
    first = low(value)
    rest = value - first.astype(jnp.float32)
    second = low(rest)
    return [first, second, low(rest - second.astype(jnp.float32))]


def head_kernel(h, table, out, logits, total, top, bulk):
    j = pl.program_id(0)

    @pl.when(j == 0)
    def _():
        top[...] = jnp.full_like(top, NEGATIVE)
        bulk[...] = jnp.zeros_like(bulk)
        total[...] = jnp.zeros_like(total)

    def part(rows):
        logits[...] = product_right_transposed(h[rows, :], table[...])
        before = top[rows, :]
        now = jnp.maximum(before, jnp.max(logits[...], axis=1, keepdims=True))
        fade = jnp.exp(before - now)
        top[rows, :] = now
        weight = jnp.exp(logits[...] - now)
        bulk[rows, :] = bulk[rows, :] * fade + jnp.sum(weight, axis=1, keepdims=True)
        total[rows, :] = total[rows, :] * fade + product_plain(low(weight), table[...])

    over_rows(h.shape[0], logits.shape[0], part)

    @pl.when(j == pl.num_programs(0) - 1)
    def _():
        out[:, :MODEL_WIDTH] = low(total[...])
        columns = three_parts(top[...]) + three_parts(bulk[...])
        rest = jnp.zeros((h.shape[0], 128 - len(columns)), jnp.bfloat16)
        out[:, MODEL_WIDTH:] = jnp.concatenate(columns + [rest], axis=1)


def head(h, table):
    tokens, vocab = h.shape[0], table.shape[0]
    steps = 3 if vocab % 48 == 0 else 1
    tile = vocab // steps
    chunk = min(512, tokens)
    (out,) = launch(
        head_kernel,
        (steps,),
        [whole(h), rows_strip(table, tile, lambda j: j)],
        [result((tokens, MODEL_WIDTH + 128), jnp.bfloat16)],
        scratch=[
            pltpu.VMEM((chunk, tile), jnp.float32),
            pltpu.VMEM((tokens, MODEL_WIDTH), jnp.float32),
            pltpu.VMEM((tokens, 1), jnp.float32),
            pltpu.VMEM((tokens, 1), jnp.float32),
        ],
        flops=4 * tokens * vocab * MODEL_WIDTH,
    )
    return out


def head_back_kernel(parts, targets, h, x3, final, mask, terms, d_x3, d_hidden):
    tails = [
        parts[n, :, MODEL_WIDTH:].astype(jnp.float32) for n in range(parts.shape[0])
    ]
    tops = [tail[:, 0:1] + tail[:, 1:2] + tail[:, 2:3] for tail in tails]
    sums = [tail[:, 3:4] + tail[:, 4:5] + tail[:, 5:6] for tail in tails]
    top = tops[0]
    for other in tops[1:]:
        top = jnp.maximum(top, other)
    whole_sum = sum(s * jnp.exp(t - top) for t, s in zip(tops, sums))
    lse = top + jnp.log(whole_sum)
    wanted = targets[...]
    logit = jnp.sum(h[...].astype(jnp.float32) * wanted, axis=1, keepdims=True)
    terms[...] = (lse - logit) * mask[...]
    gathered = -wanted
    for n, t in enumerate(tops):
        gathered = gathered + parts[n, :, :MODEL_WIDTH].astype(jnp.float32) * jnp.exp(t - lse)
    d_hidden[...] = gathered * mask[...]
    norm_back_into(d_x3, d_hidden, x3, final[...].astype(jnp.float32)[0:1])


def head_back(parts, targets, h, x3, final, mask):
    count = h.shape[0]
    return launch(
        head_back_kernel,
        (1,),
        [whole(parts), some_rows(targets, count, targets.shape[0] // count - 1), whole(h), whole(x3), whole(final), whole(mask)],
        [
            result((count, 1), jnp.float32),
            result((count, MODEL_WIDTH), jnp.float32),
        ],
        scratch=[pltpu.VMEM((count, MODEL_WIDTH), jnp.float32)],
    )


def output_back(d_heads, grad_uo, grad_do, d_x2, o, uo, w_o, u_o, d_o):
    d_low = low(d_x2[...])
    grad_uo[...] = ADAPTER_SCALE * product_left_transposed(uo[...], d_low)
    duo = low(ADAPTER_SCALE * product_right_transposed(d_low, u_o[...]))
    grad_do[...] = product_left_transposed(duo, o[...])
    d_heads[...] = low(
        product_right_transposed(d_low, w_o[...]) + product_plain(duo, d_o[...])
    )


def front_last_back_kernel(unit, index, *refs):
    pieces, refs = taken(refs, unit)
    d_query, d_key, d_value, a, a_sel, ua, ua_sel, up, down, d_x2, x, gain = refs[:12]
    d_x, grad_up, grad_down, rows, rows_sel, inner, inner_sel, slots, sems = refs[12:]
    j = pl.program_id(0)
    weight = next_strip(unit, pieces, slots, sems, BLOCK)

    @pl.when(j == 0)
    def _():
        rows[...] = jnp.zeros_like(rows)
        inner[...] = jnp.zeros_like(inner)

    @pl.when(j == 0)
    def _():
        gradient = d_query[...]
        grad_up[...] = ADAPTER_SCALE * product_left_transposed(ua_sel[...], gradient)
        inner_sel[...] = ADAPTER_SCALE * product_right_transposed(gradient, up[...])
        rows_sel[...] = product_right_transposed(gradient, weight[...])

    def step(ref):
        gradient = ref[...]
        grad_up[...] = ADAPTER_SCALE * product_left_transposed(ua[...], gradient)
        inner[...] += ADAPTER_SCALE * product_right_transposed(gradient, up[...])
        rows[...] += product_right_transposed(gradient, weight[...])

    pl.when(j == 1)(lambda: step(d_key))
    pl.when(j == 2)(lambda: step(d_value))

    @pl.when(j == pl.num_programs(0) - 1)
    def _():
        last, last_sel = low(inner[...]), low(inner_sel[...])
        grad_down[...] = product_left_transposed(last, a[...]) + product_left_transposed(
            last_sel, a_sel[...]
        )
        rows[...] += product_plain(last, down[...])
        rows_sel[...] += product_plain(last_sel, down[...])
        add_rows(index, rows_sel, rows)
        norm_back_into(d_x, rows, x, gain[...])
        add_rows(index, d_x2, d_x)


def front_last_back(index, d_query, d_key, d_value, saved, d_x2, x, unit, p, layer):
    a, a_sel, ua, ua_sel = saved
    tokens, count = x.shape[0], index.shape[0]
    return launch(
        partial(front_last_back_kernel, unit),
        (3,),
        unit.operands()
        + [
            whole(d_query),
            whole(d_key),
            whole(d_value),
            whole(a),
            whole(a_sel),
            whole(ua),
            whole(ua_sel),
            strip(p["up"], BLOCK, lambda j: j, layer),
            whole(p["down_t"], layer, 0),
            whole(d_x2),
            whole(x),
            strip(p["small"], BLOCK, 9, layer),
        ],
        [
            result((tokens, MODEL_WIDTH), jnp.float32),
            result((LANES, 3 * MODEL_WIDTH), jnp.float32, (LANES, BLOCK), lambda j, *_: (0, j)),
            result((LANES, MODEL_WIDTH), jnp.float32),
        ],
        scratch=[
            pltpu.VMEM((tokens, MODEL_WIDTH), jnp.float32),
            pltpu.VMEM((count, MODEL_WIDTH), jnp.float32),
            pltpu.VMEM((tokens, LANES), jnp.float32),
            pltpu.VMEM((count, LANES), jnp.float32),
        ]
        + slots_for(unit, MODEL_WIDTH, BLOCK),
        scalars=(index,),
        flops=4 * tokens * MODEL_WIDTH**2,
    )


def feed_back_kernel(unit, unit_fc, unit_fp, *refs):
    pieces, pieces_fc, pieces_fp, refs = taken(refs, unit, unit_fc, unit_fp)
    d_x3, x2, m, um, ug, uo, o, act, slope, d_fp, u_fc, u_fp, d_fc, gain, u_o, d_o = refs[:16]
    d_x2, d_heads, grad_ufp, grad_dfp, grad_ufc, grad_dfc, grad_uo, grad_do = refs[16:24]
    d_out, dug, d_pre, inner, d_feed, weight_o, sems_o, slots, sems = refs[24:]
    j = pl.program_id(0)
    last = pl.num_programs(0) - 1
    out_moves = moves(unit, pieces, weight_o, sems_o, 3, BLOCK)

    def each(step, act):
        slot = lax.rem(step, 2)
        for some, refs, first in ((unit_fp, pieces_fp, 0), (unit_fc, pieces_fc, FEED_STEPS)):

            @pl.when((step >= first) & (step < first + FEED_STEPS))
            def _(some=some, refs=refs, first=first):
                column = jnp.clip(step - first, 0, FEED_STEPS - 1)
                act(moves(some, refs, slots.at[slot], sems.at[slot], column, BLOCK))

    pl.when(j == 0)(lambda: each(j, begin))
    pl.when(j < last)(lambda: each(j + 1, begin))
    pl.when(j == last)(lambda: begin(out_moves))

    @pl.when(j == 0)
    def _():
        d_out[...] = low(d_x3[...])
        dug[...] = low(ADAPTER_SCALE * product_right_transposed(d_out[...], u_fp[...]))
        grad_ufp[...] = ADAPTER_SCALE * product_left_transposed(low(ug[...]), d_out[...])
        inner[...] = jnp.zeros_like(inner)
        d_feed[...] = jnp.zeros_like(d_feed)

    each(j, finish)
    weight = slots.at[lax.rem(j, 2)]

    @pl.when(j < FEED_STEPS)
    def _():
        d_act = product_right_transposed(d_out[...], weight[...])
        from_act = product_left_transposed(dug[...], act[...])
        for n in range(PIECES):
            place = pl.ds(pl.multiple_of((n * FEED_STEPS + j) * CHUNK, CHUNK), CHUNK)
            part = slice(n * CHUNK, (n + 1) * CHUNK)
            value = d_act[:, part] + product_plain(dug[...], d_fp[:, place])
            d_pre[:, place] = low(value * slope[:, place].astype(jnp.float32))
            grad_dfp[:, place] = from_act[:, part]

    @pl.when(j >= FEED_STEPS)
    def _():
        columns = pl.ds(pl.multiple_of((j - FEED_STEPS) * BLOCK, BLOCK), BLOCK)
        gradient = d_pre[:, columns]
        grad_ufc[...] = ADAPTER_SCALE * product_left_transposed(um[...], gradient)
        inner[...] += ADAPTER_SCALE * product_right_transposed(gradient, u_fc[...])
        d_feed[...] += product_right_transposed(gradient, weight[...])

    @pl.when(j == last)
    def _():
        dum = low(inner[...])
        grad_dfc[...] = product_left_transposed(dum, m[...])
        d_feed[...] += product_plain(dum, d_fc[...])
        norm_back_into(d_x2, d_feed, x2, gain[...], d_x3)
        finish(out_moves)
        output_back(d_heads, grad_uo, grad_do, d_x2, o, uo, weight_o, u_o, d_o)


def feed_back(d_x3, saved, unit, unit_fc, unit_fp, p, layer):
    x2, m, um, ug, uo, o, act, slope = saved
    tokens = x2.shape[0]
    square = (LANES, MODEL_WIDTH), jnp.float32
    return launch(
        partial(feed_back_kernel, unit, unit_fc, unit_fp),
        (2 * FEED_STEPS,),
        unit.operands()
        + unit_fc.operands()
        + unit_fp.operands()
        + [
            whole(d_x3),
            whole(x2),
            whole(m),
            whole(um),
            whole(ug),
            whole(uo),
            whole(o),
            strip(act, BLOCK, feed_step),
            whole(slope),
            whole(p["feed_t"], layer),
            strip(p["up"], BLOCK, lambda j: FIRST_FEED + late_step(j), layer),
            strip(p["up"], BLOCK, 8, layer),
            whole(p["down_t"], layer, 2),
            strip(p["small"], BLOCK, 11, layer),
            strip(p["up"], BLOCK, 3, layer),
            whole(p["down_t"], layer, 1),
        ],
        [
            result((tokens, MODEL_WIDTH), jnp.float32),
            result((tokens, MODEL_WIDTH), jnp.bfloat16),
            result(*square),
            result((LANES, HIDDEN_UNITS), jnp.float32),
            result(
                (LANES, HIDDEN_UNITS), jnp.float32, (LANES, BLOCK), lambda j: (0, late_step(j))
            ),
            result(*square),
            result(*square),
            result(*square),
        ],
        scratch=[
            pltpu.VMEM((tokens, MODEL_WIDTH), jnp.bfloat16),
            pltpu.VMEM((tokens, LANES), jnp.bfloat16),
            pltpu.VMEM((tokens, HIDDEN_UNITS), jnp.bfloat16),
            pltpu.VMEM((tokens, LANES), jnp.float32),
            pltpu.VMEM((tokens, MODEL_WIDTH), jnp.float32),
        ]
        + one_slot_for(unit)
        + slots_for(unit_fc, MODEL_WIDTH, BLOCK),
        flops=2 * tokens * MODEL_WIDTH * (MODEL_WIDTH + 2 * HIDDEN_UNITS),
    )


def front_back_kernel(d_query, d_key, d_value, a, ua, up, grad_up, grad_down):
    inner = 0.0
    for n, ref in enumerate((d_query, d_key, d_value)):
        columns = slice(n * MODEL_WIDTH, (n + 1) * MODEL_WIDTH)
        grad_up[:, columns] = ADAPTER_SCALE * product_left_transposed(ua[...], ref[...])
        inner = inner + ADAPTER_SCALE * product_right_transposed(ref[...], up[:, columns])
    grad_down[...] = product_left_transposed(low(inner), a[...])


def front_back(d_query, d_key, d_value, a, ua, p, layer):
    return launch(
        front_back_kernel,
        (1,),
        [
            whole(d_query),
            whole(d_key),
            whole(d_value),
            whole(a),
            whole(ua),
            strip(p["up"], 3 * MODEL_WIDTH, 0, layer),
        ],
        [
            result((LANES, 3 * MODEL_WIDTH), jnp.float32),
            result((LANES, MODEL_WIDTH), jnp.float32),
        ],
    )


def pack_kernel(columns, *refs):
    extras, parts, out = refs[0], refs[1:-1], refs[-1]
    shards, width = out.shape[0], out.shape[2] - 128
    three = [part.astype(jnp.float32) for part in three_parts(extras[...])]
    rest = jnp.zeros((out.shape[1] - len(three), 128), jnp.float32)
    for n in range(shards):
        out[n, :, width:] = low(jnp.concatenate(three + [rest], axis=0))
    layers = {}
    for part, (row, start) in zip(parts, columns):
        layers.setdefault(start, []).append(part)
    for start, refs in layers.items():
        values = low(jnp.concatenate([ref[0:ADAPTER_RANK, :] for ref in refs], axis=0))
        size = values.shape[1]
        done = 0
        while done < size:
            block, offset = divmod(start + done, width)
            step = min(width - offset, size - done)
            out[block, :, offset : offset + step] = values[:, done : done + step]
            done += step


def packed(by_layer, extras):
    shards = lax.axis_size("fsdp")
    columns, parts = [], []
    for layer, row in enumerate(by_layer):
        start = 0
        for part in row:
            parts.append(part)
            columns.append((layer * ADAPTER_RANK, start))
            start += part.shape[1]
    shape = (shards, len(by_layer) * ADAPTER_RANK, start // shards + 128)
    (out,) = launch(
        partial(pack_kernel, tuple(columns)),
        (1,),
        [whole(extras)] + [whole(part) for part in parts],
        [result(shape, jnp.bfloat16)],
    )
    return out


def asking(table, ids, needed):
    shards = lax.axis_size("fsdp")
    total = ids.shape[0]
    order = jnp.arange(total, dtype=jnp.int32)
    owner = ids // table.shape[0]
    local = ids - owner * table.shape[0]
    same = (ids[:, None] == ids[None, :]) & needed[None, :]
    first = jnp.min(jnp.where(same, order[None, :], total), axis=1)
    leads = needed & (first == order)
    rank = jnp.sum(
        (leads & (owner[:, None] == owner[None, :]) & (order[None, :] < first[:, None])).astype(
            jnp.int32
        ),
        axis=1,
    )
    rounds = (jnp.max(jnp.where(needed, rank, 0)) + CAPACITY) // CAPACITY

    spots = jnp.arange(shards * CAPACITY, dtype=jnp.int32)

    def place_of(turn):
        return jnp.where(
            needed & (rank // CAPACITY == turn), owner * CAPACITY + rank % CAPACITY, -1
        )

    def ask(turn):
        place = place_of(turn)
        asked = jnp.sum(
            jnp.where(leads[:, None] & (place[:, None] == spots[None, :]), local[:, None], 0), axis=0
        )
        return asked.reshape(shards, CAPACITY)

    def sent_for(asked):
        return table.at[asked.reshape(-1)].get(mode="promise_in_bounds")

    def exchanged(part):
        return lax.all_to_all(part, "fsdp", 0, 0, tiled=True)

    def found(turn, back):
        pick = (place_of(turn)[:, None] == spots[None, :]).astype(jnp.bfloat16)
        return product_plain(pick, back)

    def with_rounds(most, added):
        def more(so_far):
            return lax.fori_loop(
                1,
                most,
                lambda turn, total: total
                + found(turn, exchanged(sent_for(exchanged(ask(turn))))),
                so_far,
            )

        return lax.cond(most > 1, more, lambda so_far: so_far, added)

    return ask, rounds, exchanged, sent_for, found, with_rounds


def as_low(numbers):
    return low(numbers // 256), low(numbers % 256)


def as_numbers(high, rest):
    return high.astype(jnp.int32) * 256 + rest.astype(jnp.int32)


def swap(part, bit):
    return lax.ppermute(part, "fsdp", [(i, i ^ bit) for i in range(lax.axis_size("fsdp"))])


def tie(parts, before):
    parts, _ = lax.optimization_barrier((parts, before))
    return parts


def hop(part):
    return lax.ppermute(
        part, "fsdp", [(i, i ^ (4 if i % 2 else 2)) for i in range(lax.axis_size("fsdp"))]
    )


class Gathering:
    PLACES = (0, 0), (1, 1), (2, 4), (3, 5), (5, 3), (4, 2), (7, 7), (6, 6)

    def __init__(self, shard, in_chunks=False):
        self.shard, self.in_chunks = shard, in_chunks
        self.direct = lax.axis_size("fsdp") == PIECES

    def begin(self, before=()):
        if self.direct:
            own = chunked(self.shard) if self.in_chunks else self.shard
            own = tie(own, before)
            other = swap(own, 1)
            self.arrays = own, other, hop(own), hop(other)

    def after_first(self, value):
        return tie(value, self.arrays[1]) if self.direct else value

    def after_last(self, value):
        return tie(value, self.arrays[4]) if self.direct else value

    def pass_on(self, value):
        if self.direct:
            own, other, first, second = self.arrays
            first, value = lax.optimization_barrier((first, value))
            handed = swap(first, 1)
            self.arrays = own, other, first, second, handed, swap(second, 1), hop(handed)
        return value

    def settle(self, value):
        if not self.direct:
            parts = jnp.split(lax.all_gather(self.shard, "fsdp", axis=0, tiled=True), PIECES)
            parts = [chunked(part) for part in parts] if self.in_chunks else parts
            return value, Unit(tuple(range(PIECES)), tuple(parts), parts[0].shape[0])
        far, value = lax.optimization_barrier((self.arrays[-1], value))
        arrays = self.arrays[:-1] + (far, swap(far, 1))
        return value, Unit(self.PLACES, arrays, arrays[0].shape[0])


def everywhere(part):
    shards = lax.axis_size("fsdp")
    return lax.all_to_all(
        jnp.tile(part, (shards,) + (1,) * (part.ndim - 1)), "fsdp", 0, 0, tiled=True
    )


def owned_parts(parts):
    shards = lax.axis_size("fsdp")
    rows = parts.shape[0] // shards
    return lax.all_to_all(parts, "fsdp", 0, 0, tiled=True).reshape(
        (shards, rows) + parts.shape[1:]
    )


def summed_everywhere(blocks):
    shards, rows, columns = blocks.shape
    groups = lax.axis_size("dp")
    width = columns - 128
    parts = owned_parts(blocks.reshape(shards * rows, columns)).astype(jnp.float32)
    block = jnp.sum(parts, axis=0)
    others = [
        lax.ppermute(block, "dp", [(i, (i + k) % groups) for i in range(groups)])
        for k in range(1, groups)
    ]
    stacked = jnp.stack([block] + others)
    order = (lax.axis_index("dp") - jnp.arange(groups)) % groups
    ranks = (order[None, :] == jnp.arange(groups)[:, None])[:, :, None, None]
    total = jnp.sum(jnp.sum(jnp.where(ranks, stacked[None], 0.0), axis=1), axis=0)
    gathered = everywhere(low(total[:, :width])).reshape(shards, rows, width)
    sums = total[:3, width : width + 2]
    return (
        gathered.astype(jnp.float32).transpose(1, 0, 2).reshape(rows, shards * width),
        sums[0] + sums[1] + sums[2],
    )


def body(
    input_token_ids,
    lengths,
    scored_slots,
    scored_targets,
    wte,
    wpe,
    frozen_attention,
    frozen_feed_input,
    frozen_feed_output,
    frozen_bias_gain,
    final_norm_params,
    adapter_down,
    adapter_down_feed,
    adapter_up,
    first_moment_down,
    first_moment_feed,
    first_moment_up,
    second_moment_down,
    second_moment_feed,
    second_moment_up,
    optimizer_step,
):
    micro, seqs, seq = input_token_ids.shape
    rows = micro * seqs
    picks = scored_slots.shape[2]
    layers = frozen_attention.shape[0]
    shards = lax.axis_size("fsdp")
    row_lengths = lengths.reshape(rows)
    slots = scored_slots.reshape(rows, picks)
    valid = slots < row_lengths[:, None]
    mask = valid.reshape(-1, 1).astype(jnp.float32)
    all_slots = jnp.tile(jnp.arange(seq, dtype=jnp.int32)[None], (rows, 1))

    useful = jnp.max(jnp.where(valid, slots, -1), axis=1)
    needed = jnp.concatenate([(all_slots <= useful[:, None]).reshape(-1), valid.reshape(-1)])
    ids = jnp.concatenate([input_token_ids.reshape(-1), scored_targets.reshape(-1)])
    attention_one, attention_two = Gathering(frozen_attention[0]), Gathering(frozen_attention[1])
    feed_in_one, feed_in_two = Gathering(frozen_feed_input[0]), Gathering(frozen_feed_input[1])
    feed_out_one = Gathering(frozen_feed_output[0], in_chunks=True)
    feed_out_two = Gathering(frozen_feed_output[1], in_chunks=True)
    attention_one.begin()
    ask, rounds, exchanged, sent_for, found, with_rounds = asking(wte, ids, needed)
    count = CAPACITY
    requests = as_low(jnp.concatenate([ask(0), jnp.full((shards, 1), rounds, jnp.int32)], 1))
    biases = jnp.tile(frozen_bias_gain.reshape(1, -1), (shards, 1))
    message = jnp.concatenate([*requests, biases], 1)
    got = exchanged(attention_one.after_first(message))
    got = attention_one.pass_on(got)
    feed_in_one.begin(got)
    numbers = as_numbers(got[:, : count + 1], got[:, count + 1 : 2 * count + 2])
    small = (
        got[:, 2 * count + 2 :].reshape(shards, layers, -1).transpose(1, 0, 2).reshape(layers, 1, -1)
    )
    sent = sent_for(attention_one.after_last(numbers[:, :count]))
    most = jnp.max(numbers[:, count])
    extra = LANES - ADAPTER_RANK
    down_t = adapter_down.reshape(layers, MODEL_WIDTH, 3, ADAPTER_RANK).transpose(0, 2, 3, 1)
    p = {
        "small": small.astype(jnp.float32),
        "down_t": low(jnp.pad(down_t, ((0, 0), (0, 0), (0, extra), (0, 0)))),
        "feed_t": low(jnp.pad(adapter_down_feed.transpose(0, 2, 1), ((0, 0), (0, extra), (0, 0)))),
        "up": low(jnp.pad(adapter_up, ((0, 0), (0, extra), (0, 0)))),
    }
    places = jnp.concatenate([wpe.astype(jnp.float32)] * rows)
    places = jnp.pad(places, ((0, rows * picks), (0, 0)))
    places = with_rounds(most, places)
    back, p, places = lax.optimization_barrier((exchanged(sent), p, places))
    back, attention_one = attention_one.settle(back)
    back = feed_in_one.pass_on(back)
    feed_out_one.begin(back)
    x0 = found(0, back) + places
    index = (slots + seq * jnp.arange(rows, dtype=jnp.int32)[:, None]).reshape(-1)

    qkv, a_one, ua_one = front(x0, rows * seq, attention_one, p, 0)
    qkv = feed_out_one.pass_on(qkv)
    attention_two.begin(qkv)
    split_qkv = (qkv, 0), (qkv, 1), (qkv, 2)
    o_one = attend(row_lengths, all_slots, *split_qkv)
    o_one, feed_in_one = feed_in_one.settle(o_one)
    o_one = attention_two.pass_on(o_one)
    feed_in_two.begin(o_one)
    x2_one, uo_one, m_one, um_one, act_one, slope_one = feed_in(
        x0, o_one, attention_one, feed_in_one, p, 0
    )
    act_one, feed_out_one = feed_out_one.settle(act_one)
    act_one = feed_in_two.pass_on(act_one)
    feed_out_two.begin(act_one)
    x1, ug_one, _ = feed_out(x2_one, act_one, feed_out_one, final_norm_params, p, 0, False)
    x1, attention_two = attention_two.settle(x1)
    x1 = feed_out_two.pass_on(x1)

    query, kv, a_two, a_sel, ua_two, ua_sel, x_sel = front_last(index, x1, attention_two, p, 1)
    query, feed_in_two = feed_in_two.settle(query)
    parts_two = (query, 0), (kv, 0), (kv, 1)
    o_two = attend(row_lengths, slots, *parts_two)
    x2_two, uo_two, m_two, um_two, act_two, slope_two = feed_in(
        x_sel, o_two, attention_two, feed_in_two, p, 1
    )
    act_two, feed_out_two = feed_out_two.settle(act_two)
    x3, ug_two, h = feed_out(x2_two, act_two, feed_out_two, final_norm_params, p, 1, True)

    weighed = owned_parts(head(everywhere(h), wte))
    terms, d_x3 = head_back(weighed, x0, h, x3, final_norm_params, mask)

    d_x2, d_heads, grad_ufp, grad_dfp, grad_ufc, grad_dfc, grad_uo, grad_do = feed_back(
        d_x3,
        (x2_two, m_two, um_two, ug_two, uo_two, o_two, act_two, slope_two),
        attention_two,
        feed_in_two,
        feed_out_two,
        p,
        1,
    )
    d_parts = attend_back(row_lengths, slots, *parts_two, d_heads)
    d_x1, grad_uqkv, grad_dqkv = front_last_back(
        index, *d_parts, (a_two, a_sel, ua_two, ua_sel), d_x2, x1, attention_two, p, 1
    )
    grads_two = [
        grad_dqkv, grad_do, grad_dfc, grad_dfp, grad_uqkv, grad_uo, grad_ufc, grad_ufp
    ]

    _, d_heads, grad_ufp, grad_dfp, grad_ufc, grad_dfc, grad_uo, grad_do = feed_back(
        d_x1,
        (x2_one, m_one, um_one, ug_one, uo_one, o_one, act_one, slope_one),
        attention_one,
        feed_in_one,
        feed_out_one,
        p,
        0,
    )
    d_parts = attend_back(row_lengths, all_slots, *split_qkv, d_heads)
    grad_uqkv, grad_dqkv = front_back(*d_parts, a_one, ua_one, p, 0)
    grads_one = [
        grad_dqkv, grad_do, grad_dfc, grad_dfp, grad_uqkv, grad_uo, grad_ufc, grad_ufp
    ]

    tail = jnp.pad(jnp.stack([jnp.sum(terms), jnp.sum(mask)])[None], ((0, 0), (0, 126)))
    gradients, totals = summed_everywhere(packed((grads_one, grads_two), tail))
    loss_total, count = totals[0], totals[1]
    gradients = gradients / count
    norm = jnp.sqrt(jnp.sum(gradients * gradients))
    by_layer = gradients.reshape(layers, ADAPTER_RANK, -1)
    gradient_tree = [
        by_layer[:, :, : 3 * MODEL_WIDTH]
        .reshape(layers, ADAPTER_RANK, 3, MODEL_WIDTH)
        .transpose(0, 3, 2, 1)
        .reshape(layers, MODEL_WIDTH, 3 * ADAPTER_RANK),
        by_layer[:, :, 3 * MODEL_WIDTH : 3 * MODEL_WIDTH + HIDDEN_UNITS].transpose(0, 2, 1),
        by_layer[:, :, 3 * MODEL_WIDTH + HIDDEN_UNITS :],
    ]
    scale_factor = jnp.minimum(1.0, CLIP / (norm + 1e-06))
    step_number = optimizer_step[0].astype(jnp.float32)
    updated = [
        moment_update(weight, first, second, gradient_value, scale_factor, step_number)
        for weight, first, second, gradient_value in zip(
            (adapter_down, adapter_down_feed, adapter_up),
            (first_moment_down, first_moment_feed, first_moment_up),
            (second_moment_down, second_moment_feed, second_moment_up),
            gradient_tree,
        )
    ]
    return (
        loss_total / count,
        norm,
        *(part[0] for part in updated),
        *(part[1] for part in updated),
        *(part[2] for part in updated),
        terms.reshape(micro, seqs, picks),
    )


def solution(mesh):
    in_specs = (
        P(None, ("dp", "fsdp"), None),
        P(None, ("dp", "fsdp")),
        P(None, ("dp", "fsdp"), None),
        P(None, ("dp", "fsdp"), None),
        P("fsdp", None),
        P(),
        P(None, "fsdp", None),
        P(None, "fsdp", None),
        P(None, "fsdp", None),
        P(None, "fsdp"),
        P(),
        P(),
        P(),
        P(),
        P(),
        P(),
        P(),
        P(),
        P(),
        P(),
        P(),
    )
    out_specs = (
        P(),
        P(),
        P(),
        P(),
        P(),
        P(),
        P(),
        P(),
        P(),
        P(),
        P(),
        P(None, ("dp", "fsdp"), None),
    )
    return jax.shard_map(body, mesh=mesh, in_specs=in_specs, out_specs=out_specs, check_vma=False)
```

```python
import math
from functools import partial
from typing import NamedTuple

import jax
import jax.numpy as jnp
from jax import lax
from jax.experimental import pallas as pl
from jax.experimental.pallas import tpu as pltpu
from jax.sharding import PartitionSpec as P

MODEL_WIDTH = 1024
H = 16
HD = 64
HIDDEN_UNITS = 4096
ADAPTER_RANK = 4


ADAPTER_SCALE = 8.0
EPS_NORM = 1e-05
BETA_ONE = 0.9
BETA_TWO = 0.999
RATE = 0.02
DECAY = 0.01
EPS_ADAM = 1e-08
CLIP = 0.02
NEGATIVE = -1e30


def product_plain(left, right):
    return jnp.dot(left, right, preferred_element_type=jnp.float32)


def product_left_transposed(left, right):
    return lax.dot_general(
        left, right, (((0,), (0,)), ((), ())), preferred_element_type=jnp.float32
    )


def product_right_transposed(left, right):
    return lax.dot_general(
        left, right, (((1,), (1,)), ((), ())), preferred_element_type=jnp.float32
    )


def norm_fwd(hidden_rows, norm_gain, norm_shift):
    row_mean = jnp.mean(hidden_rows, axis=-1, keepdims=True)
    centered = hidden_rows - row_mean
    inverse_deviation = lax.rsqrt(jnp.mean(centered * centered, axis=-1, keepdims=True) + EPS_NORM)
    normalized_rows = centered * inverse_deviation
    return (normalized_rows * norm_gain + norm_shift, normalized_rows, inverse_deviation)


def norm_backward(gradient_value, normalized_rows, inverse_deviation, norm_gain):
    scaled_rows = gradient_value * norm_gain
    return inverse_deviation * (
        scaled_rows
        - jnp.mean(scaled_rows, axis=-1, keepdims=True)
        - normalized_rows * jnp.mean(scaled_rows * normalized_rows, axis=-1, keepdims=True)
    )


def moment_update(weight, first, second, gradient_value, scale_factor, step_number):
    clipped = gradient_value * scale_factor
    first_new = BETA_ONE * first + (1.0 - BETA_ONE) * clipped
    second_new = BETA_TWO * second + (1.0 - BETA_TWO) * clipped * clipped
    first_hat = first_new / (1.0 - BETA_ONE**step_number)
    second_hat = second_new / (1.0 - BETA_TWO**step_number)
    weight_new = weight - RATE * (first_hat / (jnp.sqrt(second_hat) + EPS_ADAM) + DECAY * weight)
    return (weight_new, first_new, second_new)


CAPACITY = 80


LANES = 16
HALF_TILE = 512
BLOCK = 1024
VMEM_BYTES = 63 * 2**20


def whole(array, *lead):
    shape = (None,) * len(lead) + array.shape[len(lead) :]
    place = lead + (0,) * (array.ndim - len(lead))
    return array, pl.BlockSpec(shape, lambda *_: place, pipeline_mode=pl.Buffered(1))


def some_rows(array, count, row=0):
    shape = (count, array.shape[1])
    return array, pl.BlockSpec(shape, lambda *_: (row, 0), pipeline_mode=pl.Buffered(1))


def strip(array, width, column, *lead):
    shape = (None,) * len(lead) + (array.shape[-2], width)
    if callable(column):
        return array, pl.BlockSpec(shape, lambda j, *_: lead + (0, column(j)))
    place = lead + (0, column)
    return array, pl.BlockSpec(shape, lambda *_: place, pipeline_mode=pl.Buffered(1))


def rows_strip(array, height, row, *lead):
    shape = (None,) * len(lead) + (height, array.shape[-1])
    return array, pl.BlockSpec(shape, lambda j, *_: lead + (row(j), 0))


def result(shape, dtype, block=None, place=None):
    kind = jax.ShapeDtypeStruct(shape, dtype)
    if block is None:
        block, zeros = shape, (0,) * len(shape)
        return kind, pl.BlockSpec(block, lambda *_: zeros)
    return kind, pl.BlockSpec(block, place)


def launch(kernel, grid, operands, results, scratch=(), scalars=(), flops=0):
    moved = sum(a.size * a.dtype.itemsize for a, _ in operands)
    return pl.pallas_call(
        kernel,
        out_shape=[kind for kind, _ in results],
        grid_spec=pltpu.PrefetchScalarGridSpec(
            num_scalar_prefetch=len(scalars),
            grid=grid,
            in_specs=[spec for _, spec in operands],
            out_specs=[spec for _, spec in results],
            scratch_shapes=list(scratch),
        ),
        compiler_params=pltpu.CompilerParams(vmem_limit_bytes=VMEM_BYTES),
        cost_estimate=pl.CostEstimate(flops=flops, bytes_accessed=moved, transcendentals=0),
    )(*scalars, *(a for a, _ in operands))


class Unit(NamedTuple):
    places: tuple
    arrays: tuple
    rows: int

    def operands(self):
        return [(array, pl.BlockSpec(memory_space=pltpu.HBM)) for array in self.arrays]


def shard_of(place):
    if isinstance(place, int):
        return place
    me = lax.axis_index("fsdp")
    return jnp.bitwise_xor(me, jnp.where(lax.rem(me, 2) == 0, *place))


def moves(unit, refs, target, sems, column, width):
    columns = pl.ds(pl.multiple_of(column * width, width), width)
    copies = []
    for n, (place, ref) in enumerate(zip(unit.places, refs)):
        start = pl.multiple_of(shard_of(place) * unit.rows, 16)
        copies.append(
            pltpu.make_async_copy(
                ref.at[:, columns], target.at[pl.ds(start, ref.shape[0]), :], sems.at[n]
            )
        )
    return copies


def begin(copies):
    for copy in copies:
        copy.start()


def finish(copies):
    for copy in copies:
        copy.wait()


def next_strip(unit, refs, slots, sems, width):
    j = pl.program_id(0)

    def strip_moves(step):
        slot = lax.rem(step, 2)
        return moves(unit, refs, slots.at[slot], sems.at[slot], step, width)

    pl.when(j == 0)(lambda: begin(strip_moves(j)))
    pl.when(j + 1 < pl.num_programs(0))(lambda: begin(strip_moves(j + 1)))
    finish(strip_moves(j))
    return slots.at[lax.rem(j, 2)]


def slots_for(unit, height, width):
    return [
        pltpu.VMEM((2, height, width), jnp.bfloat16),
        pltpu.SemaphoreType.DMA((2, len(unit.arrays))),
    ]


def one_slot_for(unit):
    return [
        pltpu.VMEM((MODEL_WIDTH, BLOCK), jnp.bfloat16),
        pltpu.SemaphoreType.DMA((len(unit.arrays),)),
    ]


def taken(refs, *units):
    groups = []
    for unit in units:
        groups.append(refs[: len(unit.arrays)])
        refs = refs[len(unit.arrays) :]
    return groups + [refs]


def over_rows(total, size, work):
    def turn(i, carry):
        work(pl.ds(pl.multiple_of(i * size, size), size))
        return carry

    lax.fori_loop(0, total // size, turn, 0)


def low(value):
    return value.astype(jnp.bfloat16)


def adapter(inner, up):
    return ADAPTER_SCALE * product_plain(inner, up)


def norm_into(out_ref, rows_ref, gain, shift):
    def part(rows):
        out_ref[rows, :] = low(norm_fwd(rows_ref[rows, :], gain, shift)[0])

    over_rows(rows_ref.shape[0], min(64, rows_ref.shape[0]), part)


def norm_back_into(out_ref, gradient_ref, rows_ref, gain, residual_ref=None):
    def part(rows):
        _, normalized, deviation = norm_fwd(rows_ref[rows, :], gain, 0.0)
        value = norm_backward(gradient_ref[rows, :], normalized, deviation, gain)
        if residual_ref is not None:
            value = value + residual_ref[rows, :]
        out_ref[rows, :] = value

    over_rows(rows_ref.shape[0], min(64, rows_ref.shape[0]), part)


def front_kernel(unit, *refs):
    pieces, refs = taken(refs, unit)
    x, gain, shift, bias, down, up, qkv, a, ua, slots, sems = refs
    weight = next_strip(unit, pieces, slots, sems, BLOCK)

    @pl.when(pl.program_id(0) == 0)
    def _():
        norm_into(a, x, gain[...], shift[...])
        ua[...] = low(product_right_transposed(a[...], down[...]))

    qkv[...] = low(product_plain(a[...], weight[...]) + bias[...] + adapter(ua[...], up[...]))


def front(x, tokens, unit, p, layer):
    return launch(
        partial(front_kernel, unit),
        (3,),
        unit.operands()
        + [
            some_rows(x, tokens),
            strip(p["small"], BLOCK, 9, layer),
            strip(p["small"], BLOCK, 10, layer),
            strip(p["small"], BLOCK, lambda j: j, layer),
            whole(p["down_t"], layer, 0),
            strip(p["up"], BLOCK, lambda j: j, layer),
        ],
        [
            result((tokens, 3 * MODEL_WIDTH), jnp.bfloat16, (tokens, BLOCK), lambda j: (0, j)),
            result((tokens, MODEL_WIDTH), jnp.bfloat16),
            result((tokens, LANES), jnp.bfloat16),
        ],
        scratch=slots_for(unit, MODEL_WIDTH, BLOCK),
        flops=6 * tokens * MODEL_WIDTH**2,
    )


def pick_rows(index, source, target):
    def turn(i, carry):
        target[pl.ds(i, 1), :] = source[pl.ds(index[i], 1), :]
        return carry

    lax.fori_loop(0, target.shape[0], turn, 0)


def add_rows(index, source, target):
    def turn(i, carry):
        rows = pl.ds(index[i], 1)
        target[rows, :] = target[rows, :] + source[pl.ds(i, 1), :]
        return carry

    lax.fori_loop(0, source.shape[0], turn, 0)


def front_last_kernel(unit, index, *refs):
    pieces, refs = taken(refs, unit)
    x, gain, shift, bias, down, up, q, kv, a, a_sel, ua, ua_sel, x_sel, slots, sems = refs
    j = pl.program_id(0)
    weight = next_strip(unit, pieces, slots, sems, BLOCK)

    @pl.when(j == 0)
    def _():
        norm_into(a, x, gain[...], shift[...])
        ua[...] = low(product_right_transposed(a[...], down[...]))
        pick_rows(index, x, x_sel)
        norm_into(a_sel, x_sel, gain[...], shift[...])
        ua_sel[...] = low(product_right_transposed(a_sel[...], down[...]))

    @pl.when(j == 0)
    def _():
        q[...] = low(
            product_plain(a_sel[...], weight[...]) + bias[...] + adapter(ua_sel[...], up[...])
        )

    @pl.when(j > 0)
    def _():
        kv[...] = low(product_plain(a[...], weight[...]) + bias[...] + adapter(ua[...], up[...]))


def front_last(index, x, unit, p, layer):
    tokens, count = x.shape[0], index.shape[0]
    return launch(
        partial(front_last_kernel, unit),
        (3,),
        unit.operands()
        + [
            whole(x),
            strip(p["small"], BLOCK, 9, layer),
            strip(p["small"], BLOCK, 10, layer),
            strip(p["small"], BLOCK, lambda j: j, layer),
            whole(p["down_t"], layer, 0),
            strip(p["up"], BLOCK, lambda j: j, layer),
        ],
        [
            result((count, MODEL_WIDTH), jnp.bfloat16),
            result(
                (tokens, 2 * MODEL_WIDTH),
                jnp.bfloat16,
                (tokens, BLOCK),
                lambda j, *_: (0, jnp.maximum(j - 1, 0)),
            ),
            result((tokens, MODEL_WIDTH), jnp.bfloat16),
            result((count, MODEL_WIDTH), jnp.bfloat16),
            result((tokens, LANES), jnp.bfloat16),
            result((count, LANES), jnp.bfloat16),
            result((count, MODEL_WIDTH), jnp.float32),
        ],
        scratch=slots_for(unit, MODEL_WIDTH, BLOCK),
        scalars=(index,),
        flops=4 * tokens * MODEL_WIDTH**2,
    )


def attend_kernel(lengths, slots, query, key, value, out):
    length = lengths[pl.program_id(0)]
    kpos = lax.broadcasted_iota(jnp.int32, (query.shape[0], key.shape[0]), 1)
    allowed = (kpos <= slots[...]) & (kpos < length)
    heads = []
    for start in range(0, query.shape[1], HD):
        part = slice(start, start + HD)
        raw = product_right_transposed(query[:, part], key[:, part]) * HD ** (-0.5)
        raw = jnp.where(allowed, raw, NEGATIVE)
        prob = jnp.exp(raw - jnp.max(raw, axis=1, keepdims=True))
        prob = prob * (1.0 / jnp.sum(prob, axis=1, keepdims=True))
        heads.append(product_plain(low(prob), value[:, part]))
    out[...] = low(jnp.concatenate(heads, axis=1))


def own_lanes(count, heads):
    shape = (heads * count, heads * HD)
    row = lax.broadcasted_iota(jnp.int32, shape, 0) // count
    lane = lax.broadcasted_iota(jnp.int32, shape, 1) // HD
    return row == lane


def stacked_heads(rows, own):
    heads = own.shape[0] // rows.shape[0]
    tall = jnp.concatenate([rows.astype(jnp.float32)] * heads, axis=0)
    return low(jnp.where(own, tall, 0.0))


def own_heads(tall, own, count):
    tall = jnp.where(own, tall, 0.0)
    total = tall[:count]
    for start in range(count, tall.shape[0], count):
        total = total + tall[start : start + count]
    return total


def few_scores(length, slots, tall, key):
    raw = product_right_transposed(tall, key[...]) * HD ** (-0.5)
    kpos = lax.broadcasted_iota(jnp.int32, raw.shape, 1)
    places = jnp.concatenate([slots[...]] * (raw.shape[0] // slots.shape[0]), axis=0)
    raw = jnp.where((kpos <= places) & (kpos < length), raw, NEGATIVE)
    prob = jnp.exp(raw - jnp.max(raw, axis=1, keepdims=True))
    return prob * (1.0 / jnp.sum(prob, axis=1, keepdims=True))


def attend_few_kernel(lengths, slots, query, key, value, out):
    count = query.shape[0]
    own = own_lanes(count, query.shape[1] // HD)
    prob = few_scores(lengths[pl.program_id(0)], slots, stacked_heads(query[...], own), key)
    out[...] = low(own_heads(product_plain(low(prob), value[...]), own, count))


def attend_few_back_kernel(lengths, slots, query, key, value, d_out, d_query, d_key, d_value):
    count = query.shape[0]
    own = own_lanes(count, query.shape[1] // HD)
    tall = stacked_heads(query[...], own)
    d_tall = stacked_heads(d_out[...], own)
    prob = few_scores(lengths[pl.program_id(0)], slots, tall, key)
    d_prob = product_right_transposed(d_tall, value[...])
    d_raw = low(prob * (d_prob - jnp.sum(prob * d_prob, axis=1, keepdims=True)))
    d_value[...] = low(product_left_transposed(low(prob), d_tall))
    d_key[...] = low(product_left_transposed(d_raw, tall) * HD ** (-0.5))
    d_query[...] = low(own_heads(product_plain(d_raw, key[...]), own, count) * HD ** (-0.5))


def head_blocks(array, height, third, steps):
    offset = third * steps
    return array, pl.BlockSpec((height, MODEL_WIDTH // steps), lambda r, h, *_: (r, offset + h))


def head_steps(count):
    return 1 if count > 128 else 1


def attend(lengths, slots, query, key, value):
    rows, count = slots.shape
    seq = key[0].shape[0] // rows
    steps = head_steps(count)
    column = slots.reshape(-1, 1)
    (out,) = launch(
        attend_kernel if count > 128 else attend_few_kernel,
        (rows, steps),
        [
            (column, pl.BlockSpec((count, 1), lambda r, h, *_: (r, 0))),
            head_blocks(query[0], count, query[1], steps),
            head_blocks(key[0], seq, key[1], steps),
            head_blocks(value[0], seq, value[1], steps),
        ],
        [
            result(
                (rows * count, MODEL_WIDTH),
                jnp.bfloat16,
                (count, MODEL_WIDTH // steps),
                lambda r, h, *_: (r, h),
            )
        ],
        scalars=(lengths,),
        flops=4 * rows * count * seq * MODEL_WIDTH,
    )
    return out


def attend_back_kernel(lengths, slots, query, key, value, d_out, d_query, d_key, d_value):
    length = lengths[pl.program_id(0)]
    kpos = lax.broadcasted_iota(jnp.int32, (key.shape[0], query.shape[0]), 0)
    allowed = (kpos <= slots[...]) & (kpos < length)
    parts = []
    for start in range(0, query.shape[1], HD):
        part = slice(start, start + HD)
        q, k, v, d_o = query[:, part], key[:, part], value[:, part], d_out[:, part]
        raw = product_right_transposed(k, q) * HD ** (-0.5)
        raw = jnp.where(allowed, raw, NEGATIVE)
        prob = jnp.exp(raw - jnp.max(raw, axis=0, keepdims=True))
        prob = prob * (1.0 / jnp.sum(prob, axis=0, keepdims=True))
        d_prob = product_right_transposed(v, d_o)
        d_raw = low(prob * (d_prob - jnp.sum(prob * d_prob, axis=0, keepdims=True)))
        parts.append(
            (
                product_left_transposed(d_raw, k) * HD ** (-0.5),
                product_plain(d_raw, q) * HD ** (-0.5),
                product_plain(low(prob), d_o),
            )
        )
    for n, ref in enumerate((d_query, d_key, d_value)):
        ref[...] = low(jnp.concatenate([part[n] for part in parts], axis=1))


def attend_back(lengths, slots, query, key, value, d_out):
    rows, count = slots.shape
    seq = key[0].shape[0] // rows
    steps = head_steps(count)
    heights = (count, seq, seq)
    return launch(
        attend_back_kernel if count > 128 else attend_few_back_kernel,
        (rows, steps),
        [
            (
                slots.reshape(rows, 1, count),
                pl.BlockSpec((None, 1, count), lambda r, h, *_: (r, 0, 0)),
            )
            if count > 128
            else (slots.reshape(-1, 1), pl.BlockSpec((count, 1), lambda r, h, *_: (r, 0))),
            head_blocks(query[0], count, query[1], steps),
            head_blocks(key[0], seq, key[1], steps),
            head_blocks(value[0], seq, value[1], steps),
            head_blocks(d_out, count, 0, steps),
        ],
        [
            result(
                (rows * height, MODEL_WIDTH),
                jnp.bfloat16,
                (height, MODEL_WIDTH // steps),
                lambda r, h, *_: (r, h),
            )
            for height in heights
        ],
        scalars=(lengths,),
        flops=10 * rows * count * seq * MODEL_WIDTH,
    )


def gelu_parts(value):
    root, bend = 0.7978845608028654, 0.044715
    square = value * value
    turned = jnp.tanh(value * (root + root * bend * square))
    half = 0.5 + 0.5 * turned
    steep = (1.0 - turned * turned) * (0.5 * root + 1.5 * root * bend * square)
    return value * half, half + value * steep


def middle_into(x2, uo, x, o, w_o, c_o, d_o, u_o):
    uo[...] = low(product_right_transposed(o[...], d_o[...]))
    x2[...] = x[...] + (
        product_plain(o[...], w_o[...]) + c_o[...] + adapter(uo[...], u_o[...])
    )


FIRST_FEED = 4 * MODEL_WIDTH // BLOCK
FEED_STEPS = HIDDEN_UNITS // BLOCK
PIECES = 8
CHUNK = BLOCK // PIECES


def chunk_place(unit):
    part, rest = unit // (CHUNK * FEED_STEPS), unit % (CHUNK * FEED_STEPS)
    return pl.ds(pl.multiple_of(rest // CHUNK * BLOCK + part * CHUNK, CHUNK), CHUNK)


def chunked(part):
    return jnp.concatenate(jnp.split(part, FEED_STEPS), axis=1)


def feed_step(j):
    return jnp.minimum(j, FEED_STEPS - 1)


def late_step(j):
    return jnp.maximum(j - FEED_STEPS, 0)


def feed_in_kernel(unit, unit_fc, *refs):
    pieces, pieces_fc, refs = taken(refs, unit, unit_fc)
    x, o, c_o, d_o, u_o, gain, shift, c_fc, d_fc, u_fc = refs[:10]
    x2, uo, m, um, act, slope, weight_o, sems_o, slots, sems, pre, plain = refs[10:]
    first = moves(unit, pieces, weight_o, sems_o, 3, BLOCK)
    pl.when(pl.program_id(0) == 0)(lambda: begin(first))
    weight = next_strip(unit_fc, pieces_fc, slots, sems, BLOCK)

    @pl.when(pl.program_id(0) == 0)
    def _():
        finish(first)
        middle_into(x2, uo, x, o, weight_o, c_o, d_o, u_o)
        norm_into(m, x2, gain[...], shift[...])
        um[...] = low(product_right_transposed(m[...], d_fc[...]))

    pre[...] = product_plain(m[...], weight[...]) + c_fc[...] + adapter(um[...], u_fc[...])
    j = pl.program_id(0)

    def part(rows):
        first, second = gelu_parts(pre[rows, :])
        slope[rows, :] = low(second)
        plain[rows, :] = low(first)

    over_rows(pre.shape[0], 64, part)
    for start in range(0, BLOCK, CHUNK):
        act[:, chunk_place(j * BLOCK + start)] = plain[:, start : start + CHUNK]


def feed_in(x, o, unit, unit_fc, p, layer):
    tokens = o.shape[0]
    small, up = p["small"], p["up"]
    wide = (tokens, HIDDEN_UNITS), jnp.bfloat16, (tokens, BLOCK), lambda j: (0, j)
    return launch(
        partial(feed_in_kernel, unit, unit_fc),
        (FEED_STEPS,),
        unit.operands()
        + unit_fc.operands()
        + [
            some_rows(x, tokens),
            whole(o),
            strip(small, BLOCK, 3, layer),
            whole(p["down_t"], layer, 1),
            strip(up, BLOCK, 3, layer),
            strip(small, BLOCK, 11, layer),
            strip(small, BLOCK, 12, layer),
            strip(small, BLOCK, lambda j: FIRST_FEED + j, layer),
            whole(p["down_t"], layer, 2),
            strip(up, BLOCK, lambda j: FIRST_FEED + j, layer),
        ],
        [
            result((tokens, MODEL_WIDTH), jnp.float32),
            result((tokens, LANES), jnp.bfloat16),
            result((tokens, MODEL_WIDTH), jnp.bfloat16),
            result((tokens, LANES), jnp.bfloat16),
            result((tokens, HIDDEN_UNITS), jnp.bfloat16),
            result(*wide),
        ],
        scratch=one_slot_for(unit)
        + slots_for(unit_fc, MODEL_WIDTH, BLOCK)
        + [pltpu.VMEM((tokens, BLOCK), jnp.float32), pltpu.VMEM((tokens, BLOCK), jnp.bfloat16)],
        flops=2 * tokens * MODEL_WIDTH * (MODEL_WIDTH + HIDDEN_UNITS),
    )


def feed_out_kernel(unit_fp, *refs):
    pieces_fp, refs = taken(refs, unit_fp)
    x2, act, d_fp, c_fp, u_fp, final, x3, ug, h, slots, sems = refs
    j = pl.program_id(0)
    weight = next_strip(unit_fp, pieces_fp, slots, sems, BLOCK)

    @pl.when(j == 0)
    def _():
        ug[...] = jnp.zeros_like(ug)
        x3[...] = x2[...] + c_fp[...]

    columns = pl.ds(pl.multiple_of(j * BLOCK, BLOCK), BLOCK)
    taken_act = act[:, columns]
    x3[...] += product_plain(taken_act, weight[...])
    maps = [
        d_fp[:, pl.ds(pl.multiple_of((n * FEED_STEPS + j) * CHUNK, CHUNK), CHUNK)]
        for n in range(PIECES)
    ]
    ug[...] += product_right_transposed(taken_act, jnp.concatenate(maps, axis=1))

    @pl.when(j == pl.num_programs(0) - 1)
    def _():
        x3[...] += adapter(low(ug[...]), u_fp[...])
        gains = final[...].astype(jnp.float32)
        if h.shape == x3.shape:
            norm_into(h, x3, gains[0:1], gains[1:2])


def feed_out(x2, act, unit_fp, final, p, layer, with_norm):
    tokens = x2.shape[0]
    return launch(
        partial(feed_out_kernel, unit_fp),
        (FEED_STEPS,),
        unit_fp.operands()
        + [
            whole(x2),
            whole(act),
            whole(p["feed_t"], layer),
            strip(p["small"], BLOCK, 8, layer),
            strip(p["up"], BLOCK, 8, layer),
            whole(final),
        ],
        [
            result((tokens, MODEL_WIDTH), jnp.float32),
            result((tokens, LANES), jnp.float32),
            result((tokens if with_norm else 16, MODEL_WIDTH), jnp.bfloat16),
        ],
        scratch=slots_for(unit_fp, BLOCK, MODEL_WIDTH),
        flops=2 * tokens * MODEL_WIDTH * HIDDEN_UNITS,
    )


def three_parts(value):
    first = low(value)
    rest = value - first.astype(jnp.float32)
    second = low(rest)
    return [first, second, low(rest - second.astype(jnp.float32))]


def head_kernel(h, table, out, logits, total, top, bulk):
    j = pl.program_id(0)

    @pl.when(j == 0)
    def _():
        top[...] = jnp.full_like(top, NEGATIVE)
        bulk[...] = jnp.zeros_like(bulk)
        total[...] = jnp.zeros_like(total)

    def part(rows):
        logits[...] = product_right_transposed(h[rows, :], table[...])
        before = top[rows, :]
        now = jnp.maximum(before, jnp.max(logits[...], axis=1, keepdims=True))
        fade = jnp.exp(before - now)
        top[rows, :] = now
        weight = jnp.exp(logits[...] - now)
        bulk[rows, :] = bulk[rows, :] * fade + jnp.sum(weight, axis=1, keepdims=True)
        total[rows, :] = total[rows, :] * fade + product_plain(low(weight), table[...])

    over_rows(h.shape[0], logits.shape[0], part)

    @pl.when(j == pl.num_programs(0) - 1)
    def _():
        out[:, :MODEL_WIDTH] = low(total[...])
        columns = three_parts(top[...]) + three_parts(bulk[...])
        rest = jnp.zeros((h.shape[0], 128 - len(columns)), jnp.bfloat16)
        out[:, MODEL_WIDTH:] = jnp.concatenate(columns + [rest], axis=1)


def head(h, table):
    tokens, vocab = h.shape[0], table.shape[0]
    steps = 3 if vocab % 48 == 0 else 1
    tile = vocab // steps
    chunk = min(512, tokens)
    (out,) = launch(
        head_kernel,
        (steps,),
        [whole(h), rows_strip(table, tile, lambda j: j)],
        [result((tokens, MODEL_WIDTH + 128), jnp.bfloat16)],
        scratch=[
            pltpu.VMEM((chunk, tile), jnp.float32),
            pltpu.VMEM((tokens, MODEL_WIDTH), jnp.float32),
            pltpu.VMEM((tokens, 1), jnp.float32),
            pltpu.VMEM((tokens, 1), jnp.float32),
        ],
        flops=4 * tokens * vocab * MODEL_WIDTH,
    )
    return out


def head_back_kernel(parts, targets, h, x3, final, mask, terms, d_x3, d_hidden):
    tails = [
        parts[n, :, MODEL_WIDTH:].astype(jnp.float32) for n in range(parts.shape[0])
    ]
    tops = [tail[:, 0:1] + tail[:, 1:2] + tail[:, 2:3] for tail in tails]
    sums = [tail[:, 3:4] + tail[:, 4:5] + tail[:, 5:6] for tail in tails]
    top = tops[0]
    for other in tops[1:]:
        top = jnp.maximum(top, other)
    whole_sum = sum(s * jnp.exp(t - top) for t, s in zip(tops, sums))
    lse = top + jnp.log(whole_sum)
    wanted = targets[...]
    logit = jnp.sum(h[...].astype(jnp.float32) * wanted, axis=1, keepdims=True)
    terms[...] = (lse - logit) * mask[...]
    gathered = -wanted
    for n, t in enumerate(tops):
        gathered = gathered + parts[n, :, :MODEL_WIDTH].astype(jnp.float32) * jnp.exp(t - lse)
    d_hidden[...] = gathered * mask[...]
    norm_back_into(d_x3, d_hidden, x3, final[...].astype(jnp.float32)[0:1])


def head_back(parts, targets, h, x3, final, mask):
    count = h.shape[0]
    return launch(
        head_back_kernel,
        (1,),
        [whole(parts), some_rows(targets, count, targets.shape[0] // count - 1), whole(h), whole(x3), whole(final), whole(mask)],
        [
            result((count, 1), jnp.float32),
            result((count, MODEL_WIDTH), jnp.float32),
        ],
        scratch=[pltpu.VMEM((count, MODEL_WIDTH), jnp.float32)],
    )


def output_back(d_heads, grad_uo, grad_do, d_x2, o, uo, w_o, u_o, d_o):
    d_low = low(d_x2[...])
    grad_uo[...] = ADAPTER_SCALE * product_left_transposed(uo[...], d_low)
    duo = low(ADAPTER_SCALE * product_right_transposed(d_low, u_o[...]))
    grad_do[...] = product_left_transposed(duo, o[...])
    d_heads[...] = low(
        product_right_transposed(d_low, w_o[...]) + product_plain(duo, d_o[...])
    )


def front_last_back_kernel(unit, index, *refs):
    pieces, refs = taken(refs, unit)
    d_query, d_key, d_value, a, a_sel, ua, ua_sel, up, down, d_x2, x, gain = refs[:12]
    d_x, grad_up, grad_down, rows, rows_sel, inner, inner_sel, slots, sems = refs[12:]
    j = pl.program_id(0)
    weight = next_strip(unit, pieces, slots, sems, BLOCK)

    @pl.when(j == 0)
    def _():
        rows[...] = jnp.zeros_like(rows)
        inner[...] = jnp.zeros_like(inner)

    @pl.when(j == 0)
    def _():
        gradient = d_query[...]
        grad_up[...] = ADAPTER_SCALE * product_left_transposed(ua_sel[...], gradient)
        inner_sel[...] = ADAPTER_SCALE * product_right_transposed(gradient, up[...])
        rows_sel[...] = product_right_transposed(gradient, weight[...])

    def step(ref):
        gradient = ref[...]
        grad_up[...] = ADAPTER_SCALE * product_left_transposed(ua[...], gradient)
        inner[...] += ADAPTER_SCALE * product_right_transposed(gradient, up[...])
        rows[...] += product_right_transposed(gradient, weight[...])

    pl.when(j == 1)(lambda: step(d_key))
    pl.when(j == 2)(lambda: step(d_value))

    @pl.when(j == pl.num_programs(0) - 1)
    def _():
        last, last_sel = low(inner[...]), low(inner_sel[...])
        grad_down[...] = product_left_transposed(last, a[...]) + product_left_transposed(
            last_sel, a_sel[...]
        )
        rows[...] += product_plain(last, down[...])
        rows_sel[...] += product_plain(last_sel, down[...])
        add_rows(index, rows_sel, rows)
        norm_back_into(d_x, rows, x, gain[...])
        add_rows(index, d_x2, d_x)


def front_last_back(index, d_query, d_key, d_value, saved, d_x2, x, unit, p, layer):
    a, a_sel, ua, ua_sel = saved
    tokens, count = x.shape[0], index.shape[0]
    return launch(
        partial(front_last_back_kernel, unit),
        (3,),
        unit.operands()
        + [
            whole(d_query),
            whole(d_key),
            whole(d_value),
            whole(a),
            whole(a_sel),
            whole(ua),
            whole(ua_sel),
            strip(p["up"], BLOCK, lambda j: j, layer),
            whole(p["down_t"], layer, 0),
            whole(d_x2),
            whole(x),
            strip(p["small"], BLOCK, 9, layer),
        ],
        [
            result((tokens, MODEL_WIDTH), jnp.float32),
            result((LANES, 3 * MODEL_WIDTH), jnp.float32, (LANES, BLOCK), lambda j, *_: (0, j)),
            result((LANES, MODEL_WIDTH), jnp.float32),
        ],
        scratch=[
            pltpu.VMEM((tokens, MODEL_WIDTH), jnp.float32),
            pltpu.VMEM((count, MODEL_WIDTH), jnp.float32),
            pltpu.VMEM((tokens, LANES), jnp.float32),
            pltpu.VMEM((count, LANES), jnp.float32),
        ]
        + slots_for(unit, MODEL_WIDTH, BLOCK),
        scalars=(index,),
        flops=4 * tokens * MODEL_WIDTH**2,
    )


def feed_back_kernel(unit, unit_fc, unit_fp, *refs):
    pieces, pieces_fc, pieces_fp, refs = taken(refs, unit, unit_fc, unit_fp)
    d_x3, x2, m, um, ug, uo, o, act, slope, d_fp, u_fc, u_fp, d_fc, gain, u_o, d_o = refs[:16]
    d_x2, d_heads, grad_ufp, grad_dfp, grad_ufc, grad_dfc, grad_uo, grad_do = refs[16:24]
    d_out, dug, d_pre, inner, d_feed, weight_o, sems_o, slots, sems = refs[24:]
    j = pl.program_id(0)
    last = pl.num_programs(0) - 1
    out_moves = moves(unit, pieces, weight_o, sems_o, 3, BLOCK)

    def each(step, act):
        slot = lax.rem(step, 2)
        for some, refs, first in ((unit_fp, pieces_fp, 0), (unit_fc, pieces_fc, FEED_STEPS)):

            @pl.when((step >= first) & (step < first + FEED_STEPS))
            def _(some=some, refs=refs, first=first):
                column = jnp.clip(step - first, 0, FEED_STEPS - 1)
                act(moves(some, refs, slots.at[slot], sems.at[slot], column, BLOCK))

    pl.when(j == 0)(lambda: each(j, begin))
    pl.when(j < last)(lambda: each(j + 1, begin))
    pl.when(j == last)(lambda: begin(out_moves))

    @pl.when(j == 0)
    def _():
        d_out[...] = low(d_x3[...])
        dug[...] = low(ADAPTER_SCALE * product_right_transposed(d_out[...], u_fp[...]))
        grad_ufp[...] = ADAPTER_SCALE * product_left_transposed(low(ug[...]), d_out[...])
        inner[...] = jnp.zeros_like(inner)
        d_feed[...] = jnp.zeros_like(d_feed)

    each(j, finish)
    weight = slots.at[lax.rem(j, 2)]

    @pl.when(j < FEED_STEPS)
    def _():
        d_act = product_right_transposed(d_out[...], weight[...])
        from_act = product_left_transposed(dug[...], act[...])
        for n in range(PIECES):
            place = pl.ds(pl.multiple_of((n * FEED_STEPS + j) * CHUNK, CHUNK), CHUNK)
            part = slice(n * CHUNK, (n + 1) * CHUNK)
            value = d_act[:, part] + product_plain(dug[...], d_fp[:, place])
            d_pre[:, place] = low(value * slope[:, place].astype(jnp.float32))
            grad_dfp[:, place] = from_act[:, part]

    @pl.when(j >= FEED_STEPS)
    def _():
        columns = pl.ds(pl.multiple_of((j - FEED_STEPS) * BLOCK, BLOCK), BLOCK)
        gradient = d_pre[:, columns]
        grad_ufc[...] = ADAPTER_SCALE * product_left_transposed(um[...], gradient)
        inner[...] += ADAPTER_SCALE * product_right_transposed(gradient, u_fc[...])
        d_feed[...] += product_right_transposed(gradient, weight[...])

    @pl.when(j == last)
    def _():
        dum = low(inner[...])
        grad_dfc[...] = product_left_transposed(dum, m[...])
        d_feed[...] += product_plain(dum, d_fc[...])
        norm_back_into(d_x2, d_feed, x2, gain[...], d_x3)
        finish(out_moves)
        output_back(d_heads, grad_uo, grad_do, d_x2, o, uo, weight_o, u_o, d_o)


def feed_back(d_x3, saved, unit, unit_fc, unit_fp, p, layer):
    x2, m, um, ug, uo, o, act, slope = saved
    tokens = x2.shape[0]
    square = (LANES, MODEL_WIDTH), jnp.float32
    return launch(
        partial(feed_back_kernel, unit, unit_fc, unit_fp),
        (2 * FEED_STEPS,),
        unit.operands()
        + unit_fc.operands()
        + unit_fp.operands()
        + [
            whole(d_x3),
            whole(x2),
            whole(m),
            whole(um),
            whole(ug),
            whole(uo),
            whole(o),
            strip(act, BLOCK, feed_step),
            whole(slope),
            whole(p["feed_t"], layer),
            strip(p["up"], BLOCK, lambda j: FIRST_FEED + late_step(j), layer),
            strip(p["up"], BLOCK, 8, layer),
            whole(p["down_t"], layer, 2),
            strip(p["small"], BLOCK, 11, layer),
            strip(p["up"], BLOCK, 3, layer),
            whole(p["down_t"], layer, 1),
        ],
        [
            result((tokens, MODEL_WIDTH), jnp.float32),
            result((tokens, MODEL_WIDTH), jnp.bfloat16),
            result(*square),
            result((LANES, HIDDEN_UNITS), jnp.float32),
            result(
                (LANES, HIDDEN_UNITS), jnp.float32, (LANES, BLOCK), lambda j: (0, late_step(j))
            ),
            result(*square),
            result(*square),
            result(*square),
        ],
        scratch=[
            pltpu.VMEM((tokens, MODEL_WIDTH), jnp.bfloat16),
            pltpu.VMEM((tokens, LANES), jnp.bfloat16),
            pltpu.VMEM((tokens, HIDDEN_UNITS), jnp.bfloat16),
            pltpu.VMEM((tokens, LANES), jnp.float32),
            pltpu.VMEM((tokens, MODEL_WIDTH), jnp.float32),
        ]
        + one_slot_for(unit)
        + slots_for(unit_fc, MODEL_WIDTH, BLOCK),
        flops=2 * tokens * MODEL_WIDTH * (MODEL_WIDTH + 2 * HIDDEN_UNITS),
    )


def front_back_kernel(d_query, d_key, d_value, a, ua, up, grad_up, grad_down):
    inner = 0.0
    for n, ref in enumerate((d_query, d_key, d_value)):
        columns = slice(n * MODEL_WIDTH, (n + 1) * MODEL_WIDTH)
        grad_up[:, columns] = ADAPTER_SCALE * product_left_transposed(ua[...], ref[...])
        inner = inner + ADAPTER_SCALE * product_right_transposed(ref[...], up[:, columns])
    grad_down[...] = product_left_transposed(low(inner), a[...])


def front_back(d_query, d_key, d_value, a, ua, p, layer):
    return launch(
        front_back_kernel,
        (1,),
        [
            whole(d_query),
            whole(d_key),
            whole(d_value),
            whole(a),
            whole(ua),
            strip(p["up"], 3 * MODEL_WIDTH, 0, layer),
        ],
        [
            result((LANES, 3 * MODEL_WIDTH), jnp.float32),
            result((LANES, MODEL_WIDTH), jnp.float32),
        ],
    )


def pack_kernel(columns, *refs):
    extras, parts, out = refs[0], refs[1:-1], refs[-1]
    shards, width = out.shape[0], out.shape[2] - 128
    three = [part.astype(jnp.float32) for part in three_parts(extras[...])]
    rest = jnp.zeros((out.shape[1] - len(three), 128), jnp.float32)
    for n in range(shards):
        out[n, :, width:] = low(jnp.concatenate(three + [rest], axis=0))
    layers = {}
    for part, (row, start) in zip(parts, columns):
        layers.setdefault(start, []).append(part)
    for start, refs in layers.items():
        values = low(jnp.concatenate([ref[0:ADAPTER_RANK, :] for ref in refs], axis=0))
        size = values.shape[1]
        done = 0
        while done < size:
            block, offset = divmod(start + done, width)
            step = min(width - offset, size - done)
            out[block, :, offset : offset + step] = values[:, done : done + step]
            done += step


def packed(by_layer, extras):
    shards = lax.axis_size("fsdp")
    columns, parts = [], []
    for layer, row in enumerate(by_layer):
        start = 0
        for part in row:
            parts.append(part)
            columns.append((layer * ADAPTER_RANK, start))
            start += part.shape[1]
    shape = (shards, len(by_layer) * ADAPTER_RANK, start // shards + 128)
    (out,) = launch(
        partial(pack_kernel, tuple(columns)),
        (1,),
        [whole(extras)] + [whole(part) for part in parts],
        [result(shape, jnp.bfloat16)],
    )
    return out


def asking(table, ids, needed):
    shards = lax.axis_size("fsdp")
    total = ids.shape[0]
    order = jnp.arange(total, dtype=jnp.int32)
    owner = ids // table.shape[0]
    local = ids - owner * table.shape[0]
    same = (ids[:, None] == ids[None, :]) & needed[None, :]
    first = jnp.min(jnp.where(same, order[None, :], total), axis=1)
    leads = needed & (first == order)
    rank = jnp.sum(
        (leads & (owner[:, None] == owner[None, :]) & (order[None, :] < first[:, None])).astype(
            jnp.int32
        ),
        axis=1,
    )
    rounds = (jnp.max(jnp.where(needed, rank, 0)) + CAPACITY) // CAPACITY

    spots = jnp.arange(shards * CAPACITY, dtype=jnp.int32)

    def place_of(turn):
        return jnp.where(
            needed & (rank // CAPACITY == turn), owner * CAPACITY + rank % CAPACITY, -1
        )

    def ask(turn):
        place = place_of(turn)
        asked = jnp.sum(
            jnp.where(leads[:, None] & (place[:, None] == spots[None, :]), local[:, None], 0), axis=0
        )
        return asked.reshape(shards, CAPACITY)

    def sent_for(asked):
        return table.at[asked.reshape(-1)].get(mode="promise_in_bounds")

    def exchanged(part):
        return lax.all_to_all(part, "fsdp", 0, 0, tiled=True)

    def found(turn, back):
        pick = (place_of(turn)[:, None] == spots[None, :]).astype(jnp.bfloat16)
        return product_plain(pick, back)

    def with_rounds(most, added):
        def more(so_far):
            return lax.fori_loop(
                1,
                most,
                lambda turn, total: total
                + found(turn, exchanged(sent_for(exchanged(ask(turn))))),
                so_far,
            )

        return lax.cond(most > 1, more, lambda so_far: so_far, added)

    return ask, rounds, exchanged, sent_for, found, with_rounds


def as_low(numbers):
    return low(numbers // 256), low(numbers % 256)


def as_numbers(high, rest):
    return high.astype(jnp.int32) * 256 + rest.astype(jnp.int32)


def swap(part, bit):
    return lax.ppermute(part, "fsdp", [(i, i ^ bit) for i in range(lax.axis_size("fsdp"))])


def tie(parts, before):
    parts, _ = lax.optimization_barrier((parts, before))
    return parts


def hop(part):
    return lax.ppermute(
        part, "fsdp", [(i, i ^ (4 if i % 2 else 2)) for i in range(lax.axis_size("fsdp"))]
    )


class Gathering:
    PLACES = (0, 0), (1, 1), (2, 4), (3, 5), (5, 3), (4, 2), (7, 7), (6, 6)

    def __init__(self, shard, in_chunks=False):
        self.shard, self.in_chunks = shard, in_chunks
        self.direct = lax.axis_size("fsdp") == PIECES

    def begin(self, before=()):
        if self.direct:
            own = chunked(self.shard) if self.in_chunks else self.shard
            own = tie(own, before)
            other = swap(own, 1)
            self.arrays = own, other, hop(own), hop(other)

    def after_first(self, value):
        return tie(value, self.arrays[1]) if self.direct else value

    def after_last(self, value):
        return tie(value, self.arrays[4]) if self.direct else value

    def pass_on(self, value):
        if self.direct:
            own, other, first, second = self.arrays
            first, value = lax.optimization_barrier((first, value))
            handed = swap(first, 1)
            self.arrays = own, other, first, second, handed, swap(second, 1), hop(handed)
        return value

    def settle(self, value):
        if not self.direct:
            parts = jnp.split(lax.all_gather(self.shard, "fsdp", axis=0, tiled=True), PIECES)
            parts = [chunked(part) for part in parts] if self.in_chunks else parts
            return value, Unit(tuple(range(PIECES)), tuple(parts), parts[0].shape[0])
        far, value = lax.optimization_barrier((self.arrays[-1], value))
        arrays = self.arrays[:-1] + (far, swap(far, 1))
        return value, Unit(self.PLACES, arrays, arrays[0].shape[0])


def everywhere(part):
    shards = lax.axis_size("fsdp")
    return lax.all_to_all(
        jnp.tile(part, (shards,) + (1,) * (part.ndim - 1)), "fsdp", 0, 0, tiled=True
    )


def owned_parts(parts):
    shards = lax.axis_size("fsdp")
    rows = parts.shape[0] // shards
    return lax.all_to_all(parts, "fsdp", 0, 0, tiled=True).reshape(
        (shards, rows) + parts.shape[1:]
    )


def summed_everywhere(blocks):
    shards, rows, columns = blocks.shape
    groups = lax.axis_size("dp")
    width = columns - 128
    parts = owned_parts(blocks.reshape(shards * rows, columns)).astype(jnp.float32)
    block = jnp.sum(parts, axis=0)
    others = [
        lax.ppermute(block, "dp", [(i, (i + k) % groups) for i in range(groups)])
        for k in range(1, groups)
    ]
    stacked = jnp.stack([block] + others)
    order = (lax.axis_index("dp") - jnp.arange(groups)) % groups
    ranks = (order[None, :] == jnp.arange(groups)[:, None])[:, :, None, None]
    total = jnp.sum(jnp.sum(jnp.where(ranks, stacked[None], 0.0), axis=1), axis=0)
    gathered = everywhere(low(total[:, :width])).reshape(shards, rows, width)
    sums = total[:3, width : width + 2]
    return (
        gathered.astype(jnp.float32).transpose(1, 0, 2).reshape(rows, shards * width),
        sums[0] + sums[1] + sums[2],
    )


def body(
    input_token_ids,
    lengths,
    scored_slots,
    scored_targets,
    wte,
    wpe,
    frozen_attention,
    frozen_feed_input,
    frozen_feed_output,
    frozen_bias_gain,
    final_norm_params,
    adapter_down,
    adapter_down_feed,
    adapter_up,
    first_moment_down,
    first_moment_feed,
    first_moment_up,
    second_moment_down,
    second_moment_feed,
    second_moment_up,
    optimizer_step,
):
    micro, seqs, seq = input_token_ids.shape
    rows = micro * seqs
    picks = scored_slots.shape[2]
    layers = frozen_attention.shape[0]
    shards = lax.axis_size("fsdp")
    row_lengths = lengths.reshape(rows)
    slots = scored_slots.reshape(rows, picks)
    valid = slots < row_lengths[:, None]
    mask = valid.reshape(-1, 1).astype(jnp.float32)
    all_slots = jnp.tile(jnp.arange(seq, dtype=jnp.int32)[None], (rows, 1))

    useful = jnp.max(jnp.where(valid, slots, -1), axis=1)
    needed = jnp.concatenate([(all_slots <= useful[:, None]).reshape(-1), valid.reshape(-1)])
    ids = jnp.concatenate([input_token_ids.reshape(-1), scored_targets.reshape(-1)])
    attention_one, attention_two = Gathering(frozen_attention[0]), Gathering(frozen_attention[1])
    feed_in_one, feed_in_two = Gathering(frozen_feed_input[0]), Gathering(frozen_feed_input[1])
    feed_out_one = Gathering(frozen_feed_output[0], in_chunks=True)
    feed_out_two = Gathering(frozen_feed_output[1], in_chunks=True)
    attention_one.begin()
    ask, rounds, exchanged, sent_for, found, with_rounds = asking(wte, ids, needed)
    count = CAPACITY
    requests = as_low(jnp.concatenate([ask(0), jnp.full((shards, 1), rounds, jnp.int32)], 1))
    biases = jnp.tile(frozen_bias_gain.reshape(1, -1), (shards, 1))
    message = jnp.concatenate([*requests, biases], 1)
    got = exchanged(attention_one.after_first(message))
    got = attention_one.pass_on(got)
    feed_in_one.begin(got)
    numbers = as_numbers(got[:, : count + 1], got[:, count + 1 : 2 * count + 2])
    small = (
        got[:, 2 * count + 2 :].reshape(shards, layers, -1).transpose(1, 0, 2).reshape(layers, 1, -1)
    )
    sent = sent_for(attention_one.after_last(numbers[:, :count]))
    most = jnp.max(numbers[:, count])
    extra = LANES - ADAPTER_RANK
    down_t = adapter_down.reshape(layers, MODEL_WIDTH, 3, ADAPTER_RANK).transpose(0, 2, 3, 1)
    p = {
        "small": small.astype(jnp.float32),
        "down_t": low(jnp.pad(down_t, ((0, 0), (0, 0), (0, extra), (0, 0)))),
        "feed_t": low(jnp.pad(adapter_down_feed.transpose(0, 2, 1), ((0, 0), (0, extra), (0, 0)))),
        "up": low(jnp.pad(adapter_up, ((0, 0), (0, extra), (0, 0)))),
    }
    places = jnp.concatenate([wpe.astype(jnp.float32)] * rows)
    places = jnp.pad(places, ((0, rows * picks), (0, 0)))
    places = with_rounds(most, places)
    back, p, places = lax.optimization_barrier((exchanged(sent), p, places))
    back, attention_one = attention_one.settle(back)
    back = feed_in_one.pass_on(back)
    feed_out_one.begin(back)
    x0 = found(0, back) + places
    index = (slots + seq * jnp.arange(rows, dtype=jnp.int32)[:, None]).reshape(-1)

    qkv, a_one, ua_one = front(x0, rows * seq, attention_one, p, 0)
    qkv = feed_out_one.pass_on(qkv)
    attention_two.begin(qkv)
    split_qkv = (qkv, 0), (qkv, 1), (qkv, 2)
    o_one = attend(row_lengths, all_slots, *split_qkv)
    o_one, feed_in_one = feed_in_one.settle(o_one)
    o_one = attention_two.pass_on(o_one)
    feed_in_two.begin(o_one)
    x2_one, uo_one, m_one, um_one, act_one, slope_one = feed_in(
        x0, o_one, attention_one, feed_in_one, p, 0
    )
    act_one, feed_out_one = feed_out_one.settle(act_one)
    act_one = feed_in_two.pass_on(act_one)
    feed_out_two.begin(act_one)
    x1, ug_one, _ = feed_out(x2_one, act_one, feed_out_one, final_norm_params, p, 0, False)
    x1, attention_two = attention_two.settle(x1)
    x1 = feed_out_two.pass_on(x1)

    query, kv, a_two, a_sel, ua_two, ua_sel, x_sel = front_last(index, x1, attention_two, p, 1)
    query, feed_in_two = feed_in_two.settle(query)
    parts_two = (query, 0), (kv, 0), (kv, 1)
    o_two = attend(row_lengths, slots, *parts_two)
    x2_two, uo_two, m_two, um_two, act_two, slope_two = feed_in(
        x_sel, o_two, attention_two, feed_in_two, p, 1
    )
    act_two, feed_out_two = feed_out_two.settle(act_two)
    x3, ug_two, h = feed_out(x2_two, act_two, feed_out_two, final_norm_params, p, 1, True)

    weighed = owned_parts(head(everywhere(h), wte))
    terms, d_x3 = head_back(weighed, x0, h, x3, final_norm_params, mask)

    d_x2, d_heads, grad_ufp, grad_dfp, grad_ufc, grad_dfc, grad_uo, grad_do = feed_back(
        d_x3,
        (x2_two, m_two, um_two, ug_two, uo_two, o_two, act_two, slope_two),
        attention_two,
        feed_in_two,
        feed_out_two,
        p,
        1,
    )
    d_parts = attend_back(row_lengths, slots, *parts_two, d_heads)
    d_x1, grad_uqkv, grad_dqkv = front_last_back(
        index, *d_parts, (a_two, a_sel, ua_two, ua_sel), d_x2, x1, attention_two, p, 1
    )
    grads_two = [
        grad_dqkv, grad_do, grad_dfc, grad_dfp, grad_uqkv, grad_uo, grad_ufc, grad_ufp
    ]

    _, d_heads, grad_ufp, grad_dfp, grad_ufc, grad_dfc, grad_uo, grad_do = feed_back(
        d_x1,
        (x2_one, m_one, um_one, ug_one, uo_one, o_one, act_one, slope_one),
        attention_one,
        feed_in_one,
        feed_out_one,
        p,
        0,
    )
    d_parts = attend_back(row_lengths, all_slots, *split_qkv, d_heads)
    grad_uqkv, grad_dqkv = front_back(*d_parts, a_one, ua_one, p, 0)
    grads_one = [
        grad_dqkv, grad_do, grad_dfc, grad_dfp, grad_uqkv, grad_uo, grad_ufc, grad_ufp
    ]

    tail = jnp.pad(jnp.stack([jnp.sum(terms), jnp.sum(mask)])[None], ((0, 0), (0, 126)))
    gradients, totals = summed_everywhere(packed((grads_one, grads_two), tail))
    loss_total, count = totals[0], totals[1]
    gradients = gradients / count
    norm = jnp.sqrt(jnp.sum(gradients * gradients))
    by_layer = gradients.reshape(layers, ADAPTER_RANK, -1)
    gradient_tree = [
        by_layer[:, :, : 3 * MODEL_WIDTH]
        .reshape(layers, ADAPTER_RANK, 3, MODEL_WIDTH)
        .transpose(0, 3, 2, 1)
        .reshape(layers, MODEL_WIDTH, 3 * ADAPTER_RANK),
        by_layer[:, :, 3 * MODEL_WIDTH : 3 * MODEL_WIDTH + HIDDEN_UNITS].transpose(0, 2, 1),
        by_layer[:, :, 3 * MODEL_WIDTH + HIDDEN_UNITS :],
    ]
    scale_factor = jnp.minimum(1.0, CLIP / (norm + 1e-06))
    step_number = optimizer_step[0].astype(jnp.float32)
    updated = [
        moment_update(weight, first, second, gradient_value, scale_factor, step_number)
        for weight, first, second, gradient_value in zip(
            (adapter_down, adapter_down_feed, adapter_up),
            (first_moment_down, first_moment_feed, first_moment_up),
            (second_moment_down, second_moment_feed, second_moment_up),
            gradient_tree,
        )
    ]
    return (
        loss_total / count,
        norm,
        *(part[0] for part in updated),
        *(part[1] for part in updated),
        *(part[2] for part in updated),
        terms.reshape(micro, seqs, picks),
    )


def solution(mesh):
    in_specs = (
        P(None, ("dp", "fsdp"), None),
        P(None, ("dp", "fsdp")),
        P(None, ("dp", "fsdp"), None),
        P(None, ("dp", "fsdp"), None),
        P("fsdp", None),
        P(),
        P(None, "fsdp", None),
        P(None, "fsdp", None),
        P(None, "fsdp", None),
        P(None, "fsdp"),
        P(),
        P(),
        P(),
        P(),
        P(),
        P(),
        P(),
        P(),
        P(),
        P(),
        P(),
    )
    out_specs = (
        P(),
        P(),
        P(),
        P(),
        P(),
        P(),
        P(),
        P(),
        P(),
        P(),
        P(),
        P(None, ("dp", "fsdp"), None),
    )
    return jax.shard_map(body, mesh=mesh, in_specs=in_specs, out_specs=out_specs, check_vma=False)
```

```python
import math
from functools import partial
from typing import NamedTuple

import jax
import jax.numpy as jnp
from jax import lax
from jax.experimental import pallas as pl
from jax.experimental.pallas import tpu as pltpu
from jax.sharding import PartitionSpec as P

MODEL_WIDTH = 1024
H = 16
HD = 64
HIDDEN_UNITS = 4096
ADAPTER_RANK = 4


ADAPTER_SCALE = 8.0
EPS_NORM = 1e-05
BETA_ONE = 0.9
BETA_TWO = 0.999
RATE = 0.02
DECAY = 0.01
EPS_ADAM = 1e-08
CLIP = 0.02
NEGATIVE = -1e30


def product_plain(left, right):
    return jnp.dot(left, right, preferred_element_type=jnp.float32)


def product_left_transposed(left, right):
    return lax.dot_general(
        left, right, (((0,), (0,)), ((), ())), preferred_element_type=jnp.float32
    )


def product_right_transposed(left, right):
    return lax.dot_general(
        left, right, (((1,), (1,)), ((), ())), preferred_element_type=jnp.float32
    )


def norm_fwd(hidden_rows, norm_gain, norm_shift):
    row_mean = jnp.mean(hidden_rows, axis=-1, keepdims=True)
    centered = hidden_rows - row_mean
    inverse_deviation = lax.rsqrt(jnp.mean(centered * centered, axis=-1, keepdims=True) + EPS_NORM)
    normalized_rows = centered * inverse_deviation
    return (normalized_rows * norm_gain + norm_shift, normalized_rows, inverse_deviation)


def norm_backward(gradient_value, normalized_rows, inverse_deviation, norm_gain):
    scaled_rows = gradient_value * norm_gain
    return inverse_deviation * (
        scaled_rows
        - jnp.mean(scaled_rows, axis=-1, keepdims=True)
        - normalized_rows * jnp.mean(scaled_rows * normalized_rows, axis=-1, keepdims=True)
    )


def moment_update(weight, first, second, gradient_value, scale_factor, step_number):
    clipped = gradient_value * scale_factor
    first_new = BETA_ONE * first + (1.0 - BETA_ONE) * clipped
    second_new = BETA_TWO * second + (1.0 - BETA_TWO) * clipped * clipped
    first_hat = first_new / (1.0 - BETA_ONE**step_number)
    second_hat = second_new / (1.0 - BETA_TWO**step_number)
    weight_new = weight - RATE * (first_hat / (jnp.sqrt(second_hat) + EPS_ADAM) + DECAY * weight)
    return (weight_new, first_new, second_new)


CAPACITY = 80


LANES = 16
HALF_TILE = 512
BLOCK = 1024
VMEM_BYTES = 63 * 2**20


def whole(array, *lead):
    shape = (None,) * len(lead) + array.shape[len(lead) :]
    place = lead + (0,) * (array.ndim - len(lead))
    return array, pl.BlockSpec(shape, lambda *_: place, pipeline_mode=pl.Buffered(1))


def some_rows(array, count, row=0):
    shape = (count, array.shape[1])
    return array, pl.BlockSpec(shape, lambda *_: (row, 0), pipeline_mode=pl.Buffered(1))


def strip(array, width, column, *lead):
    shape = (None,) * len(lead) + (array.shape[-2], width)
    if callable(column):
        return array, pl.BlockSpec(shape, lambda j, *_: lead + (0, column(j)))
    place = lead + (0, column)
    return array, pl.BlockSpec(shape, lambda *_: place, pipeline_mode=pl.Buffered(1))


def rows_strip(array, height, row, *lead):
    shape = (None,) * len(lead) + (height, array.shape[-1])
    return array, pl.BlockSpec(shape, lambda j, *_: lead + (row(j), 0))


def result(shape, dtype, block=None, place=None):
    kind = jax.ShapeDtypeStruct(shape, dtype)
    if block is None:
        block, zeros = shape, (0,) * len(shape)
        return kind, pl.BlockSpec(block, lambda *_: zeros)
    return kind, pl.BlockSpec(block, place)


def launch(kernel, grid, operands, results, scratch=(), scalars=(), flops=0):
    moved = sum(a.size * a.dtype.itemsize for a, _ in operands)
    return pl.pallas_call(
        kernel,
        out_shape=[kind for kind, _ in results],
        grid_spec=pltpu.PrefetchScalarGridSpec(
            num_scalar_prefetch=len(scalars),
            grid=grid,
            in_specs=[spec for _, spec in operands],
            out_specs=[spec for _, spec in results],
            scratch_shapes=list(scratch),
        ),
        compiler_params=pltpu.CompilerParams(vmem_limit_bytes=VMEM_BYTES),
        cost_estimate=pl.CostEstimate(flops=flops, bytes_accessed=moved, transcendentals=0),
    )(*scalars, *(a for a, _ in operands))


class Unit(NamedTuple):
    places: tuple
    arrays: tuple
    rows: int

    def operands(self):
        return [(array, pl.BlockSpec(memory_space=pltpu.HBM)) for array in self.arrays]


def shard_of(place):
    if isinstance(place, int):
        return place
    me = lax.axis_index("fsdp")
    return jnp.bitwise_xor(me, jnp.where(lax.rem(me, 2) == 0, *place))


def moves(unit, refs, target, sems, column, width):
    columns = pl.ds(pl.multiple_of(column * width, width), width)
    copies = []
    for n, (place, ref) in enumerate(zip(unit.places, refs)):
        start = pl.multiple_of(shard_of(place) * unit.rows, 16)
        copies.append(
            pltpu.make_async_copy(
                ref.at[:, columns], target.at[pl.ds(start, ref.shape[0]), :], sems.at[n]
            )
        )
    return copies


def begin(copies):
    for copy in copies:
        copy.start()


def finish(copies):
    for copy in copies:
        copy.wait()


def next_strip(unit, refs, slots, sems, width):
    j = pl.program_id(0)

    def strip_moves(step):
        slot = lax.rem(step, 2)
        return moves(unit, refs, slots.at[slot], sems.at[slot], step, width)

    pl.when(j == 0)(lambda: begin(strip_moves(j)))
    pl.when(j + 1 < pl.num_programs(0))(lambda: begin(strip_moves(j + 1)))
    finish(strip_moves(j))
    return slots.at[lax.rem(j, 2)]


def slots_for(unit, height, width):
    return [
        pltpu.VMEM((2, height, width), jnp.bfloat16),
        pltpu.SemaphoreType.DMA((2, len(unit.arrays))),
    ]


def one_slot_for(unit):
    return [
        pltpu.VMEM((MODEL_WIDTH, BLOCK), jnp.bfloat16),
        pltpu.SemaphoreType.DMA((len(unit.arrays),)),
    ]


def taken(refs, *units):
    groups = []
    for unit in units:
        groups.append(refs[: len(unit.arrays)])
        refs = refs[len(unit.arrays) :]
    return groups + [refs]


def over_rows(total, size, work):
    def turn(i, carry):
        work(pl.ds(pl.multiple_of(i * size, size), size))
        return carry

    lax.fori_loop(0, total // size, turn, 0)


def low(value):
    return value.astype(jnp.bfloat16)


def adapter(inner, up):
    return ADAPTER_SCALE * product_plain(inner, up)


def norm_into(out_ref, rows_ref, gain, shift):
    def part(rows):
        out_ref[rows, :] = low(norm_fwd(rows_ref[rows, :], gain, shift)[0])

    over_rows(rows_ref.shape[0], min(64, rows_ref.shape[0]), part)


def norm_back_into(out_ref, gradient_ref, rows_ref, gain, residual_ref=None):
    def part(rows):
        _, normalized, deviation = norm_fwd(rows_ref[rows, :], gain, 0.0)
        value = norm_backward(gradient_ref[rows, :], normalized, deviation, gain)
        if residual_ref is not None:
            value = value + residual_ref[rows, :]
        out_ref[rows, :] = value

    over_rows(rows_ref.shape[0], min(64, rows_ref.shape[0]), part)


def front_kernel(unit, *refs):
    pieces, refs = taken(refs, unit)
    x, gain, shift, bias, down, up, qkv, a, ua, slots, sems = refs
    weight = next_strip(unit, pieces, slots, sems, BLOCK)

    @pl.when(pl.program_id(0) == 0)
    def _():
        norm_into(a, x, gain[...], shift[...])
        ua[...] = low(product_right_transposed(a[...], down[...]))

    qkv[...] = low(product_plain(a[...], weight[...]) + bias[...] + adapter(ua[...], up[...]))


def front(x, tokens, unit, p, layer):
    return launch(
        partial(front_kernel, unit),
        (3,),
        unit.operands()
        + [
            some_rows(x, tokens),
            strip(p["small"], BLOCK, 9, layer),
            strip(p["small"], BLOCK, 10, layer),
            strip(p["small"], BLOCK, lambda j: j, layer),
            whole(p["down_t"], layer, 0),
            strip(p["up"], BLOCK, lambda j: j, layer),
        ],
        [
            result((tokens, 3 * MODEL_WIDTH), jnp.bfloat16, (tokens, BLOCK), lambda j: (0, j)),
            result((tokens, MODEL_WIDTH), jnp.bfloat16),
            result((tokens, LANES), jnp.bfloat16),
        ],
        scratch=slots_for(unit, MODEL_WIDTH, BLOCK),
        flops=6 * tokens * MODEL_WIDTH**2,
    )


def pick_rows(index, source, target):
    def turn(i, carry):
        target[pl.ds(i, 1), :] = source[pl.ds(index[i], 1), :]
        return carry

    lax.fori_loop(0, target.shape[0], turn, 0)


def add_rows(index, source, target):
    def turn(i, carry):
        rows = pl.ds(index[i], 1)
        target[rows, :] = target[rows, :] + source[pl.ds(i, 1), :]
        return carry

    lax.fori_loop(0, source.shape[0], turn, 0)


def front_last_kernel(unit, index, *refs):
    pieces, refs = taken(refs, unit)
    x, gain, shift, bias, down, up, q, kv, a, a_sel, ua, ua_sel, x_sel, slots, sems = refs
    j = pl.program_id(0)
    weight = next_strip(unit, pieces, slots, sems, BLOCK)

    @pl.when(j == 0)
    def _():
        norm_into(a, x, gain[...], shift[...])
        ua[...] = low(product_right_transposed(a[...], down[...]))
        pick_rows(index, x, x_sel)
        norm_into(a_sel, x_sel, gain[...], shift[...])
        ua_sel[...] = low(product_right_transposed(a_sel[...], down[...]))

    @pl.when(j == 0)
    def _():
        q[...] = low(
            product_plain(a_sel[...], weight[...]) + bias[...] + adapter(ua_sel[...], up[...])
        )

    @pl.when(j > 0)
    def _():
        kv[...] = low(product_plain(a[...], weight[...]) + bias[...] + adapter(ua[...], up[...]))


def front_last(index, x, unit, p, layer):
    tokens, count = x.shape[0], index.shape[0]
    return launch(
        partial(front_last_kernel, unit),
        (3,),
        unit.operands()
        + [
            whole(x),
            strip(p["small"], BLOCK, 9, layer),
            strip(p["small"], BLOCK, 10, layer),
            strip(p["small"], BLOCK, lambda j: j, layer),
            whole(p["down_t"], layer, 0),
            strip(p["up"], BLOCK, lambda j: j, layer),
        ],
        [
            result((count, MODEL_WIDTH), jnp.bfloat16),
            result(
                (tokens, 2 * MODEL_WIDTH),
                jnp.bfloat16,
                (tokens, BLOCK),
                lambda j, *_: (0, jnp.maximum(j - 1, 0)),
            ),
            result((tokens, MODEL_WIDTH), jnp.bfloat16),
            result((count, MODEL_WIDTH), jnp.bfloat16),
            result((tokens, LANES), jnp.bfloat16),
            result((count, LANES), jnp.bfloat16),
            result((count, MODEL_WIDTH), jnp.float32),
        ],
        scratch=slots_for(unit, MODEL_WIDTH, BLOCK),
        scalars=(index,),
        flops=4 * tokens * MODEL_WIDTH**2,
    )


def attend_kernel(lengths, slots, query, key, value, out):
    length = lengths[pl.program_id(0)]
    kpos = lax.broadcasted_iota(jnp.int32, (query.shape[0], key.shape[0]), 1)
    allowed = (kpos <= slots[...]) & (kpos < length)
    heads = []
    for start in range(0, query.shape[1], HD):
        part = slice(start, start + HD)
        raw = product_right_transposed(query[:, part], key[:, part]) * HD ** (-0.5)
        raw = jnp.where(allowed, raw, NEGATIVE)
        prob = jnp.exp(raw - jnp.max(raw, axis=1, keepdims=True))
        prob = prob * (1.0 / jnp.sum(prob, axis=1, keepdims=True))
        heads.append(product_plain(low(prob), value[:, part]))
    out[...] = low(jnp.concatenate(heads, axis=1))


def own_lanes(count, heads):
    shape = (heads * count, heads * HD)
    row = lax.broadcasted_iota(jnp.int32, shape, 0) // count
    lane = lax.broadcasted_iota(jnp.int32, shape, 1) // HD
    return row == lane


def stacked_heads(rows, own):
    heads = own.shape[0] // rows.shape[0]
    tall = jnp.concatenate([rows.astype(jnp.float32)] * heads, axis=0)
    return low(jnp.where(own, tall, 0.0))


def own_heads(tall, own, count):
    tall = jnp.where(own, tall, 0.0)
    total = tall[:count]
    for start in range(count, tall.shape[0], count):
        total = total + tall[start : start + count]
    return total


def few_scores(length, slots, tall, key):
    raw = product_right_transposed(tall, key[...]) * HD ** (-0.5)
    kpos = lax.broadcasted_iota(jnp.int32, raw.shape, 1)
    places = jnp.concatenate([slots[...]] * (raw.shape[0] // slots.shape[0]), axis=0)
    raw = jnp.where((kpos <= places) & (kpos < length), raw, NEGATIVE)
    prob = jnp.exp(raw - jnp.max(raw, axis=1, keepdims=True))
    return prob * (1.0 / jnp.sum(prob, axis=1, keepdims=True))


def attend_few_kernel(lengths, slots, query, key, value, out):
    count = query.shape[0]
    own = own_lanes(count, query.shape[1] // HD)
    prob = few_scores(lengths[pl.program_id(0)], slots, stacked_heads(query[...], own), key)
    out[...] = low(own_heads(product_plain(low(prob), value[...]), own, count))


def attend_few_back_kernel(lengths, slots, query, key, value, d_out, d_query, d_key, d_value):
    count = query.shape[0]
    own = own_lanes(count, query.shape[1] // HD)
    tall = stacked_heads(query[...], own)
    d_tall = stacked_heads(d_out[...], own)
    prob = few_scores(lengths[pl.program_id(0)], slots, tall, key)
    d_prob = product_right_transposed(d_tall, value[...])
    d_raw = low(prob * (d_prob - jnp.sum(prob * d_prob, axis=1, keepdims=True)))
    d_value[...] = low(product_left_transposed(low(prob), d_tall))
    d_key[...] = low(product_left_transposed(d_raw, tall) * HD ** (-0.5))
    d_query[...] = low(own_heads(product_plain(d_raw, key[...]), own, count) * HD ** (-0.5))


def head_blocks(array, height, third, steps):
    offset = third * steps
    return array, pl.BlockSpec((height, MODEL_WIDTH // steps), lambda r, h, *_: (r, offset + h))


def head_steps(count):
    return 1 if count > 128 else 1


def attend(lengths, slots, query, key, value):
    rows, count = slots.shape
    seq = key[0].shape[0] // rows
    steps = head_steps(count)
    column = slots.reshape(-1, 1)
    (out,) = launch(
        attend_kernel if count > 128 else attend_few_kernel,
        (rows, steps),
        [
            (column, pl.BlockSpec((count, 1), lambda r, h, *_: (r, 0))),
            head_blocks(query[0], count, query[1], steps),
            head_blocks(key[0], seq, key[1], steps),
            head_blocks(value[0], seq, value[1], steps),
        ],
        [
            result(
                (rows * count, MODEL_WIDTH),
                jnp.bfloat16,
                (count, MODEL_WIDTH // steps),
                lambda r, h, *_: (r, h),
            )
        ],
        scalars=(lengths,),
        flops=4 * rows * count * seq * MODEL_WIDTH,
    )
    return out


def attend_back_kernel(lengths, slots, query, key, value, d_out, d_query, d_key, d_value):
    length = lengths[pl.program_id(0)]
    kpos = lax.broadcasted_iota(jnp.int32, (key.shape[0], query.shape[0]), 0)
    allowed = (kpos <= slots[...]) & (kpos < length)
    parts = []
    for start in range(0, query.shape[1], HD):
        part = slice(start, start + HD)
        q, k, v, d_o = query[:, part], key[:, part], value[:, part], d_out[:, part]
        raw = product_right_transposed(k, q) * HD ** (-0.5)
        raw = jnp.where(allowed, raw, NEGATIVE)
        prob = jnp.exp(raw - jnp.max(raw, axis=0, keepdims=True))
        prob = prob * (1.0 / jnp.sum(prob, axis=0, keepdims=True))
        d_prob = product_right_transposed(v, d_o)
        d_raw = low(prob * (d_prob - jnp.sum(prob * d_prob, axis=0, keepdims=True)))
        parts.append(
            (
                product_left_transposed(d_raw, k) * HD ** (-0.5),
                product_plain(d_raw, q) * HD ** (-0.5),
                product_plain(low(prob), d_o),
            )
        )
    for n, ref in enumerate((d_query, d_key, d_value)):
        ref[...] = low(jnp.concatenate([part[n] for part in parts], axis=1))


def attend_back(lengths, slots, query, key, value, d_out):
    rows, count = slots.shape
    seq = key[0].shape[0] // rows
    steps = head_steps(count)
    heights = (count, seq, seq)
    return launch(
        attend_back_kernel if count > 128 else attend_few_back_kernel,
        (rows, steps),
        [
            (
                slots.reshape(rows, 1, count),
                pl.BlockSpec((None, 1, count), lambda r, h, *_: (r, 0, 0)),
            )
            if count > 128
            else (slots.reshape(-1, 1), pl.BlockSpec((count, 1), lambda r, h, *_: (r, 0))),
            head_blocks(query[0], count, query[1], steps),
            head_blocks(key[0], seq, key[1], steps),
            head_blocks(value[0], seq, value[1], steps),
            head_blocks(d_out, count, 0, steps),
        ],
        [
            result(
                (rows * height, MODEL_WIDTH),
                jnp.bfloat16,
                (height, MODEL_WIDTH // steps),
                lambda r, h, *_: (r, h),
            )
            for height in heights
        ],
        scalars=(lengths,),
        flops=10 * rows * count * seq * MODEL_WIDTH,
    )


def gelu_parts(value):
    root, bend = 0.7978845608028654, 0.044715
    square = value * value
    turned = jnp.tanh(value * (root + root * bend * square))
    half = 0.5 + 0.5 * turned
    steep = (1.0 - turned * turned) * (0.5 * root + 1.5 * root * bend * square)
    return value * half, half + value * steep


def middle_into(x2, uo, x, o, w_o, c_o, d_o, u_o):
    uo[...] = low(product_right_transposed(o[...], d_o[...]))
    x2[...] = x[...] + (
        product_plain(o[...], w_o[...]) + c_o[...] + adapter(uo[...], u_o[...])
    )


FIRST_FEED = 4 * MODEL_WIDTH // BLOCK
FEED_STEPS = HIDDEN_UNITS // BLOCK
PIECES = 8
CHUNK = BLOCK // PIECES


def chunk_place(unit):
    part, rest = unit // (CHUNK * FEED_STEPS), unit % (CHUNK * FEED_STEPS)
    return pl.ds(pl.multiple_of(rest // CHUNK * BLOCK + part * CHUNK, CHUNK), CHUNK)


def chunked(part):
    return jnp.concatenate(jnp.split(part, FEED_STEPS), axis=1)


def feed_step(j):
    return jnp.minimum(j, FEED_STEPS - 1)


def late_step(j):
    return jnp.maximum(j - FEED_STEPS, 0)


def feed_in_kernel(unit, unit_fc, *refs):
    pieces, pieces_fc, refs = taken(refs, unit, unit_fc)
    x, o, c_o, d_o, u_o, gain, shift, c_fc, d_fc, u_fc = refs[:10]
    x2, uo, m, um, act, slope, weight_o, sems_o, slots, sems, pre, plain = refs[10:]
    first = moves(unit, pieces, weight_o, sems_o, 3, BLOCK)
    pl.when(pl.program_id(0) == 0)(lambda: begin(first))
    weight = next_strip(unit_fc, pieces_fc, slots, sems, BLOCK)

    @pl.when(pl.program_id(0) == 0)
    def _():
        finish(first)
        middle_into(x2, uo, x, o, weight_o, c_o, d_o, u_o)
        norm_into(m, x2, gain[...], shift[...])
        um[...] = low(product_right_transposed(m[...], d_fc[...]))

    pre[...] = product_plain(m[...], weight[...]) + c_fc[...] + adapter(um[...], u_fc[...])
    j = pl.program_id(0)

    def part(rows):
        first, second = gelu_parts(pre[rows, :])
        slope[rows, :] = low(second)
        plain[rows, :] = low(first)

    over_rows(pre.shape[0], 64, part)
    for start in range(0, BLOCK, CHUNK):
        act[:, chunk_place(j * BLOCK + start)] = plain[:, start : start + CHUNK]


def feed_in(x, o, unit, unit_fc, p, layer):
    tokens = o.shape[0]
    small, up = p["small"], p["up"]
    wide = (tokens, HIDDEN_UNITS), jnp.bfloat16, (tokens, BLOCK), lambda j: (0, j)
    return launch(
        partial(feed_in_kernel, unit, unit_fc),
        (FEED_STEPS,),
        unit.operands()
        + unit_fc.operands()
        + [
            some_rows(x, tokens),
            whole(o),
            strip(small, BLOCK, 3, layer),
            whole(p["down_t"], layer, 1),
            strip(up, BLOCK, 3, layer),
            strip(small, BLOCK, 11, layer),
            strip(small, BLOCK, 12, layer),
            strip(small, BLOCK, lambda j: FIRST_FEED + j, layer),
            whole(p["down_t"], layer, 2),
            strip(up, BLOCK, lambda j: FIRST_FEED + j, layer),
        ],
        [
            result((tokens, MODEL_WIDTH), jnp.float32),
            result((tokens, LANES), jnp.bfloat16),
            result((tokens, MODEL_WIDTH), jnp.bfloat16),
            result((tokens, LANES), jnp.bfloat16),
            result((tokens, HIDDEN_UNITS), jnp.bfloat16),
            result(*wide),
        ],
        scratch=one_slot_for(unit)
        + slots_for(unit_fc, MODEL_WIDTH, BLOCK)
        + [pltpu.VMEM((tokens, BLOCK), jnp.float32), pltpu.VMEM((tokens, BLOCK), jnp.bfloat16)],
        flops=2 * tokens * MODEL_WIDTH * (MODEL_WIDTH + HIDDEN_UNITS),
    )


def feed_out_kernel(unit_fp, *refs):
    pieces_fp, refs = taken(refs, unit_fp)
    x2, act, d_fp, c_fp, u_fp, final, x3, ug, h, slots, sems = refs
    j = pl.program_id(0)
    weight = next_strip(unit_fp, pieces_fp, slots, sems, BLOCK)

    @pl.when(j == 0)
    def _():
        ug[...] = jnp.zeros_like(ug)
        x3[...] = x2[...] + c_fp[...]

    taken_act = act[...]
    x3[...] += product_plain(taken_act, weight[...])
    maps = [
        d_fp[:, pl.ds(pl.multiple_of((n * FEED_STEPS + j) * CHUNK, CHUNK), CHUNK)]
        for n in range(PIECES)
    ]
    ug[...] += product_right_transposed(taken_act, jnp.concatenate(maps, axis=1))

    @pl.when(j == pl.num_programs(0) - 1)
    def _():
        x3[...] += adapter(low(ug[...]), u_fp[...])
        gains = final[...].astype(jnp.float32)
        if h.shape == x3.shape:
            norm_into(h, x3, gains[0:1], gains[1:2])


def feed_out(x2, act, unit_fp, final, p, layer, with_norm):
    tokens = x2.shape[0]
    return launch(
        partial(feed_out_kernel, unit_fp),
        (FEED_STEPS,),
        unit_fp.operands()
        + [
            whole(x2),
            strip(act, BLOCK, lambda j: j),
            whole(p["feed_t"], layer),
            strip(p["small"], BLOCK, 8, layer),
            strip(p["up"], BLOCK, 8, layer),
            whole(final),
        ],
        [
            result((tokens, MODEL_WIDTH), jnp.float32),
            result((tokens, LANES), jnp.float32),
            result((tokens if with_norm else 16, MODEL_WIDTH), jnp.bfloat16),
        ],
        scratch=slots_for(unit_fp, BLOCK, MODEL_WIDTH),
        flops=2 * tokens * MODEL_WIDTH * HIDDEN_UNITS,
    )


def three_parts(value):
    first = low(value)
    rest = value - first.astype(jnp.float32)
    second = low(rest)
    return [first, second, low(rest - second.astype(jnp.float32))]


def head_kernel(h, table, out, logits, total, top, bulk):
    j = pl.program_id(0)

    @pl.when(j == 0)
    def _():
        top[...] = jnp.full_like(top, NEGATIVE)
        bulk[...] = jnp.zeros_like(bulk)
        total[...] = jnp.zeros_like(total)

    def part(rows):
        logits[...] = product_right_transposed(h[rows, :], table[...])
        before = top[rows, :]
        now = jnp.maximum(before, jnp.max(logits[...], axis=1, keepdims=True))
        fade = jnp.exp(before - now)
        top[rows, :] = now
        weight = jnp.exp(logits[...] - now)
        bulk[rows, :] = bulk[rows, :] * fade + jnp.sum(weight, axis=1, keepdims=True)
        total[rows, :] = total[rows, :] * fade + product_plain(low(weight), table[...])

    over_rows(h.shape[0], logits.shape[0], part)

    @pl.when(j == pl.num_programs(0) - 1)
    def _():
        out[:, :MODEL_WIDTH] = low(total[...])
        columns = three_parts(top[...]) + three_parts(bulk[...])
        rest = jnp.zeros((h.shape[0], 128 - len(columns)), jnp.bfloat16)
        out[:, MODEL_WIDTH:] = jnp.concatenate(columns + [rest], axis=1)


def head(h, table):
    tokens, vocab = h.shape[0], table.shape[0]
    steps = 3 if vocab % 48 == 0 else 1
    tile = vocab // steps
    chunk = min(512, tokens)
    (out,) = launch(
        head_kernel,
        (steps,),
        [whole(h), rows_strip(table, tile, lambda j: j)],
        [result((tokens, MODEL_WIDTH + 128), jnp.bfloat16)],
        scratch=[
            pltpu.VMEM((chunk, tile), jnp.float32),
            pltpu.VMEM((tokens, MODEL_WIDTH), jnp.float32),
            pltpu.VMEM((tokens, 1), jnp.float32),
            pltpu.VMEM((tokens, 1), jnp.float32),
        ],
        flops=4 * tokens * vocab * MODEL_WIDTH,
    )
    return out


def head_back_kernel(parts, targets, h, x3, final, mask, terms, d_x3, d_hidden):
    tails = [
        parts[n, :, MODEL_WIDTH:].astype(jnp.float32) for n in range(parts.shape[0])
    ]
    tops = [tail[:, 0:1] + tail[:, 1:2] + tail[:, 2:3] for tail in tails]
    sums = [tail[:, 3:4] + tail[:, 4:5] + tail[:, 5:6] for tail in tails]
    top = tops[0]
    for other in tops[1:]:
        top = jnp.maximum(top, other)
    whole_sum = sum(s * jnp.exp(t - top) for t, s in zip(tops, sums))
    lse = top + jnp.log(whole_sum)
    wanted = targets[...]
    logit = jnp.sum(h[...].astype(jnp.float32) * wanted, axis=1, keepdims=True)
    terms[...] = (lse - logit) * mask[...]
    gathered = -wanted
    for n, t in enumerate(tops):
        gathered = gathered + parts[n, :, :MODEL_WIDTH].astype(jnp.float32) * jnp.exp(t - lse)
    d_hidden[...] = gathered * mask[...]
    norm_back_into(d_x3, d_hidden, x3, final[...].astype(jnp.float32)[0:1])


def head_back(parts, targets, h, x3, final, mask):
    count = h.shape[0]
    return launch(
        head_back_kernel,
        (1,),
        [whole(parts), some_rows(targets, count, targets.shape[0] // count - 1), whole(h), whole(x3), whole(final), whole(mask)],
        [
            result((count, 1), jnp.float32),
            result((count, MODEL_WIDTH), jnp.float32),
        ],
        scratch=[pltpu.VMEM((count, MODEL_WIDTH), jnp.float32)],
    )


def output_back(d_heads, grad_uo, grad_do, d_x2, o, uo, w_o, u_o, d_o):
    d_low = low(d_x2[...])
    grad_uo[...] = ADAPTER_SCALE * product_left_transposed(uo[...], d_low)
    duo = low(ADAPTER_SCALE * product_right_transposed(d_low, u_o[...]))
    grad_do[...] = product_left_transposed(duo, o[...])
    d_heads[...] = low(
        product_right_transposed(d_low, w_o[...]) + product_plain(duo, d_o[...])
    )


def front_last_back_kernel(unit, index, *refs):
    pieces, refs = taken(refs, unit)
    d_query, d_key, d_value, a, a_sel, ua, ua_sel, up, down, d_x2, x, gain = refs[:12]
    d_x, grad_up, grad_down, rows, rows_sel, inner, inner_sel, slots, sems = refs[12:]
    j = pl.program_id(0)
    weight = next_strip(unit, pieces, slots, sems, BLOCK)

    @pl.when(j == 0)
    def _():
        rows[...] = jnp.zeros_like(rows)
        inner[...] = jnp.zeros_like(inner)

    @pl.when(j == 0)
    def _():
        gradient = d_query[...]
        grad_up[...] = ADAPTER_SCALE * product_left_transposed(ua_sel[...], gradient)
        inner_sel[...] = ADAPTER_SCALE * product_right_transposed(gradient, up[...])
        rows_sel[...] = product_right_transposed(gradient, weight[...])

    def step(ref):
        gradient = ref[...]
        grad_up[...] = ADAPTER_SCALE * product_left_transposed(ua[...], gradient)
        inner[...] += ADAPTER_SCALE * product_right_transposed(gradient, up[...])
        rows[...] += product_right_transposed(gradient, weight[...])

    pl.when(j == 1)(lambda: step(d_key))
    pl.when(j == 2)(lambda: step(d_value))

    @pl.when(j == pl.num_programs(0) - 1)
    def _():
        last, last_sel = low(inner[...]), low(inner_sel[...])
        grad_down[...] = product_left_transposed(last, a[...]) + product_left_transposed(
            last_sel, a_sel[...]
        )
        rows[...] += product_plain(last, down[...])
        rows_sel[...] += product_plain(last_sel, down[...])
        add_rows(index, rows_sel, rows)
        norm_back_into(d_x, rows, x, gain[...])
        add_rows(index, d_x2, d_x)


def front_last_back(index, d_query, d_key, d_value, saved, d_x2, x, unit, p, layer):
    a, a_sel, ua, ua_sel = saved
    tokens, count = x.shape[0], index.shape[0]
    return launch(
        partial(front_last_back_kernel, unit),
        (3,),
        unit.operands()
        + [
            whole(d_query),
            whole(d_key),
            whole(d_value),
            whole(a),
            whole(a_sel),
            whole(ua),
            whole(ua_sel),
            strip(p["up"], BLOCK, lambda j: j, layer),
            whole(p["down_t"], layer, 0),
            whole(d_x2),
            whole(x),
            strip(p["small"], BLOCK, 9, layer),
        ],
        [
            result((tokens, MODEL_WIDTH), jnp.float32),
            result((LANES, 3 * MODEL_WIDTH), jnp.float32, (LANES, BLOCK), lambda j, *_: (0, j)),
            result((LANES, MODEL_WIDTH), jnp.float32),
        ],
        scratch=[
            pltpu.VMEM((tokens, MODEL_WIDTH), jnp.float32),
            pltpu.VMEM((count, MODEL_WIDTH), jnp.float32),
            pltpu.VMEM((tokens, LANES), jnp.float32),
            pltpu.VMEM((count, LANES), jnp.float32),
        ]
        + slots_for(unit, MODEL_WIDTH, BLOCK),
        scalars=(index,),
        flops=4 * tokens * MODEL_WIDTH**2,
    )


def feed_back_kernel(unit, unit_fc, unit_fp, *refs):
    pieces, pieces_fc, pieces_fp, refs = taken(refs, unit, unit_fc, unit_fp)
    d_x3, far_x2, far_m, um, ug, uo, far_o, act, slope = refs[:9]
    d_fp, u_fc, u_fp, d_fc, gain, u_o, d_o = refs[9:16]
    d_x2, d_heads, grad_ufp, grad_dfp, grad_ufc, grad_dfc, grad_uo, grad_do = refs[16:24]
    d_out, dug, d_pre, inner, d_feed, x2, m, o, late_sems = refs[24:33]
    weight_o, sems_o, slots, sems = refs[33:]
    late = [
        pltpu.make_async_copy(source, target, late_sems.at[n])
        for n, (source, target) in enumerate(((far_x2, x2), (far_m, m), (far_o, o)))
    ]
    j = pl.program_id(0)
    last = pl.num_programs(0) - 1
    out_moves = moves(unit, pieces, weight_o, sems_o, 3, BLOCK)

    def each(step, act):
        slot = lax.rem(step, 2)
        for some, refs, first in ((unit_fp, pieces_fp, 0), (unit_fc, pieces_fc, FEED_STEPS)):

            @pl.when((step >= first) & (step < first + FEED_STEPS))
            def _(some=some, refs=refs, first=first):
                column = jnp.clip(step - first, 0, FEED_STEPS - 1)
                act(moves(some, refs, slots.at[slot], sems.at[slot], column, BLOCK))

    pl.when(j == 0)(lambda: each(j, begin))

    @pl.when(j == 0)
    def _():
        for copy in late:
            copy.start()

    pl.when(j < last)(lambda: each(j + 1, begin))
    pl.when(j == last)(lambda: begin(out_moves))

    @pl.when(j == 0)
    def _():
        d_out[...] = low(d_x3[...])
        dug[...] = low(ADAPTER_SCALE * product_right_transposed(d_out[...], u_fp[...]))
        grad_ufp[...] = ADAPTER_SCALE * product_left_transposed(low(ug[...]), d_out[...])
        inner[...] = jnp.zeros_like(inner)
        d_feed[...] = jnp.zeros_like(d_feed)

    each(j, finish)
    weight = slots.at[lax.rem(j, 2)]

    @pl.when(j < FEED_STEPS)
    def _():
        d_act = product_right_transposed(d_out[...], weight[...])
        from_act = product_left_transposed(dug[...], act[...])
        for n in range(PIECES):
            place = pl.ds(pl.multiple_of((n * FEED_STEPS + j) * CHUNK, CHUNK), CHUNK)
            part = slice(n * CHUNK, (n + 1) * CHUNK)
            value = d_act[:, part] + product_plain(dug[...], d_fp[:, place])
            d_pre[:, place] = low(value * slope[:, place].astype(jnp.float32))
            grad_dfp[:, place] = from_act[:, part]

    @pl.when(j >= FEED_STEPS)
    def _():
        columns = pl.ds(pl.multiple_of((j - FEED_STEPS) * BLOCK, BLOCK), BLOCK)
        gradient = d_pre[:, columns]
        grad_ufc[...] = ADAPTER_SCALE * product_left_transposed(um[...], gradient)
        inner[...] += ADAPTER_SCALE * product_right_transposed(gradient, u_fc[...])
        d_feed[...] += product_right_transposed(gradient, weight[...])

    @pl.when(j == last)
    def _():
        for copy in late:
            copy.wait()
        dum = low(inner[...])
        grad_dfc[...] = product_left_transposed(dum, m[...])
        d_feed[...] += product_plain(dum, d_fc[...])
        norm_back_into(d_x2, d_feed, x2, gain[...], d_x3)
        finish(out_moves)
        output_back(d_heads, grad_uo, grad_do, d_x2, o, uo, weight_o, u_o, d_o)


def feed_back(d_x3, saved, unit, unit_fc, unit_fp, p, layer):
    x2, m, um, ug, uo, o, act, slope = saved
    tokens = x2.shape[0]
    square = (LANES, MODEL_WIDTH), jnp.float32
    return launch(
        partial(feed_back_kernel, unit, unit_fc, unit_fp),
        (2 * FEED_STEPS,),
        unit.operands()
        + unit_fc.operands()
        + unit_fp.operands()
        + [
            whole(d_x3),
            (x2, pl.BlockSpec(memory_space=pltpu.HBM)),
            (m, pl.BlockSpec(memory_space=pltpu.HBM)),
            whole(um),
            whole(ug),
            whole(uo),
            (o, pl.BlockSpec(memory_space=pltpu.HBM)),
            strip(act, BLOCK, feed_step),
            whole(slope),
            whole(p["feed_t"], layer),
            strip(p["up"], BLOCK, lambda j: FIRST_FEED + late_step(j), layer),
            strip(p["up"], BLOCK, 8, layer),
            whole(p["down_t"], layer, 2),
            strip(p["small"], BLOCK, 11, layer),
            strip(p["up"], BLOCK, 3, layer),
            whole(p["down_t"], layer, 1),
        ],
        [
            result((tokens, MODEL_WIDTH), jnp.float32),
            result((tokens, MODEL_WIDTH), jnp.bfloat16),
            result(*square),
            result((LANES, HIDDEN_UNITS), jnp.float32),
            result(
                (LANES, HIDDEN_UNITS), jnp.float32, (LANES, BLOCK), lambda j: (0, late_step(j))
            ),
            result(*square),
            result(*square),
            result(*square),
        ],
        scratch=[
            pltpu.VMEM((tokens, MODEL_WIDTH), jnp.bfloat16),
            pltpu.VMEM((tokens, LANES), jnp.bfloat16),
            pltpu.VMEM((tokens, HIDDEN_UNITS), jnp.bfloat16),
            pltpu.VMEM((tokens, LANES), jnp.float32),
            pltpu.VMEM((tokens, MODEL_WIDTH), jnp.float32),
            pltpu.VMEM((tokens, MODEL_WIDTH), jnp.float32),
            pltpu.VMEM((tokens, MODEL_WIDTH), jnp.bfloat16),
            pltpu.VMEM((tokens, MODEL_WIDTH), jnp.bfloat16),
            pltpu.SemaphoreType.DMA((3,)),
        ]
        + one_slot_for(unit)
        + slots_for(unit_fc, MODEL_WIDTH, BLOCK),
        flops=2 * tokens * MODEL_WIDTH * (MODEL_WIDTH + 2 * HIDDEN_UNITS),
    )


def front_back_kernel(d_query, d_key, d_value, a, ua, up, grad_up, grad_down):
    inner = 0.0
    for n, ref in enumerate((d_query, d_key, d_value)):
        columns = slice(n * MODEL_WIDTH, (n + 1) * MODEL_WIDTH)
        grad_up[:, columns] = ADAPTER_SCALE * product_left_transposed(ua[...], ref[...])
        inner = inner + ADAPTER_SCALE * product_right_transposed(ref[...], up[:, columns])
    grad_down[...] = product_left_transposed(low(inner), a[...])


def front_back(d_query, d_key, d_value, a, ua, p, layer):
    return launch(
        front_back_kernel,
        (1,),
        [
            whole(d_query),
            whole(d_key),
            whole(d_value),
            whole(a),
            whole(ua),
            strip(p["up"], 3 * MODEL_WIDTH, 0, layer),
        ],
        [
            result((LANES, 3 * MODEL_WIDTH), jnp.float32),
            result((LANES, MODEL_WIDTH), jnp.float32),
        ],
    )


def pack_kernel(columns, *refs):
    extras, parts, out = refs[0], refs[1:-1], refs[-1]
    shards, width = out.shape[0], out.shape[2] - 128
    three = [part.astype(jnp.float32) for part in three_parts(extras[...])]
    rest = jnp.zeros((out.shape[1] - len(three), 128), jnp.float32)
    for n in range(shards):
        out[n, :, width:] = low(jnp.concatenate(three + [rest], axis=0))
    layers = {}
    for part, (row, start) in zip(parts, columns):
        layers.setdefault(start, []).append(part)
    for start, refs in layers.items():
        values = low(jnp.concatenate([ref[0:ADAPTER_RANK, :] for ref in refs], axis=0))
        size = values.shape[1]
        done = 0
        while done < size:
            block, offset = divmod(start + done, width)
            step = min(width - offset, size - done)
            out[block, :, offset : offset + step] = values[:, done : done + step]
            done += step


def packed(by_layer, extras):
    shards = lax.axis_size("fsdp")
    columns, parts = [], []
    for layer, row in enumerate(by_layer):
        start = 0
        for part in row:
            parts.append(part)
            columns.append((layer * ADAPTER_RANK, start))
            start += part.shape[1]
    shape = (shards, len(by_layer) * ADAPTER_RANK, start // shards + 128)
    (out,) = launch(
        partial(pack_kernel, tuple(columns)),
        (1,),
        [whole(extras)] + [whole(part) for part in parts],
        [result(shape, jnp.bfloat16)],
    )
    return out


def asking(table, ids, needed):
    shards = lax.axis_size("fsdp")
    total = ids.shape[0]
    order = jnp.arange(total, dtype=jnp.int32)
    owner = ids // table.shape[0]
    local = ids - owner * table.shape[0]
    same = (ids[:, None] == ids[None, :]) & needed[None, :]
    first = jnp.min(jnp.where(same, order[None, :], total), axis=1)
    leads = needed & (first == order)
    rank = jnp.sum(
        (leads & (owner[:, None] == owner[None, :]) & (order[None, :] < first[:, None])).astype(
            jnp.int32
        ),
        axis=1,
    )
    rounds = (jnp.max(jnp.where(needed, rank, 0)) + CAPACITY) // CAPACITY

    spots = jnp.arange(shards * CAPACITY, dtype=jnp.int32)

    def place_of(turn):
        return jnp.where(
            needed & (rank // CAPACITY == turn), owner * CAPACITY + rank % CAPACITY, -1
        )

    def ask(turn):
        place = place_of(turn)
        asked = jnp.sum(
            jnp.where(leads[:, None] & (place[:, None] == spots[None, :]), local[:, None], 0), axis=0
        )
        return asked.reshape(shards, CAPACITY)

    def sent_for(asked):
        return table.at[asked.reshape(-1)].get(mode="promise_in_bounds")

    def exchanged(part):
        return lax.all_to_all(part, "fsdp", 0, 0, tiled=True)

    def found(turn, back):
        pick = (place_of(turn)[:, None] == spots[None, :]).astype(jnp.bfloat16)
        return product_plain(pick, back)

    def with_rounds(most, added):
        def more(so_far):
            return lax.fori_loop(
                1,
                most,
                lambda turn, total: total
                + found(turn, exchanged(sent_for(exchanged(ask(turn))))),
                so_far,
            )

        return lax.cond(most > 1, more, lambda so_far: so_far, added)

    return ask, rounds, exchanged, sent_for, found, with_rounds


def as_low(numbers):
    return low(numbers // 256), low(numbers % 256)


def as_numbers(high, rest):
    return high.astype(jnp.int32) * 256 + rest.astype(jnp.int32)


def swap(part, bit):
    return lax.ppermute(part, "fsdp", [(i, i ^ bit) for i in range(lax.axis_size("fsdp"))])


def tie(parts, before):
    parts, _ = lax.optimization_barrier((parts, before))
    return parts


def hop(part):
    return lax.ppermute(
        part, "fsdp", [(i, i ^ (4 if i % 2 else 2)) for i in range(lax.axis_size("fsdp"))]
    )


class Gathering:
    PLACES = (0, 0), (1, 1), (2, 4), (3, 5), (5, 3), (4, 2), (7, 7), (6, 6)

    def __init__(self, shard, in_chunks=False):
        self.shard, self.in_chunks = shard, in_chunks
        self.direct = lax.axis_size("fsdp") == PIECES

    def begin(self, before=()):
        if self.direct:
            own = chunked(self.shard) if self.in_chunks else self.shard
            own = tie(own, before)
            other = swap(own, 1)
            self.arrays = own, other, hop(own), hop(other)

    def after_first(self, value):
        return tie(value, self.arrays[1]) if self.direct else value

    def after_last(self, value):
        return tie(value, self.arrays[4]) if self.direct else value

    def pass_on(self, value):
        if self.direct:
            own, other, first, second = self.arrays
            first, value = lax.optimization_barrier((first, value))
            handed = swap(first, 1)
            self.arrays = own, other, first, second, handed, swap(second, 1), hop(handed)
        return value

    def settle(self, value):
        if not self.direct:
            parts = jnp.split(lax.all_gather(self.shard, "fsdp", axis=0, tiled=True), PIECES)
            parts = [chunked(part) for part in parts] if self.in_chunks else parts
            return value, Unit(tuple(range(PIECES)), tuple(parts), parts[0].shape[0])
        far, value = lax.optimization_barrier((self.arrays[-1], value))
        arrays = self.arrays[:-1] + (far, swap(far, 1))
        return value, Unit(self.PLACES, arrays, arrays[0].shape[0])


def everywhere(part):
    shards = lax.axis_size("fsdp")
    return lax.all_to_all(
        jnp.tile(part, (shards,) + (1,) * (part.ndim - 1)), "fsdp", 0, 0, tiled=True
    )


def owned_parts(parts):
    shards = lax.axis_size("fsdp")
    rows = parts.shape[0] // shards
    return lax.all_to_all(parts, "fsdp", 0, 0, tiled=True).reshape(
        (shards, rows) + parts.shape[1:]
    )


def summed_everywhere(blocks):
    shards, rows, columns = blocks.shape
    groups = lax.axis_size("dp")
    width = columns - 128
    parts = owned_parts(blocks.reshape(shards * rows, columns)).astype(jnp.float32)
    block = jnp.sum(parts, axis=0)
    others = [
        lax.ppermute(block, "dp", [(i, (i + k) % groups) for i in range(groups)])
        for k in range(1, groups)
    ]
    stacked = jnp.stack([block] + others)
    order = (lax.axis_index("dp") - jnp.arange(groups)) % groups
    ranks = (order[None, :] == jnp.arange(groups)[:, None])[:, :, None, None]
    total = jnp.sum(jnp.sum(jnp.where(ranks, stacked[None], 0.0), axis=1), axis=0)
    gathered = everywhere(low(total[:, :width])).reshape(shards, rows, width)
    sums = total[:3, width : width + 2]
    return (
        gathered.astype(jnp.float32).transpose(1, 0, 2).reshape(rows, shards * width),
        sums[0] + sums[1] + sums[2],
    )


def body(
    input_token_ids,
    lengths,
    scored_slots,
    scored_targets,
    wte,
    wpe,
    frozen_attention,
    frozen_feed_input,
    frozen_feed_output,
    frozen_bias_gain,
    final_norm_params,
    adapter_down,
    adapter_down_feed,
    adapter_up,
    first_moment_down,
    first_moment_feed,
    first_moment_up,
    second_moment_down,
    second_moment_feed,
    second_moment_up,
    optimizer_step,
):
    micro, seqs, seq = input_token_ids.shape
    rows = micro * seqs
    picks = scored_slots.shape[2]
    layers = frozen_attention.shape[0]
    shards = lax.axis_size("fsdp")
    row_lengths = lengths.reshape(rows)
    slots = scored_slots.reshape(rows, picks)
    valid = slots < row_lengths[:, None]
    mask = valid.reshape(-1, 1).astype(jnp.float32)
    all_slots = jnp.tile(jnp.arange(seq, dtype=jnp.int32)[None], (rows, 1))

    useful = jnp.max(jnp.where(valid, slots, -1), axis=1)
    needed = jnp.concatenate([(all_slots <= useful[:, None]).reshape(-1), valid.reshape(-1)])
    ids = jnp.concatenate([input_token_ids.reshape(-1), scored_targets.reshape(-1)])
    attention_one, attention_two = Gathering(frozen_attention[0]), Gathering(frozen_attention[1])
    feed_in_one, feed_in_two = Gathering(frozen_feed_input[0]), Gathering(frozen_feed_input[1])
    feed_out_one = Gathering(frozen_feed_output[0], in_chunks=True)
    feed_out_two = Gathering(frozen_feed_output[1], in_chunks=True)
    attention_one.begin()
    ask, rounds, exchanged, sent_for, found, with_rounds = asking(wte, ids, needed)
    count = CAPACITY
    requests = as_low(jnp.concatenate([ask(0), jnp.full((shards, 1), rounds, jnp.int32)], 1))
    biases = jnp.tile(frozen_bias_gain.reshape(1, -1), (shards, 1))
    message = jnp.concatenate([*requests, biases], 1)
    got = exchanged(attention_one.after_first(message))
    got = attention_one.pass_on(got)
    feed_in_one.begin(got)
    numbers = as_numbers(got[:, : count + 1], got[:, count + 1 : 2 * count + 2])
    small = (
        got[:, 2 * count + 2 :].reshape(shards, layers, -1).transpose(1, 0, 2).reshape(layers, 1, -1)
    )
    sent = sent_for(attention_one.after_last(numbers[:, :count]))
    most = jnp.max(numbers[:, count])
    extra = LANES - ADAPTER_RANK
    down_t = adapter_down.reshape(layers, MODEL_WIDTH, 3, ADAPTER_RANK).transpose(0, 2, 3, 1)
    p = {
        "small": small.astype(jnp.float32),
        "down_t": low(jnp.pad(down_t, ((0, 0), (0, 0), (0, extra), (0, 0)))),
        "feed_t": low(jnp.pad(adapter_down_feed.transpose(0, 2, 1), ((0, 0), (0, extra), (0, 0)))),
        "up": low(jnp.pad(adapter_up, ((0, 0), (0, extra), (0, 0)))),
    }
    places = jnp.concatenate([wpe.astype(jnp.float32)] * rows)
    places = jnp.pad(places, ((0, rows * picks), (0, 0)))
    places = with_rounds(most, places)
    back, p, places = lax.optimization_barrier((exchanged(sent), p, places))
    back, attention_one = attention_one.settle(back)
    back = feed_in_one.pass_on(back)
    feed_out_one.begin(back)
    x0 = found(0, back) + places
    index = (slots + seq * jnp.arange(rows, dtype=jnp.int32)[:, None]).reshape(-1)

    qkv, a_one, ua_one = front(x0, rows * seq, attention_one, p, 0)
    qkv = feed_out_one.pass_on(qkv)
    attention_two.begin(qkv)
    split_qkv = (qkv, 0), (qkv, 1), (qkv, 2)
    o_one = attend(row_lengths, all_slots, *split_qkv)
    o_one, feed_in_one = feed_in_one.settle(o_one)
    o_one = attention_two.pass_on(o_one)
    feed_in_two.begin(o_one)
    x2_one, uo_one, m_one, um_one, act_one, slope_one = feed_in(
        x0, o_one, attention_one, feed_in_one, p, 0
    )
    act_one, feed_out_one = feed_out_one.settle(act_one)
    act_one = feed_in_two.pass_on(act_one)
    feed_out_two.begin(act_one)
    x1, ug_one, _ = feed_out(x2_one, act_one, feed_out_one, final_norm_params, p, 0, False)
    x1, attention_two = attention_two.settle(x1)
    x1 = feed_out_two.pass_on(x1)

    query, kv, a_two, a_sel, ua_two, ua_sel, x_sel = front_last(index, x1, attention_two, p, 1)
    query, feed_in_two = feed_in_two.settle(query)
    parts_two = (query, 0), (kv, 0), (kv, 1)
    o_two = attend(row_lengths, slots, *parts_two)
    x2_two, uo_two, m_two, um_two, act_two, slope_two = feed_in(
        x_sel, o_two, attention_two, feed_in_two, p, 1
    )
    act_two, feed_out_two = feed_out_two.settle(act_two)
    x3, ug_two, h = feed_out(x2_two, act_two, feed_out_two, final_norm_params, p, 1, True)

    weighed = owned_parts(head(everywhere(h), wte))
    terms, d_x3 = head_back(weighed, x0, h, x3, final_norm_params, mask)

    d_x2, d_heads, grad_ufp, grad_dfp, grad_ufc, grad_dfc, grad_uo, grad_do = feed_back(
        d_x3,
        (x2_two, m_two, um_two, ug_two, uo_two, o_two, act_two, slope_two),
        attention_two,
        feed_in_two,
        feed_out_two,
        p,
        1,
    )
    d_parts = attend_back(row_lengths, slots, *parts_two, d_heads)
    d_x1, grad_uqkv, grad_dqkv = front_last_back(
        index, *d_parts, (a_two, a_sel, ua_two, ua_sel), d_x2, x1, attention_two, p, 1
    )
    grads_two = [
        grad_dqkv, grad_do, grad_dfc, grad_dfp, grad_uqkv, grad_uo, grad_ufc, grad_ufp
    ]

    _, d_heads, grad_ufp, grad_dfp, grad_ufc, grad_dfc, grad_uo, grad_do = feed_back(
        d_x1,
        (x2_one, m_one, um_one, ug_one, uo_one, o_one, act_one, slope_one),
        attention_one,
        feed_in_one,
        feed_out_one,
        p,
        0,
    )
    d_parts = attend_back(row_lengths, all_slots, *split_qkv, d_heads)
    grad_uqkv, grad_dqkv = front_back(*d_parts, a_one, ua_one, p, 0)
    grads_one = [
        grad_dqkv, grad_do, grad_dfc, grad_dfp, grad_uqkv, grad_uo, grad_ufc, grad_ufp
    ]

    tail = jnp.pad(jnp.stack([jnp.sum(terms), jnp.sum(mask)])[None], ((0, 0), (0, 126)))
    gradients, totals = summed_everywhere(packed((grads_one, grads_two), tail))
    loss_total, count = totals[0], totals[1]
    gradients = gradients / count
    norm = jnp.sqrt(jnp.sum(gradients * gradients))
    by_layer = gradients.reshape(layers, ADAPTER_RANK, -1)
    gradient_tree = [
        by_layer[:, :, : 3 * MODEL_WIDTH]
        .reshape(layers, ADAPTER_RANK, 3, MODEL_WIDTH)
        .transpose(0, 3, 2, 1)
        .reshape(layers, MODEL_WIDTH, 3 * ADAPTER_RANK),
        by_layer[:, :, 3 * MODEL_WIDTH : 3 * MODEL_WIDTH + HIDDEN_UNITS].transpose(0, 2, 1),
        by_layer[:, :, 3 * MODEL_WIDTH + HIDDEN_UNITS :],
    ]
    scale_factor = jnp.minimum(1.0, CLIP / (norm + 1e-06))
    step_number = optimizer_step[0].astype(jnp.float32)
    updated = [
        moment_update(weight, first, second, gradient_value, scale_factor, step_number)
        for weight, first, second, gradient_value in zip(
            (adapter_down, adapter_down_feed, adapter_up),
            (first_moment_down, first_moment_feed, first_moment_up),
            (second_moment_down, second_moment_feed, second_moment_up),
            gradient_tree,
        )
    ]
    return (
        loss_total / count,
        norm,
        *(part[0] for part in updated),
        *(part[1] for part in updated),
        *(part[2] for part in updated),
        terms.reshape(micro, seqs, picks),
    )


def solution(mesh):
    in_specs = (
        P(None, ("dp", "fsdp"), None),
        P(None, ("dp", "fsdp")),
        P(None, ("dp", "fsdp"), None),
        P(None, ("dp", "fsdp"), None),
        P("fsdp", None),
        P(),
        P(None, "fsdp", None),
        P(None, "fsdp", None),
        P(None, "fsdp", None),
        P(None, "fsdp"),
        P(),
        P(),
        P(),
        P(),
        P(),
        P(),
        P(),
        P(),
        P(),
        P(),
        P(),
    )
    out_specs = (
        P(),
        P(),
        P(),
        P(),
        P(),
        P(),
        P(),
        P(),
        P(),
        P(),
        P(),
        P(None, ("dp", "fsdp"), None),
    )
    return jax.shard_map(body, mesh=mesh, in_specs=in_specs, out_specs=out_specs, check_vma=False)
```
